32 devices in a mesh: wide: 8 (over y, x, core), narrow: 4 (over z).
Axes of the slice: x: 2, y: 2, z: 4, core: 2. Of those that a mesh axis runs over, the one named last changes fastest.
Arguments:
- patches: bfloat16 [192, 576, 384], P(('wide', 'narrow')), may hold values from -6 to 6
- valid: int32 [192, 576], P(('wide', 'narrow')), may hold values from 0 to 1, as said below
- attn_weights: bfloat16 [384, 1536], P(None, ('wide', 'narrow')), may hold values from -2.5005208 to 2.5005208
- norm_gains: bfloat16 [768], P(('wide', 'narrow')), may hold values from 0.099609375 to 1.8984375
- vec_biases: bfloat16 [1536], P(('wide', 'narrow')), may hold values from -0.3125 to 0.3125
- slot_params: bfloat16 [3072], P(('wide', 'narrow')), may hold values from -0.625 to 0.625
- expert_in: bfloat16 [8, 384, 1536], P(None, None, ('wide', 'narrow')), may hold values from -0.875 to 0.875
- expert_in_bias: bfloat16 [8, 1536], P(None, ('wide', 'narrow')), may hold values from -1.75 to 1.75
- expert_out: bfloat16 [8, 1536, 384], P(None, ('wide', 'narrow')), may hold values from -0.375 to 0.375
- expert_out_bias: bfloat16 [3072], P(('wide', 'narrow')), may hold values from -0.625 to 0.625
- out_grad: bfloat16 [192, 576, 384], P(('wide', 'narrow')), may hold values from -12 to 12
Outputs:
- mixed_out: bfloat16 [192, 576, 384], P(('wide', 'narrow'))
- patch_grad: bfloat16 [192, 576, 384], P(('wide', 'narrow'))
- attn_weights_grad: float32 [384, 1536], P(None, ('wide', 'narrow'))
- norm_gains_grad: float32 [768], P(('wide', 'narrow'))
- vec_biases_grad: float32 [1536], P(('wide', 'narrow'))
- slot_params_grad: float32 [3072], P(('wide', 'narrow'))
- expert_in_grad: float32 [8, 384, 1536], P(None, None, ('wide', 'narrow'))
- expert_in_bias_grad: float32 [8, 1536], P(None, ('wide', 'narrow'))
- expert_out_grad: float32 [8, 1536, 384], P(None, ('wide', 'narrow'))
- expert_out_bias_grad: float32 [3072], P(('wide', 'narrow'))
The draws below stay inside these ranges and needn't reach their ends.
Inputs may be any that keep to these rules, and one draw needn't show every extreme that they name: In each image the first 196 patches are valid; the others are either all valid or all padding.
All inputs are finite; a program needn't handle non-finite values.
Results may differ from the reference program's by a relative error of at most 0.019.
Values may be sent and summed in bfloat16 or wider, within the bound.
A program may use at most 192 MiB of HBM per device.

```python
import jax
import jax.numpy as jnp
from jax import lax

D = 384
FF = 1536
HEAD_DIM = 64
EXPERTS = 8
PATCH = 576
SHORT = 196
IMG_DEV = 6
IMAGES = 192


def draw_valid(key, part):
    key = jax.random.fold_in(key, 7)
    whole = jax.random.randint(key, (IMAGES, 1), 0, 2)
    bound = jnp.where(whole == 1, PATCH, SHORT)
    place = lax.broadcasted_iota(jnp.int32, (IMAGES, PATCH), 1)
    return (place < bound).astype(jnp.int32)


def draw_attn_weights(key, part):
    key = jax.random.fold_in(key, 5)
    base = jnp.clip(jax.random.normal(key, (D, 4 * D), jnp.float32), -4.0, 4.0)
    column = lax.broadcasted_iota(jnp.int32, (D, 4 * D), 1)
    factor = jnp.where(column >= 3 * D, 12.0, 1.0)
    return (base * factor * D ** (-0.5)).astype(jnp.bfloat16)


def with_spikes(values, stream_key, source, target, blocks, factor):
    def block_of(axis_at):
        return (jnp.arange(values.shape[axis_at]) // (values.shape[axis_at] // blocks)).reshape((-1,) + (1,) * (values.ndim - 1 - axis_at))

    one_side = jax.random.permutation(stream_key, blocks)[block_of(target)]
    other_side = (block_of(target) + blocks // 2) % blocks
    return jnp.where((block_of(source) == one_side) | (block_of(source) == other_side), factor * values, values)


def block_scale(own_key, extent, shards, least, largest):
    level = 1.0
    for dim, blocks in shards:
        heights = jax.random.uniform(jax.random.fold_in(jax.random.fold_in(own_key, 6), dim), (blocks,), jnp.float32, least / len(shards), largest / len(shards))
        level = level * jnp.repeat(jnp.exp(heights), extent[dim] // blocks).reshape((-1,) + (1,) * (len(extent) - 1 - dim))
    return level


def noise(rng, shape, deviation, most, pieces=(), dtype=jnp.bfloat16):
    factor_of = block_scale(rng, shape, pieces, -0.22, 0.18) if pieces else 1.0
    array = jax.random.normal(rng, shape, jnp.float32) * deviation * factor_of
    return jnp.minimum(jnp.maximum(array, -most), most).astype(dtype)


def heavy_noise(own_key, shape, scale, limit, split, heavy, kind=jnp.bfloat16):
    array = scale * jax.random.normal(own_key, shape, jnp.float32)
    if split:
        array = array * block_scale(own_key, shape, split, -0.22, 0.18)
    return jnp.clip(with_spikes(array, jax.random.fold_in(own_key, 3), *heavy), -limit, limit).astype(kind)


def setup_inputs(seed: int = 0) -> dict:
    splits = jax.random.split(jax.random.key(seed), 12)
    patches = noise(splits[0], (IMAGES, PATCH, D), 1.0, 6.0, ((0, 32),))
    valid = draw_valid(jax.random.fold_in(splits[11], 71), 0)
    attn_weights = draw_attn_weights(jax.random.fold_in(splits[11], 71), 0)
    norm_gains = jnp.clip(1.0 + 0.18 * jax.random.normal(splits[3], (2 * D,), jnp.float32), 0.099609375, 1.8984375).astype(jnp.bfloat16)
    vec_biases = noise(splits[4], (4 * D,), 0.05, 0.3125, ((0, 32),))
    slot_params = noise(splits[5], (EXPERTS * D,), 0.1, 0.625, ((0, 32),))
    expert_in = noise(splits[6], (EXPERTS, D, FF), (D // 8) ** -0.5, 0.875, ((2, 32),))
    expert_in_bias = noise(splits[7], (EXPERTS, FF), 0.3, 1.75, ((1, 32),))
    expert_out = noise(splits[8], (EXPERTS, FF, D), (FF // 6) ** -0.5, 0.375, ((1, 32),))
    expert_out_bias = noise(splits[9], (EXPERTS * D,), 0.1, 0.625, ((0, 32),))
    out_grad = heavy_noise(splits[10], (IMAGES, PATCH, D), 1.0, 12.0, ((0, 32),), (0, 2, 32, 2.75))
    return {"patches": patches, "valid": valid, "attn_weights": attn_weights, "norm_gains": norm_gains, "vec_biases": vec_biases, "slot_params": slot_params, "expert_in": expert_in, "expert_in_bias": expert_in_bias, "expert_out": expert_out, "expert_out_bias": expert_out_bias, "out_grad": out_grad}


highest = lax.Precision.HIGHEST
masked_score = -1000000000.0

@jax.custom_vjp
def low(v):
    return lax.optimization_barrier(v.astype(jnp.bfloat16)).astype(jnp.float32)

@jax.custom_vjp
def low_back(v):
    return v

def low_keep(v):
    return (low(v), None)

def low_pass(kept, grad):
    return (grad,)

def back_keep(v):
    return (v, None)

def back_low(kept, grad):
    return (low(grad),)
low.defvjp(low_keep, low_pass)
low_back.defvjp(back_keep, back_low)

def standard(values):
    centred = values - lax.optimization_barrier(jnp.mean(values, axis=-1, keepdims=True))
    variance = lax.optimization_barrier(jnp.mean(centred * centred, axis=-1, keepdims=True))
    return centred * lax.rsqrt(variance + 1e-06)

def block(params, images, masks):
    attn_weights, norm_gains, vec_biases, slot_params, expert_in, expert_in_bias, expert_out, expert_out_bias = params
    keep = masks > 0
    count, length, width = images.shape
    heads = width // HEAD_DIM
    experts = expert_in.shape[0]
    first = low(standard(images) * norm_gains[:width] + vec_biases[:width])
    project = jnp.einsum('gpd,de->gpe', first, attn_weights[:, :3 * width], precision=highest)
    query = low(low_back(project[..., :width])).reshape(count, length, heads, HEAD_DIM)
    keys = low(low_back(project[..., width:2 * width])).reshape(count, length, heads, HEAD_DIM)
    values = low(low_back(project[..., 2 * width:] + vec_biases[width:2 * width])).reshape(count, length, heads, HEAD_DIM)
    scores = jnp.einsum('gqhc,gkhc->ghqk', query, keys, precision=highest) * HEAD_DIM ** (-0.5)
    scores = low_back(jnp.where(keep[:, None, None, :], scores, masked_score))
    weights = low(jax.nn.softmax(scores, axis=-1))
    attended = jnp.einsum('ghqk,gkhc->gqhc', weights, values, precision=highest).reshape(count, length, width)
    attended = low(low_back(attended))
    branch = jnp.einsum('gpd,de->gpe', attended, attn_weights[:, 3 * width:], precision=highest)
    branch = low_back(branch + vec_biases[2 * width:3 * width])
    middle = images + branch
    second = low(standard(middle) * norm_gains[width:] + vec_biases[3 * width:])
    table = slot_params.reshape(experts, width)
    logits = low_back(jnp.einsum('gpd,ed->gpe', second, table, precision=highest))
    dispatch = low(jax.nn.softmax(jnp.where(keep[:, :, None], logits, masked_score), axis=1))
    combine = low(jax.nn.softmax(logits, axis=2))
    slots = low(low_back(jnp.einsum('gpe,gpd->ged', dispatch, second, precision=highest)))
    hidden = low_back(jnp.einsum('ged,edf->gef', slots, expert_in, precision=highest) + expert_in_bias)
    active = low(jax.nn.gelu(hidden, approximate=False))
    produced = jnp.einsum('gef,efd->ged', active, expert_out, precision=highest) + expert_out_bias.reshape(experts, width)
    produced = low(low_back(produced))
    mixed = low_back(jnp.einsum('gpe,ged->gpd', combine, produced, precision=highest))
    return middle + mixed

def reference(patches, valid, attn_weights, norm_gains, vec_biases, slot_params, expert_in, expert_in_bias, expert_out, expert_out_bias, out_grad):
    params = tuple((item.astype(jnp.float32) for item in (attn_weights, norm_gains, vec_biases, slot_params, expert_in, expert_in_bias, expert_out, expert_out_bias)))
    width = patches.shape[-1]
    groups = IMAGES // IMG_DEV
    inputs = (patches.reshape(groups, IMG_DEV, PATCH, width), valid.reshape(groups, IMG_DEV, PATCH).astype(jnp.int32), out_grad.reshape(groups, IMG_DEV, PATCH, width))
    start = tuple((jnp.zeros(item.shape, jnp.float32) for item in params))

    def visit(totals, group):
        images, masks, cotangent = group
        result, pullback = jax.vjp(lambda weights, values: block(weights, values, masks), params, images.astype(jnp.float32))
        grads, image_grad = pullback(cotangent.astype(jnp.float32))
        totals = tuple((total + part for total, part in zip(totals, grads)))
        return (totals, (result.astype(jnp.bfloat16), image_grad.astype(jnp.bfloat16)))
    totals, (mixed, backward) = lax.scan(visit, start, inputs)
    return (mixed.reshape(IMAGES, PATCH, width), backward.reshape(IMAGES, PATCH, width), totals[0], totals[1], totals[2], totals[3], totals[4], totals[5], totals[6], totals[7])
```

```python
import jax
import jax.numpy as jnp
from jax import lax
from jax.sharding import PartitionSpec as P

HEAD_DIM = 64
MASKED = -1000000000.0
AXES = ("wide", "narrow")


def normalize(values):
    centred = values - jnp.mean(values, axis=-1, keepdims=True)
    variance = jnp.mean(centred * centred, axis=-1, keepdims=True)
    factor = lax.rsqrt(variance + 1e-06)
    return (centred * factor, factor)


def norm_back(grad_hat, normed, factor):
    return factor * (
        grad_hat
        - jnp.mean(grad_hat, axis=-1, keepdims=True)
        - normed * jnp.mean(grad_hat * normed, axis=-1, keepdims=True)
    )


def smooth(values):
    return jax.nn.gelu(values, approximate=False)


def masked_scores(query, keys, keep):
    scores = jnp.einsum(
        "qhc,khc->hqk", query, keys, preferred_element_type=jnp.float32
    ) * query.shape[-1] ** (-0.5)
    return jnp.where(keep[None, None, :], scores, MASKED)


def attend(item):
    query, keys, values, keep = item
    scores = masked_scores(query, keys, keep)
    peak = jnp.max(scores, axis=-1, keepdims=True)
    spread = peak + jnp.log(jnp.sum(jnp.exp(scores - peak), axis=-1, keepdims=True))
    weights = jnp.exp(scores - spread).astype(jnp.bfloat16)
    attended = jnp.einsum("hqk,khc->qhc", weights, values, preferred_element_type=jnp.float32)
    return (attended.astype(jnp.bfloat16), spread)


def attend_back(item):
    query, keys, values, keep, spread, upstream = item
    weights = jnp.exp(masked_scores(query, keys, keep) - spread)
    prob_grad = jnp.einsum("qhc,khc->hqk", upstream, values, preferred_element_type=jnp.float32)
    score_grad = (
        weights * (prob_grad - jnp.sum(weights * prob_grad, axis=-1, keepdims=True))
    ).astype(jnp.bfloat16)
    factor = query.shape[-1] ** (-0.5)
    query_grad = (
        jnp.einsum("hqk,khc->qhc", score_grad, keys, preferred_element_type=jnp.float32) * factor
    ).astype(jnp.bfloat16)
    key_grad = (
        jnp.einsum("hqk,qhc->khc", score_grad, query, preferred_element_type=jnp.float32) * factor
    ).astype(jnp.bfloat16)
    value_grad = jnp.einsum(
        "hqk,qhc->khc", weights.astype(jnp.bfloat16), upstream, preferred_element_type=jnp.float32
    ).astype(jnp.bfloat16)
    return (query_grad, key_grad, value_grad)


def scatter_sum(parts):
    got = lax.all_to_all(parts.astype(jnp.bfloat16), AXES, 0, 0, tiled=True)
    return jnp.sum(got.astype(jnp.float32), axis=0)


def experts_at_home(slots, produced_grad, expert_in, expert_in_bias, expert_out, devices):
    local_images, experts, width = slots.shape
    every = lax.all_gather(jnp.stack([slots, produced_grad]), AXES, axis=1, tiled=True)
    all_slots, all_grads = every[0], every[1]
    hidden = jnp.einsum(
        "bed,edf->bef", all_slots, expert_in, preferred_element_type=jnp.float32
    ) + expert_in_bias.astype(jnp.float32)
    active, gelu_back = jax.vjp(smooth, hidden)
    active = active.astype(jnp.bfloat16)
    partial = jnp.einsum("bef,efd->bed", active, expert_out, preferred_element_type=jnp.float32)
    active_grad = jnp.einsum(
        "bed,efd->bef", all_grads, expert_out, preferred_element_type=jnp.float32
    )
    hidden_grad = gelu_back(active_grad)[0].astype(jnp.bfloat16)
    partial_back = jnp.einsum(
        "bef,edf->bed", hidden_grad, expert_in, preferred_element_type=jnp.float32
    )
    contract_grad = jnp.einsum(
        "bef,bed->efd", active, all_grads, preferred_element_type=jnp.float32
    )
    expand_grad = jnp.einsum(
        "bed,bef->edf", all_slots, hidden_grad, preferred_element_type=jnp.float32
    )
    inner_grad = jnp.sum(hidden_grad.astype(jnp.float32), axis=0)
    both = jnp.stack([partial, partial_back]).reshape(2, devices, local_images, experts, width)
    both = scatter_sum(jnp.moveaxis(both, 1, 0))
    return (both[0], both[1], expand_grad, inner_grad, contract_grad)


def on_device(
    patches,
    valid,
    attn_weights,
    norm_gains,
    vec_biases,
    slot_params,
    expert_in,
    expert_in_bias,
    expert_out,
    expert_out_bias,
    out_grad,
):
    local_images, patch_count, width = patches.shape
    experts = expert_in.shape[0]
    heads = width // HEAD_DIM
    head_shape = (local_images, patch_count, heads, HEAD_DIM)
    flat_shape = (local_images, patch_count, width)
    devices = lax.axis_size("wide") * lax.axis_size("narrow")

    vectors = (norm_gains, vec_biases, slot_params, expert_out_bias)
    lengths = [v.shape[0] for v in vectors]
    small = lax.all_gather(jnp.concatenate(vectors), AXES)
    pieces = []
    at = 0
    for length in lengths:
        pieces.append(small[:, at : at + length].reshape(devices * length))
        at += length
    gains, biases, slot_flat, expert_shift = pieces
    weights = lax.all_gather(attn_weights.T, AXES, axis=0, tiled=True)
    gains = gains.astype(jnp.float32)
    biases = biases.astype(jnp.float32)
    first_gain = gains[:width]
    second_gain = gains[width:]
    keep = valid > 0
    images = patches.astype(jnp.float32)
    normed_one, factor_one = normalize(images)
    first = (normed_one * first_gain + biases[:width]).astype(jnp.bfloat16)
    project = jnp.einsum(
        "bpd,ed->bpe", first, weights[: 3 * width], preferred_element_type=jnp.float32
    )
    query = project[..., :width].astype(jnp.bfloat16).reshape(head_shape)
    keys = project[..., width : 2 * width].astype(jnp.bfloat16).reshape(head_shape)
    values = (
        (project[..., 2 * width :] + biases[width : 2 * width])
        .astype(jnp.bfloat16)
        .reshape(head_shape)
    )
    attended, spread = lax.map(attend, (query, keys, values, keep))
    attended = attended.reshape(flat_shape)
    branch = jnp.einsum(
        "bpd,ed->bpe", attended, weights[3 * width :], preferred_element_type=jnp.float32
    )
    middle = images + branch + biases[2 * width : 3 * width]
    normed_two, factor_two = normalize(middle)
    second = (normed_two * second_gain + biases[3 * width :]).astype(jnp.bfloat16)
    slot_table = slot_flat.reshape(experts, width)
    logits = jnp.einsum("bpd,ed->bpe", second, slot_table, preferred_element_type=jnp.float32)
    dispatch = jax.nn.softmax(jnp.where(keep[:, :, None], logits, MASKED), axis=1)
    combine = jax.nn.softmax(logits, axis=2)
    dispatch_low = dispatch.astype(jnp.bfloat16)
    combine_low = combine.astype(jnp.bfloat16)
    slots = jnp.einsum(
        "bpe,bpd->bed", dispatch_low, second, preferred_element_type=jnp.float32
    ).astype(jnp.bfloat16)
    produced_grad = jnp.einsum(
        "bpe,bpd->bed", combine_low, out_grad, preferred_element_type=jnp.float32
    ).astype(jnp.bfloat16)

    produced, slot_grad, expand_grad, inner_grad, contract_grad = experts_at_home(
        slots, produced_grad, expert_in, expert_in_bias, expert_out, devices
    )
    shift_rows = expert_shift.reshape(experts, width).astype(jnp.float32)
    produced = (produced + shift_rows).astype(jnp.bfloat16)
    slot_grad = slot_grad.astype(jnp.bfloat16)
    shift_grad = jnp.sum(produced_grad.astype(jnp.float32), axis=0).reshape(experts * width)

    mixture = jnp.einsum("bpe,bed->bpd", combine_low, produced, preferred_element_type=jnp.float32)
    mixed_out = (middle + mixture).astype(jnp.bfloat16)
    upstream = out_grad.astype(jnp.float32)
    combine_grad = jnp.einsum(
        "bpd,bed->bpe", out_grad, produced, preferred_element_type=jnp.float32
    )
    dispatch_grad = jnp.einsum(
        "bpd,bed->bpe", second, slot_grad, preferred_element_type=jnp.float32
    )
    second_grad = jnp.einsum(
        "bpe,bed->bpd", dispatch_low, slot_grad, preferred_element_type=jnp.float32
    )
    logit_grad = dispatch * (
        dispatch_grad - jnp.sum(dispatch * dispatch_grad, axis=1, keepdims=True)
    )
    logit_grad = logit_grad + combine * (
        combine_grad - jnp.sum(combine * combine_grad, axis=2, keepdims=True)
    )
    logit_grad = logit_grad.astype(jnp.bfloat16)
    table_grad = jnp.einsum(
        "bpd,bpe->ed", second, logit_grad, preferred_element_type=jnp.float32
    ).reshape(experts * width)
    second_grad = second_grad + jnp.einsum(
        "bpe,ed->bpd", logit_grad, slot_table, preferred_element_type=jnp.float32
    )
    gain_two = jnp.sum(second_grad * normed_two, axis=(0, 1))
    shift_two = jnp.sum(second_grad, axis=(0, 1))
    middle_grad = upstream + norm_back(second_grad * second_gain, normed_two, factor_two)
    branch_grad = middle_grad.astype(jnp.bfloat16)
    output_grad = jnp.einsum(
        "bpd,bpe->ed", attended, branch_grad, preferred_element_type=jnp.float32
    )
    branch_shift = jnp.sum(branch_grad.astype(jnp.float32), axis=(0, 1))
    attended_grad = jnp.einsum(
        "bpe,ed->bpd", branch_grad, weights[3 * width :], preferred_element_type=jnp.float32
    ).astype(jnp.bfloat16)
    query_grad, key_grad, value_grad = lax.map(
        attend_back, (query, keys, values, keep, spread, attended_grad.reshape(head_shape))
    )
    project_grad = jnp.concatenate(
        [
            query_grad.reshape(flat_shape),
            key_grad.reshape(flat_shape),
            value_grad.reshape(flat_shape),
        ],
        axis=-1,
    )
    weight_front = jnp.einsum(
        "bpd,bpe->ed", first, project_grad, preferred_element_type=jnp.float32
    )
    value_shift = jnp.sum(value_grad.astype(jnp.float32), axis=(0, 1)).reshape(width)
    first_grad = jnp.einsum(
        "bpe,ed->bpd", project_grad, weights[: 3 * width], preferred_element_type=jnp.float32
    )
    gain_one = jnp.sum(first_grad * normed_one, axis=(0, 1))
    shift_one = jnp.sum(first_grad, axis=(0, 1))
    patch_grad = (middle_grad + norm_back(first_grad * first_gain, normed_one, factor_one)).astype(
        jnp.bfloat16
    )
    weight_grad = jnp.concatenate([weight_front, output_grad], axis=0)
    weight_grad = scatter_sum(weight_grad.reshape(devices, -1, width)).T
    gain_grads = jnp.concatenate([gain_one, gain_two])
    bias_grads = jnp.concatenate([shift_one, value_shift, branch_shift, shift_two])
    small_grads = jnp.concatenate(
        [v.reshape(devices, -1) for v in (gain_grads, bias_grads, table_grad, shift_grad)], axis=1
    )
    small_grads = jnp.sum(lax.all_to_all(small_grads, AXES, 0, 0, tiled=True), axis=0)
    grads = []
    at = 0
    for length in lengths:
        grads.append(small_grads[at : at + length])
        at += length
    return (
        mixed_out,
        patch_grad,
        weight_grad,
        grads[0],
        grads[1],
        grads[2],
        expand_grad,
        inner_grad,
        contract_grad,
        grads[3],
    )


def solution(mesh):
    images = P(AXES, None, None)
    vector = P(AXES)
    second = P(None, AXES)
    return jax.shard_map(
        on_device,
        mesh=mesh,
        in_specs=(
            images,
            P(AXES, None),
            second,
            vector,
            vector,
            vector,
            P(None, None, AXES),
            second,
            P(None, AXES, None),
            vector,
            images,
        ),
        out_specs=(
            images,
            images,
            second,
            vector,
            vector,
            vector,
            P(None, None, AXES),
            second,
            P(None, AXES, None),
            vector,
        ),
        check_vma=False,
    )
```

```python
import jax
import jax.numpy as jnp
from jax import lax
from jax.experimental import pallas as pl
from jax.experimental.pallas import tpu as pltpu
from jax.sharding import PartitionSpec as P

HEAD_DIM = 64
PAIR = 2 * HEAD_DIM
MASKED = -1000000000.0
AXES = ("wide", "narrow")
BF16 = jnp.bfloat16
F32 = jnp.float32
VMEM_LIMIT = 60 * 1024 * 1024
GAIN1, GAIN2, BIAS1, VBIAS, OBIAS, BIAS2 = range(6)


def dot(left, right, left_dim, right_dim):
    return lax.dot_general(
        left, right, (((left_dim,), (right_dim,)), ((), ())), preferred_element_type=F32
    )


def normalize(values):
    centred = values - jnp.mean(values, axis=-1, keepdims=True)
    factor = lax.rsqrt(jnp.mean(centred * centred, axis=-1, keepdims=True) + 1e-06)
    return (centred * factor, factor)


def norm_back(grad_hat, normed, factor):
    return factor * (
        grad_hat
        - jnp.mean(grad_hat, axis=-1, keepdims=True)
        - normed * jnp.mean(grad_hat * normed, axis=-1, keepdims=True)
    )


def smooth(values):
    return jax.nn.gelu(values, approximate=False)


def lower_half(shape):
    return lax.broadcasted_iota(jnp.int32, shape, 1) < HEAD_DIM


def own_half(low, head, own, other):
    return jnp.where(low, own, other) if head % 2 == 0 else jnp.where(low, other, own)


def forward_image(x, g, valid_row, wt, vec, table, q_ref, k_ref, v_ref, p_ref, att_ref, inv_ref):
    patches, width = x.shape
    heads = width // HEAD_DIM
    images = x.astype(F32)
    normed, _ = normalize(images)
    first = (normed * vec[GAIN1 : GAIN1 + 1] + vec[BIAS1 : BIAS1 + 1]).astype(BF16)
    q_ref[...] = (dot(first, wt[:width], 1, 1) * HEAD_DIM ** (-0.5)).astype(BF16)
    k_ref[...] = dot(first, wt[width : 2 * width], 1, 1).astype(BF16)
    v_ref[...] = (dot(first, wt[2 * width : 3 * width], 1, 1) + vec[VBIAS : VBIAS + 1]).astype(BF16)
    bias_row = jnp.where(valid_row > 0, 0.0, MASKED).astype(F32)
    fill = jnp.broadcast_to(bias_row * (1.0 / HEAD_DIM), (PAIR, patches)).T.astype(BF16)
    low = lower_half((patches, PAIR))
    one = jnp.ones((patches, PAIR), BF16)
    scores = {}

    def pair_of(ref, head):
        at = head // 2 * PAIR
        return ref[:, at : at + PAIR]

    def score(head):
        scores[head] = dot(
            own_half(low, head, pair_of(q_ref, head), one),
            own_half(low, head, pair_of(k_ref, head), fill),
            1,
            1,
        )

    sums = {}
    score(0)
    for head in range(heads):
        if head + 1 < heads:
            score(head + 1)
        raw = scores.pop(head)
        prob = jnp.exp(raw - jnp.max(raw, axis=1, keepdims=True)).astype(BF16)
        p_ref[head] = prob
        sums[head] = dot(prob, own_half(low, head, pair_of(v_ref, head), one), 1, 0)
        if head % 2 == 1:
            even, odd = sums.pop(head - 1), sums.pop(head)
            inverse = 1.0 / pltpu.roll(jnp.where(low, odd, even), HEAD_DIM, 1)
            at = head // 2 * PAIR
            inv_ref[:, at : at + PAIR] = inverse
            att_ref[:, at : at + PAIR] = (jnp.where(low, even, odd) * inverse).astype(BF16)
    branch = dot(att_ref[...], wt[3 * width :], 1, 1)
    middle = images + branch + vec[OBIAS : OBIAS + 1]
    normed, _ = normalize(middle)
    second = (normed * vec[GAIN2 : GAIN2 + 1] + vec[BIAS2 : BIAS2 + 1]).astype(BF16)
    logits = dot(table, second, 1, 1)
    masked = jnp.where(valid_row > 0, logits, MASKED)
    dispatch = jnp.exp(masked - jnp.max(masked, axis=1, keepdims=True))
    dispatch = dispatch / jnp.sum(dispatch, axis=1, keepdims=True)
    combine = jnp.exp(logits - jnp.max(logits, axis=0, keepdims=True))
    combine = combine / jnp.sum(combine, axis=0, keepdims=True)
    slots = dot(dispatch.astype(BF16), second, 1, 0).astype(BF16)
    produced_grad = dot(combine.astype(BF16), g, 1, 0).astype(BF16)
    return middle, second, dispatch, combine, slots, produced_grad


def backward_image(
    x, g, middle, second, dispatch, combine, produced, slot_grad, wt, vec, table,
    q_ref, k_ref, v_ref, p_ref, att_ref, inv_ref, ds_ref, grad_t_ref, grad_ref,
):
    patches, width = x.shape
    heads = width // HEAD_DIM
    combine_low = combine.astype(BF16)
    dispatch_low = dispatch.astype(BF16)
    mixed = (middle + dot(combine_low, produced, 0, 0)).astype(BF16)
    combine_grad = dot(produced, g, 1, 1)
    dispatch_grad = dot(slot_grad, second, 1, 1)
    logit_grad = dispatch * (
        dispatch_grad - jnp.sum(dispatch * dispatch_grad, axis=1, keepdims=True)
    ) + combine * (combine_grad - jnp.sum(combine * combine_grad, axis=0, keepdims=True))
    logit_grad = logit_grad.astype(BF16)
    table_grad = dot(logit_grad, second, 1, 0)
    second_grad = dot(
        jnp.concatenate([dispatch_low, logit_grad], axis=0),
        jnp.concatenate([slot_grad, table], axis=0),
        0,
        0,
    )
    normed, factor = normalize(middle)
    gain_two = jnp.sum(second_grad * normed, axis=0, keepdims=True)
    shift_two = jnp.sum(second_grad, axis=0, keepdims=True)
    middle_grad = g.astype(F32) + norm_back(second_grad * vec[GAIN2 : GAIN2 + 1], normed, factor)
    branch_grad = middle_grad.astype(BF16)
    branch_shift = jnp.sum(branch_grad.astype(F32), axis=0, keepdims=True)
    output_grad = dot(branch_grad.T, att_ref[...], 1, 0)
    attended_grad = dot(branch_grad, wt[3 * width :], 1, 0).astype(BF16).astype(F32)
    scaled = attended_grad * inv_ref[...]
    drop = -(scaled * att_ref[...].astype(F32))
    scaled = scaled.astype(BF16)
    scaled_t = scaled.T
    query_t = q_ref[...].T
    low = lower_half((patches, PAIR))
    one = jnp.ones((patches, PAIR), BF16)
    prob_grads = {}

    def pair_of(ref, head):
        at = head // 2 * PAIR
        return ref[:, at : at + PAIR]

    def prob_grad(head):
        rolled = pltpu.roll(pair_of(drop, head), HEAD_DIM, 1).astype(BF16)
        prob_grads[head] = dot(
            own_half(low, head, pair_of(scaled, head), rolled),
            own_half(low, head, pair_of(v_ref, head), one),
            1,
            1,
        )

    query_grads = {}
    prob_grad(0)
    for head in range(heads):
        if head + 1 < heads:
            prob_grad(head + 1)
        rows = slice(head * HEAD_DIM, (head + 1) * HEAD_DIM)
        prob = p_ref[head]
        grad_t_ref[2 * width + rows.start : 2 * width + rows.stop, :] = dot(
            scaled_t[rows], prob, 1, 0
        ).astype(BF16)
        score_grad = (prob.astype(F32) * prob_grads.pop(head)).astype(BF16)
        ds_ref[head % 2] = score_grad
        score_grad = ds_ref[head % 2]
        query_grads[head] = dot(score_grad, pair_of(k_ref, head), 1, 0)
        grad_t_ref[width + rows.start : width + rows.stop, :] = dot(
            query_t[rows], score_grad, 1, 0
        ).astype(BF16)
        if head % 2 == 1:
            both = jnp.where(low, query_grads.pop(head - 1), query_grads.pop(head))
            at = head // 2 * PAIR
            grad_ref[:, at : at + PAIR] = (both * HEAD_DIM ** (-0.5)).astype(BF16)
    grad_t_ref[:width, :] = grad_ref[:, :width].T
    grad_ref[:, width:] = grad_t_ref[width:, :].T
    normed, factor = normalize(x.astype(F32))
    first = (normed * vec[GAIN1 : GAIN1 + 1] + vec[BIAS1 : BIAS1 + 1]).astype(BF16)
    front_grad = dot(grad_t_ref[...], first, 1, 0)
    value_shift = jnp.sum(grad_ref[:, 2 * width :].astype(F32), axis=0, keepdims=True)
    first_grad = dot(grad_ref[...], wt[: 3 * width], 1, 0)
    gain_one = jnp.sum(first_grad * normed, axis=0, keepdims=True)
    shift_one = jnp.sum(first_grad, axis=0, keepdims=True)
    patch_grad = middle_grad + norm_back(first_grad * vec[GAIN1 : GAIN1 + 1], normed, factor)
    rows = jnp.concatenate(
        [gain_one, gain_two, shift_one, value_shift, branch_shift, shift_two, jnp.zeros((2, width), F32)],
        axis=0,
    )
    return mixed, patch_grad.astype(BF16), front_grad, output_grad, rows, table_grad


def forward_kernel(
    x, g, valid, wt, vec, table,
    q, k, v, p, att, inv, middle, second, dispatch, combine, slots, produced_grad,
):
    got = forward_image(
        x[0], g[0], valid[0], wt[...], vec[...], table[...],
        q.at[0], k.at[0], v.at[0], p.at[0], att.at[0], inv.at[0],
    )
    for ref, value in zip((middle, second, dispatch, combine, slots, produced_grad), got):
        ref[0] = value


def backward_kernel(
    x, g, middle, second, dispatch, combine, produced, slot_grad, wt, vec, table,
    q, k, v, p, att, inv,
    mixed, patch_grad, weight_grad, rows, table_grad,
    ds, grad_t, grad,
):
    @pl.when(pl.program_id(0) == 0)
    def _():
        weight_grad[...] = jnp.zeros_like(weight_grad)
        rows[...] = jnp.zeros_like(rows)
        table_grad[...] = jnp.zeros_like(table_grad)

    width = x.shape[-1]
    got = backward_image(
        x[0], g[0], middle[0], second[0], dispatch[0], combine[0], produced[0], slot_grad[0],
        wt[...], vec[...], table[...],
        q.at[0], k.at[0], v.at[0], p.at[0], att.at[0], inv.at[0], ds, grad_t, grad,
    )
    mixed[0] = got[0]
    patch_grad[0] = got[1]
    weight_grad[: 3 * width, :] += got[2]
    weight_grad[3 * width :, :] += got[3]
    rows[...] += got[4]
    table_grad[...] += got[5]


def per_image(*shape):
    return pl.BlockSpec((1,) + shape, lambda i: (i,) + (0,) * len(shape))


def whole(*shape):
    return pl.BlockSpec(shape, lambda i: (0,) * len(shape))


def run_forward(x, g, valid, wt, vec, table):
    count, patches, width = x.shape
    heads = width // HEAD_DIM
    experts = table.shape[0]
    flat = (patches, width)
    outs = [
        (flat, BF16), (flat, BF16), (flat, BF16), ((heads, patches, patches), BF16),
        (flat, BF16), (flat, F32), (flat, F32), (flat, BF16),
        ((experts, patches), F32), ((experts, patches), F32),
        ((experts, width), BF16), ((experts, width), BF16),
    ]
    return pl.pallas_call(
        forward_kernel,
        grid=(count,),
        in_specs=[
            per_image(*flat), per_image(*flat), per_image(1, patches),
            whole(*wt.shape), whole(*vec.shape), whole(*table.shape),
        ],
        out_specs=[per_image(*shape) for shape, _ in outs],
        out_shape=[jax.ShapeDtypeStruct((count,) + shape, kind) for shape, kind in outs],
        compiler_params=pltpu.CompilerParams(vmem_limit_bytes=VMEM_LIMIT),
        name="forward",
    )(x, g, valid, wt, vec, table)


def run_backward(x, g, kept, produced, slot_grad, wt, vec, table):
    count, patches, width = x.shape
    heads = width // HEAD_DIM
    experts = table.shape[0]
    flat = (patches, width)
    q, k, v, p, att, inv, middle, second, dispatch, combine = kept
    return pl.pallas_call(
        backward_kernel,
        grid=(count,),
        in_specs=[
            per_image(*flat), per_image(*flat), per_image(*flat), per_image(*flat),
            per_image(experts, patches), per_image(experts, patches),
            per_image(experts, width), per_image(experts, width),
            whole(*wt.shape), whole(*vec.shape), whole(*table.shape),
            per_image(*flat), per_image(*flat), per_image(*flat),
            per_image(heads, patches, patches), per_image(*flat), per_image(*flat),
        ],
        out_specs=[
            per_image(*flat), per_image(*flat),
            whole(4 * width, width), whole(8, width), whole(experts, width),
        ],
        out_shape=[
            jax.ShapeDtypeStruct(x.shape, BF16), jax.ShapeDtypeStruct(x.shape, BF16),
            jax.ShapeDtypeStruct((4 * width, width), F32), jax.ShapeDtypeStruct((8, width), F32),
            jax.ShapeDtypeStruct((experts, width), F32),
        ],
        scratch_shapes=[
            pltpu.VMEM((2, patches, patches), BF16),
            pltpu.VMEM((3 * width, patches), BF16),
            pltpu.VMEM((patches, 3 * width), BF16),
        ],
        compiler_params=pltpu.CompilerParams(vmem_limit_bytes=VMEM_LIMIT),
        name="backward",
    )(x, g, middle, second, dispatch, combine, produced, slot_grad, wt, vec, table, q, k, v, p, att, inv)


def scatter_sum(parts):
    got = lax.all_to_all(parts.astype(BF16), AXES, 0, 0, tiled=True)
    return jnp.sum(got.astype(F32), axis=0)


def experts_at_home(slots, produced_grad, expert_in, expert_in_bias, expert_out, devices):
    local_images, experts, width = slots.shape
    every = lax.all_gather(jnp.stack([slots, produced_grad]), AXES, axis=1, tiled=True)
    all_slots, all_grads = every[0], every[1]
    hidden = jnp.einsum(
        "bed,edf->bef", all_slots, expert_in, preferred_element_type=F32
    ) + expert_in_bias.astype(F32)
    active, gelu_back = jax.vjp(smooth, hidden)
    active = active.astype(BF16)
    partial = jnp.einsum("bef,efd->bed", active, expert_out, preferred_element_type=F32)
    active_grad = jnp.einsum("bed,efd->bef", all_grads, expert_out, preferred_element_type=F32)
    hidden_grad = gelu_back(active_grad)[0].astype(BF16)
    partial_back = jnp.einsum("bef,edf->bed", hidden_grad, expert_in, preferred_element_type=F32)
    contract_grad = jnp.einsum("bef,bed->efd", active, all_grads, preferred_element_type=F32)
    expand_grad = jnp.einsum("bed,bef->edf", all_slots, hidden_grad, preferred_element_type=F32)
    inner_grad = jnp.sum(hidden_grad.astype(F32), axis=0)
    both = jnp.stack([partial, partial_back]).reshape(2, devices, local_images, experts, width)
    both = scatter_sum(jnp.moveaxis(both, 1, 0))
    return (both[0], both[1], expand_grad, inner_grad, contract_grad)


def on_device(
    patches,
    valid,
    attn_weights,
    norm_gains,
    vec_biases,
    slot_params,
    expert_in,
    expert_in_bias,
    expert_out,
    expert_out_bias,
    out_grad,
):
    local_images, patch_count, width = patches.shape
    experts = expert_in.shape[0]
    devices = lax.axis_size("wide") * lax.axis_size("narrow")

    vectors = (norm_gains, vec_biases, slot_params, expert_out_bias)
    lengths = [v.shape[0] for v in vectors]
    small = lax.all_gather(jnp.concatenate(vectors), AXES)
    pieces = []
    at = 0
    for length in lengths:
        pieces.append(small[:, at : at + length].reshape(-1, width))
        at += length
    gains, biases, table, expert_shift = pieces
    vec = jnp.concatenate([gains, biases, jnp.zeros((2, width), BF16)]).astype(F32)
    wt = lax.all_gather(attn_weights.T, AXES, axis=0, tiled=True)

    *kept, slots, produced_grad = run_forward(
        patches, out_grad, valid.reshape(local_images, 1, patch_count), wt, vec, table
    )
    produced, slot_grad, expand_grad, inner_grad, contract_grad = experts_at_home(
        slots, produced_grad, expert_in, expert_in_bias, expert_out, devices
    )
    produced = (produced + expert_shift.astype(F32)).astype(BF16)
    slot_grad = slot_grad.astype(BF16)
    shift_grad = jnp.sum(produced_grad.astype(F32), axis=0)
    mixed_out, patch_grad, weight_grad, rows, table_grad = run_backward(
        patches, out_grad, kept, produced, slot_grad, wt, vec, table
    )
    weight_grad = scatter_sum(weight_grad.reshape(devices, -1, width)).T
    small_grads = jnp.concatenate(
        [v.reshape(devices, -1) for v in (rows[:2], rows[2:6], table_grad, shift_grad)], axis=1
    )
    small_grads = jnp.sum(lax.all_to_all(small_grads, AXES, 0, 0, tiled=True), axis=0)
    grads = []
    at = 0
    for length in lengths:
        grads.append(small_grads[at : at + length])
        at += length
    return (
        mixed_out,
        patch_grad,
        weight_grad,
        grads[0],
        grads[1],
        grads[2],
        expand_grad,
        inner_grad,
        contract_grad,
        grads[3],
    )


def solution(mesh):
    images = P(AXES, None, None)
    vector = P(AXES)
    second = P(None, AXES)
    return jax.shard_map(
        on_device,
        mesh=mesh,
        in_specs=(
            images, P(AXES, None), second, vector, vector, vector,
            P(None, None, AXES), second, P(None, AXES, None), vector, images,
        ),
        out_specs=(
            images, images, second, vector, vector, vector,
            P(None, None, AXES), second, P(None, AXES, None), vector,
        ),
        check_vma=False,
    )
```

```python
import jax
import jax.numpy as jnp
from jax import lax
from jax.experimental import pallas as pl
from jax.experimental.pallas import tpu as pltpu
from jax.sharding import PartitionSpec as P

HEAD_DIM = 64
PAIR = 2 * HEAD_DIM
MASKED = -1000000000.0
AXES = ("wide", "narrow")
BF16 = jnp.bfloat16
F32 = jnp.float32
MESH = pl.DeviceIdType.MESH
VMEM_LIMIT = 60 * 1024 * 1024
GAIN1, GAIN2, BIAS1, VBIAS, OBIAS, BIAS2 = range(6)


def dot(left, right, left_dim, right_dim):
    return lax.dot_general(
        left, right, (((left_dim,), (right_dim,)), ((), ())), preferred_element_type=F32
    )


def normalize(values):
    centred = values - jnp.mean(values, axis=-1, keepdims=True)
    factor = lax.rsqrt(jnp.mean(centred * centred, axis=-1, keepdims=True) + 1e-06)
    return (centred * factor, factor)


def norm_back(grad_hat, normed, factor):
    return factor * (
        grad_hat
        - jnp.mean(grad_hat, axis=-1, keepdims=True)
        - normed * jnp.mean(grad_hat * normed, axis=-1, keepdims=True)
    )


def smooth(values):
    return jax.nn.gelu(values, approximate=False)


def lower_half(shape):
    return lax.broadcasted_iota(jnp.int32, shape, 1) < HEAD_DIM


def own_half(low, head, own, other):
    return jnp.where(low, own, other) if head % 2 == 0 else jnp.where(low, other, own)


def forward_image(x, g, valid_row, wt, vec, table, q_ref, k_ref, v_ref, p_ref, att_ref, inv_ref):
    patches, width = x.shape
    heads = width // HEAD_DIM
    images = x.astype(F32)
    normed, _ = normalize(images)
    first = (normed * vec[GAIN1 : GAIN1 + 1] + vec[BIAS1 : BIAS1 + 1]).astype(BF16)
    q_ref[...] = (dot(first, wt[:width], 1, 1) * HEAD_DIM ** (-0.5)).astype(BF16)
    k_ref[...] = dot(first, wt[width : 2 * width], 1, 1).astype(BF16)
    v_ref[...] = (dot(first, wt[2 * width : 3 * width], 1, 1) + vec[VBIAS : VBIAS + 1]).astype(BF16)
    bias_row = jnp.where(valid_row > 0, 0.0, MASKED).astype(F32)
    fill = jnp.broadcast_to(bias_row * (1.0 / HEAD_DIM), (PAIR, patches)).T.astype(BF16)
    low = lower_half((patches, PAIR))
    one = jnp.ones((patches, PAIR), BF16)
    scores = {}

    def pair_of(ref, head):
        at = head // 2 * PAIR
        return ref[:, at : at + PAIR]

    def score(head):
        scores[head] = dot(
            own_half(low, head, pair_of(q_ref, head), one),
            own_half(low, head, pair_of(k_ref, head), fill),
            1,
            1,
        )

    sums = {}
    score(0)
    for head in range(heads):
        if head + 1 < heads:
            score(head + 1)
        raw = scores.pop(head)
        prob = jnp.exp(raw - jnp.max(raw, axis=1, keepdims=True)).astype(BF16)
        p_ref[head] = prob
        sums[head] = dot(prob, own_half(low, head, pair_of(v_ref, head), one), 1, 0)
        if head % 2 == 1:
            even, odd = sums.pop(head - 1), sums.pop(head)
            inverse = 1.0 / pltpu.roll(jnp.where(low, odd, even), HEAD_DIM, 1)
            at = head // 2 * PAIR
            inv_ref[:, at : at + PAIR] = inverse
            att_ref[:, at : at + PAIR] = (jnp.where(low, even, odd) * inverse).astype(BF16)
    branch = dot(att_ref[...], wt[3 * width :], 1, 1)
    middle = images + branch + vec[OBIAS : OBIAS + 1]
    normed, _ = normalize(middle)
    second = (normed * vec[GAIN2 : GAIN2 + 1] + vec[BIAS2 : BIAS2 + 1]).astype(BF16)
    logits = dot(table, second, 1, 1)
    masked = jnp.where(valid_row > 0, logits, MASKED)
    dispatch = jnp.exp(masked - jnp.max(masked, axis=1, keepdims=True))
    dispatch = dispatch / jnp.sum(dispatch, axis=1, keepdims=True)
    combine = jnp.exp(logits - jnp.max(logits, axis=0, keepdims=True))
    combine = combine / jnp.sum(combine, axis=0, keepdims=True)
    slots = dot(dispatch.astype(BF16), second, 1, 0).astype(BF16)
    produced_grad = dot(combine.astype(BF16), g, 1, 0).astype(BF16)
    return middle, second, dispatch, combine, slots, produced_grad


def backward_image(
    x, g, middle, second, dispatch, combine, produced, slot_grad, wt, vec, table,
    q_ref, k_ref, v_ref, p_ref, att_ref, inv_ref, ds_ref, grad_t_ref, grad_ref,
):
    patches, width = x.shape
    heads = width // HEAD_DIM
    combine_low = combine.astype(BF16)
    dispatch_low = dispatch.astype(BF16)
    mixed = (middle + dot(combine_low, produced, 0, 0)).astype(BF16)
    combine_grad = dot(produced, g, 1, 1)
    dispatch_grad = dot(slot_grad, second, 1, 1)
    logit_grad = dispatch * (
        dispatch_grad - jnp.sum(dispatch * dispatch_grad, axis=1, keepdims=True)
    ) + combine * (combine_grad - jnp.sum(combine * combine_grad, axis=0, keepdims=True))
    logit_grad = logit_grad.astype(BF16)
    table_grad = dot(logit_grad, second, 1, 0)
    second_grad = dot(
        jnp.concatenate([dispatch_low, logit_grad], axis=0),
        jnp.concatenate([slot_grad, table], axis=0),
        0,
        0,
    )
    normed, factor = normalize(middle)
    gain_two = jnp.sum(second_grad * normed, axis=0, keepdims=True)
    shift_two = jnp.sum(second_grad, axis=0, keepdims=True)
    middle_grad = g.astype(F32) + norm_back(second_grad * vec[GAIN2 : GAIN2 + 1], normed, factor)
    branch_grad = middle_grad.astype(BF16)
    branch_shift = jnp.sum(branch_grad.astype(F32), axis=0, keepdims=True)
    output_grad = dot(branch_grad.T, att_ref[...], 1, 0)
    attended_grad = dot(branch_grad, wt[3 * width :], 1, 0).astype(BF16).astype(F32)
    scaled = attended_grad * inv_ref[...]
    drop = -(scaled * att_ref[...].astype(F32))
    scaled = scaled.astype(BF16)
    scaled_t = scaled.T
    query_t = q_ref[...].T
    low = lower_half((patches, PAIR))
    one = jnp.ones((patches, PAIR), BF16)
    prob_grads = {}

    def pair_of(ref, head):
        at = head // 2 * PAIR
        return ref[:, at : at + PAIR]

    def prob_grad(head):
        rolled = pltpu.roll(pair_of(drop, head), HEAD_DIM, 1).astype(BF16)
        prob_grads[head] = dot(
            own_half(low, head, pair_of(scaled, head), rolled),
            own_half(low, head, pair_of(v_ref, head), one),
            1,
            1,
        )

    query_grads = {}
    prob_grad(0)
    for head in range(heads):
        if head + 1 < heads:
            prob_grad(head + 1)
        rows = slice(head * HEAD_DIM, (head + 1) * HEAD_DIM)
        prob = p_ref[head]
        grad_t_ref[2 * width + rows.start : 2 * width + rows.stop, :] = dot(
            scaled_t[rows], prob, 1, 0
        ).astype(BF16)
        score_grad = (prob.astype(F32) * prob_grads.pop(head)).astype(BF16)
        ds_ref[head % 2] = score_grad
        score_grad = ds_ref[head % 2]
        query_grads[head] = dot(score_grad, pair_of(k_ref, head), 1, 0)
        grad_t_ref[width + rows.start : width + rows.stop, :] = dot(
            query_t[rows], score_grad, 1, 0
        ).astype(BF16)
        if head % 2 == 1:
            both = jnp.where(low, query_grads.pop(head - 1), query_grads.pop(head))
            at = head // 2 * PAIR
            grad_ref[:, at : at + PAIR] = (both * HEAD_DIM ** (-0.5)).astype(BF16)
    grad_t_ref[:width, :] = grad_ref[:, :width].T
    grad_ref[:, width:] = grad_t_ref[width:, :].T
    normed, factor = normalize(x.astype(F32))
    first = (normed * vec[GAIN1 : GAIN1 + 1] + vec[BIAS1 : BIAS1 + 1]).astype(BF16)
    front_grad = dot(grad_t_ref[...], first, 1, 0)
    value_shift = jnp.sum(grad_ref[:, 2 * width :].astype(F32), axis=0, keepdims=True)
    first_grad = dot(grad_ref[...], wt[: 3 * width], 1, 0)
    gain_one = jnp.sum(first_grad * normed, axis=0, keepdims=True)
    shift_one = jnp.sum(first_grad, axis=0, keepdims=True)
    patch_grad = middle_grad + norm_back(first_grad * vec[GAIN1 : GAIN1 + 1], normed, factor)
    rows = jnp.concatenate(
        [gain_one, gain_two, shift_one, value_shift, branch_shift, shift_two, jnp.zeros((2, width), F32)],
        axis=0,
    )
    return mixed, patch_grad.astype(BF16), front_grad, output_grad, rows, table_grad


def forward_kernel(
    x, g, valid, wt, vec, table,
    q, k, v, p, att, inv, middle, second, dispatch, combine, slots, produced_grad,
):
    got = forward_image(
        x[0], g[0], valid[0], wt[...], vec[...], table[...],
        q.at[0], k.at[0], v.at[0], p.at[0], att.at[0], inv.at[0],
    )
    for ref, value in zip((middle, second, dispatch, combine, slots, produced_grad), got):
        ref[0] = value


def backward_kernel(
    x, g, middle, second, dispatch, combine, produced, slot_grad, wt, vec, table,
    q, k, v, p, att, inv,
    mixed, patch_grad, weight_grad, rows, table_grad,
    ds, grad_t, grad,
):
    @pl.when(pl.program_id(0) == 0)
    def _():
        weight_grad[...] = jnp.zeros_like(weight_grad)
        rows[...] = jnp.zeros_like(rows)
        table_grad[...] = jnp.zeros_like(table_grad)

    width = x.shape[-1]
    got = backward_image(
        x[0], g[0], middle[0], second[0], dispatch[0], combine[0], produced[0], slot_grad[0],
        wt[...], vec[...], table[...],
        q.at[0], k.at[0], v.at[0], p.at[0], att.at[0], inv.at[0], ds, grad_t, grad,
    )
    mixed[0] = got[0]
    patch_grad[0] = got[1]
    weight_grad[: 3 * width, :] += got[2]
    weight_grad[3 * width :, :] += got[3]
    rows[...] += got[4]
    table_grad[...] += got[5]


def per_image(*shape):
    return pl.BlockSpec((1,) + shape, lambda i: (i,) + (0,) * len(shape))


def whole(*shape):
    return pl.BlockSpec(shape, lambda i: (0,) * len(shape))


def run_forward(x, g, valid, wt, vec, table):
    count, patches, width = x.shape
    heads = width // HEAD_DIM
    experts = table.shape[0]
    flat = (patches, width)
    outs = [
        (flat, BF16), (flat, BF16), (flat, BF16), ((heads, patches, patches), BF16),
        (flat, BF16), (flat, F32), (flat, F32), (flat, BF16),
        ((experts, patches), F32), ((experts, patches), F32),
        ((experts, width), BF16), ((experts, width), BF16),
    ]
    return pl.pallas_call(
        forward_kernel,
        grid=(count,),
        in_specs=[
            per_image(*flat), per_image(*flat), per_image(1, patches),
            whole(*wt.shape), whole(*vec.shape), whole(*table.shape),
        ],
        out_specs=[per_image(*shape) for shape, _ in outs],
        out_shape=[jax.ShapeDtypeStruct((count,) + shape, kind) for shape, kind in outs],
        compiler_params=pltpu.CompilerParams(vmem_limit_bytes=VMEM_LIMIT),
        name="forward",
    )(x, g, valid, wt, vec, table)


def run_backward(x, g, kept, produced, slot_grad, wt, vec, table):
    count, patches, width = x.shape
    heads = width // HEAD_DIM
    experts = table.shape[0]
    flat = (patches, width)
    q, k, v, p, att, inv, middle, second, dispatch, combine = kept
    return pl.pallas_call(
        backward_kernel,
        grid=(count,),
        in_specs=[
            per_image(*flat), per_image(*flat), per_image(*flat), per_image(*flat),
            per_image(experts, patches), per_image(experts, patches),
            per_image(experts, width), per_image(experts, width),
            whole(*wt.shape), whole(*vec.shape), whole(*table.shape),
            per_image(*flat), per_image(*flat), per_image(*flat),
            per_image(heads, patches, patches), per_image(*flat), per_image(*flat),
        ],
        out_specs=[
            per_image(*flat), per_image(*flat),
            whole(4 * width, width), whole(8, width), whole(experts, width),
        ],
        out_shape=[
            jax.ShapeDtypeStruct(x.shape, BF16), jax.ShapeDtypeStruct(x.shape, BF16),
            jax.ShapeDtypeStruct((4 * width, width), F32), jax.ShapeDtypeStruct((8, width), F32),
            jax.ShapeDtypeStruct((experts, width), F32),
        ],
        scratch_shapes=[
            pltpu.VMEM((2, patches, patches), BF16),
            pltpu.VMEM((3 * width, patches), BF16),
            pltpu.VMEM((patches, 3 * width), BF16),
        ],
        compiler_params=pltpu.CompilerParams(vmem_limit_bytes=VMEM_LIMIT),
        name="backward",
    )(x, g, middle, second, dispatch, combine, produced, slot_grad, wt, vec, table, q, k, v, p, att, inv)


def here():
    return lax.axis_index("wide"), lax.axis_index("narrow")


def along_z(w, z):
    return [(w, lax.rem(z + step, 4)) for step in (1, 2, 3)]


def in_plane(w, z):
    x_flip = 2 - 4 * lax.rem(w // 2, 2)
    y_flip = 4 - 8 * (w // 4)
    return [(w + x_flip, z), (w + y_flip, z), (w + x_flip + y_flip, z)]


def other_core(w, z):
    return (w + 1 - 2 * lax.rem(w, 2), z)


def greet():
    w, z = here()
    barrier = pltpu.get_barrier_semaphore()
    peers = along_z(w, z) + in_plane(w, z) + [other_core(w, z)]
    for peer in peers:
        pl.semaphore_signal(barrier, inc=1, device_id=peer, device_id_type=MESH)
    pl.semaphore_wait(barrier, len(peers))


def remote(src, dst, send, recv, peer):
    return pltpu.make_async_remote_copy(
        src_ref=src, dst_ref=dst, send_sem=send, recv_sem=recv, device_id=peer, device_id_type=MESH
    )


class Gather:
    def __init__(self, every, send, recv):
        self.every, self.send, self.recv = every, send, recv
        self.w, self.z = here()

    def z_copies(self):
        own = self.every.at[self.w, self.z]
        return [
            remote(own, own, self.send.at[n], self.recv.at[n], peer)
            for n, peer in enumerate(along_z(self.w, self.z))
        ]

    def plane_copies(self):
        own = self.every.at[self.w]
        return [
            remote(own, own, self.send.at[3 + n], self.recv.at[3 + n], peer)
            for n, peer in enumerate(in_plane(self.w, self.z))
        ]

    def core_copies(self):
        peer = other_core(self.w, self.z)
        groups = [self.w] + [there for there, _ in in_plane(self.w, self.z)]
        return [
            remote(self.every.at[g], self.every.at[g], self.send.at[6 + n], self.recv.at[6 + n], peer)
            for n, g in enumerate(groups)
        ]

    def start_z(self):
        for copy in self.z_copies():
            copy.start()

    def start_plane(self):
        for copy in self.z_copies():
            copy.wait()
        for copy in self.plane_copies():
            copy.start()
        self.core_copies()[0].start()

    def start_core(self):
        for copy, onward in zip(self.plane_copies(), self.core_copies()[1:]):
            copy.wait()
            onward.start()

    def finish(self):
        for copy in self.core_copies():
            copy.wait()


class Scatter:
    def __init__(self, parts, from_core, chips, from_plane, column, from_z, send, recv):
        self.parts, self.from_core, self.chips = parts, from_core, chips
        self.from_plane, self.column, self.from_z = from_plane, column, from_z
        self.send, self.recv = send, recv
        self.w, self.z = here()
        self.core = lax.rem(self.w, 2)

    def core_copies(self):
        peer = other_core(self.w, self.z)
        return [
            remote(
                self.parts.at[2 * chip + 1 - self.core], self.from_core.at[chip],
                self.send.at[chip], self.recv.at[chip], peer,
            )
            for chip in range(4)
        ]

    def plane_copies(self):
        return [
            remote(
                self.chips.at[peer[0] // 2], self.from_plane.at[n],
                self.send.at[4 + n], self.recv.at[4 + n], peer,
            )
            for n, peer in enumerate(in_plane(self.w, self.z))
        ]

    def z_copies(self):
        return [
            remote(
                self.column.at[peer[1]], self.from_z.at[n],
                self.send.at[7 + n], self.recv.at[7 + n], peer,
            )
            for n, peer in enumerate(along_z(self.w, self.z))
        ]

    def start_core(self):
        for copy in self.core_copies():
            copy.start()

    def start_plane(self):
        for chip, copy in enumerate(self.core_copies()):
            copy.wait()
            own = self.parts[2 * chip + self.core].astype(F32)
            self.chips[chip] = (own + self.from_core[chip].astype(F32)).astype(BF16)
        for copy in self.plane_copies():
            copy.start()

    def start_z(self):
        for copy in self.plane_copies():
            copy.wait()
        total = self.chips[self.w // 2].astype(F32)
        for n in range(3):
            total = total + self.from_plane[n].astype(F32)
        self.column[...] = total.astype(BF16)
        for copy in self.z_copies():
            copy.start()

    def finish(self):
        for copy in self.z_copies():
            copy.wait()
        total = self.column[self.z].astype(F32)
        for n in range(3):
            total = total + self.from_z[n].astype(F32)
        return total


def gather_scratch(rows, width):
    return [
        pltpu.VMEM((8, 4, rows, width), BF16),
        pltpu.SemaphoreType.DMA((10,)),
        pltpu.SemaphoreType.DMA((10,)),
    ]


def scatter_scratch(rows, width):
    return [
        pltpu.VMEM((8, 4, rows, width), BF16),
        pltpu.VMEM((4, 4, rows, width), BF16),
        pltpu.VMEM((4, 4, rows, width), BF16),
        pltpu.VMEM((3, 4, rows, width), BF16),
        pltpu.VMEM((4, rows, width), BF16),
        pltpu.VMEM((3, rows, width), BF16),
        pltpu.SemaphoreType.DMA((10,)),
        pltpu.SemaphoreType.DMA((10,)),
    ]

def gather_kernel(own, out, every, send, recv):
    w, z = here()
    every[w, z] = own[...]
    greet()
    gather = Gather(every, send, recv)
    gather.start_z()
    gather.start_plane()
    gather.start_core()
    gather.finish()
    out[...] = every[...]


def run_gather(own):
    rows, width = own.shape
    return pl.pallas_call(
        gather_kernel,
        out_shape=jax.ShapeDtypeStruct((8, 4, rows, width), BF16),
        in_specs=[pl.BlockSpec(memory_space=pltpu.VMEM)],
        out_specs=pl.BlockSpec(memory_space=pltpu.VMEM),
        scratch_shapes=gather_scratch(rows, width),
        compiler_params=pltpu.CompilerParams(
            collective_id=0, has_side_effects=True, vmem_limit_bytes=VMEM_LIMIT
        ),
        name="gather",
    )(own)


def scatter_kernel(parts_in, out, parts, *rest):
    parts[...] = parts_in[...].astype(BF16)
    greet()
    scatter = Scatter(parts, *rest)
    scatter.start_core()
    scatter.start_plane()
    scatter.start_z()
    out[...] = scatter.finish()


def run_scatter(parts):
    _, rows, width = parts.shape
    return pl.pallas_call(
        scatter_kernel,
        out_shape=jax.ShapeDtypeStruct((rows, width), F32),
        in_specs=[pl.BlockSpec(memory_space=pltpu.VMEM)],
        out_specs=pl.BlockSpec(memory_space=pltpu.VMEM),
        scratch_shapes=scatter_scratch(rows, width),
        compiler_params=pltpu.CompilerParams(
            collective_id=1, has_side_effects=True, vmem_limit_bytes=VMEM_LIMIT
        ),
        name="scatter",
    )(parts.reshape(8, 4, rows, width))


def expert_rows(slots, grads, w_in, bias, w_out):
    rows, width = slots.shape
    units = w_in.shape[0]
    shape = (rows, units)
    own = lax.rem(lax.broadcasted_iota(jnp.int32, shape, 0), 8)
    start = own * (units // 8)
    lane = lax.broadcasted_iota(jnp.int32, shape, 1)
    keep = (lane >= start) & (lane < start + units // 8)
    hidden = dot(slots, w_in, 1, 1) + bias
    active_grad = dot(grads, w_out, 1, 1)
    half = 0.5 * (1.0 + lax.erf(hidden * 0.7071067811865476))
    active = jnp.where(keep, hidden * half, 0.0).astype(BF16)
    slope = half + hidden * jnp.exp(hidden * hidden * -0.5) * 0.3989422804014327
    hidden_grad = jnp.where(keep, active_grad * slope, 0.0).astype(BF16)
    produced = dot(active, w_out, 1, 0).astype(BF16)
    slot_grad = dot(hidden_grad, w_in, 1, 0).astype(BF16)
    in_grad = dot(hidden_grad, slots, 0, 0)
    out_grad = dot(active, grads, 0, 0)
    bias_grad = jnp.sum(hidden_grad.astype(F32), axis=0, keepdims=True)
    return produced, slot_grad, in_grad, out_grad, bias_grad


def experts_kernel(
    slots, grads, w_in, bias, w_out, produced, slot_grad, in_grad, out_grad, bias_grad,
    every, g_send, g_recv, parts, *rest,
):
    w, z = here()
    count = slots.shape[0]
    every[w, z, :count] = slots[...]
    every[w, z, count:] = grads[...]
    greet()
    gather = Gather(every, g_send, g_recv)
    gather.start_z()
    gather.start_plane()
    gather.start_core()
    gather.finish()
    in_grad[...] = jnp.zeros_like(in_grad)
    out_grad[...] = jnp.zeros_like(out_grad)
    bias_grad[...] = jnp.zeros_like(bias_grad)
    width = slots.shape[1]
    rows = 8 * count

    def step(n, carry):
        at = pl.ds(n * 2, 2)
        got = expert_rows(
            every[at, :, :count].reshape(rows, width), every[at, :, count:].reshape(rows, width),
            w_in[...], bias[...], w_out[...],
        )
        parts[at, :, :count] = got[0].reshape(2, 4, count, width)
        parts[at, :, count:] = got[1].reshape(2, 4, count, width)
        in_grad[...] += got[2]
        out_grad[...] += got[3]
        bias_grad[...] += got[4]
        return carry

    lax.fori_loop(0, 4, step, 0)
    scatter = Scatter(parts, *rest)
    scatter.start_core()
    scatter.start_plane()
    scatter.start_z()
    total = scatter.finish()
    produced[...] = total[:count]
    slot_grad[...] = total[count:]


def run_experts(slots, grads, w_in, bias, w_out):
    count, width = slots.shape
    units = w_in.shape[0]
    full = pl.BlockSpec(memory_space=pltpu.VMEM)
    return pl.pallas_call(
        experts_kernel,
        out_shape=[
            jax.ShapeDtypeStruct((count, width), F32), jax.ShapeDtypeStruct((count, width), F32),
            jax.ShapeDtypeStruct((units, width), F32), jax.ShapeDtypeStruct((units, width), F32),
            jax.ShapeDtypeStruct((1, units), F32),
        ],
        in_specs=[full] * 5,
        out_specs=[full] * 5,
        scratch_shapes=gather_scratch(2 * count, width) + scatter_scratch(2 * count, width),
        compiler_params=pltpu.CompilerParams(
            collective_id=2, has_side_effects=True, vmem_limit_bytes=VMEM_LIMIT
        ),
        name="experts",
    )(slots, grads, w_in, bias, w_out)


def scatter_sum(parts):
    got = lax.all_to_all(parts.astype(BF16), AXES, 0, 0, tiled=True)
    return jnp.sum(got.astype(F32), axis=0)


def experts_at_home(slots, produced_grad, expert_in, expert_in_bias, expert_out, devices):
    local_images, experts, width = slots.shape
    every = lax.all_gather(jnp.stack([slots, produced_grad]), AXES, axis=1, tiled=True)
    all_slots, all_grads = every[0], every[1]
    hidden = jnp.einsum(
        "bed,edf->bef", all_slots, expert_in, preferred_element_type=F32
    ) + expert_in_bias.astype(F32)
    active, gelu_back = jax.vjp(smooth, hidden)
    active = active.astype(BF16)
    partial = jnp.einsum("bef,efd->bed", active, expert_out, preferred_element_type=F32)
    active_grad = jnp.einsum("bed,efd->bef", all_grads, expert_out, preferred_element_type=F32)
    hidden_grad = gelu_back(active_grad)[0].astype(BF16)
    partial_back = jnp.einsum("bef,edf->bed", hidden_grad, expert_in, preferred_element_type=F32)
    contract_grad = jnp.einsum("bef,bed->efd", active, all_grads, preferred_element_type=F32)
    expand_grad = jnp.einsum("bed,bef->edf", all_slots, hidden_grad, preferred_element_type=F32)
    inner_grad = jnp.sum(hidden_grad.astype(F32), axis=0)
    both = jnp.stack([partial, partial_back]).reshape(2, devices, local_images, experts, width)
    both = scatter_sum(jnp.moveaxis(both, 1, 0))
    return (both[0], both[1], expand_grad, inner_grad, contract_grad)


def on_device(
    patches,
    valid,
    attn_weights,
    norm_gains,
    vec_biases,
    slot_params,
    expert_in,
    expert_in_bias,
    expert_out,
    expert_out_bias,
    out_grad,
):
    local_images, patch_count, width = patches.shape
    experts = expert_in.shape[0]
    devices = lax.axis_size("wide") * lax.axis_size("narrow")

    vectors = (norm_gains, vec_biases, slot_params, expert_out_bias)
    lengths = [v.shape[0] for v in vectors]
    small = jnp.concatenate(vectors)
    by_hand = lax.axis_size("wide") == 8 and lax.axis_size("narrow") == 4
    if by_hand:
        rows = attn_weights.shape[1]
        every = run_gather(
            jnp.concatenate([attn_weights.T, jnp.pad(small[None], ((0, 15), (0, width - small.shape[0])))])
        )
        wt = every[:, :, :rows].reshape(-1, width)
        small = every[:, :, rows].reshape(devices, width)
    else:
        wt = lax.all_gather(attn_weights.T, AXES, axis=0, tiled=True)
        small = lax.all_gather(small, AXES)
    pieces = []
    at = 0
    for length in lengths:
        pieces.append(small[:, at : at + length].reshape(-1, width))
        at += length
    gains, biases, table, expert_shift = pieces
    vec = jnp.concatenate([gains, biases, jnp.zeros((2, width), BF16)]).astype(F32)

    *kept, slots, produced_grad = run_forward(
        patches, out_grad, valid.reshape(local_images, 1, patch_count), wt, vec, table
    )
    if by_hand:
        units = expert_in.shape[2]
        produced, slot_grad, expand_grad, contract_grad, inner_grad = run_experts(
            slots.reshape(-1, width), produced_grad.reshape(-1, width),
            expert_in.transpose(0, 2, 1).reshape(experts * units, width),
            expert_in_bias.reshape(1, experts * units).astype(F32),
            expert_out.reshape(experts * units, width),
        )
        produced = produced.reshape(slots.shape)
        slot_grad = slot_grad.reshape(slots.shape)
        expand_grad = expand_grad.reshape(experts, units, width).transpose(0, 2, 1)
        contract_grad = contract_grad.reshape(experts, units, width)
        inner_grad = inner_grad.reshape(experts, units)
    else:
        produced, slot_grad, expand_grad, inner_grad, contract_grad = experts_at_home(
            slots, produced_grad, expert_in, expert_in_bias, expert_out, devices
        )
    produced = (produced + expert_shift.astype(F32)).astype(BF16)
    slot_grad = slot_grad.astype(BF16)
    shift_grad = jnp.sum(produced_grad.astype(F32), axis=0)
    mixed_out, patch_grad, weight_grad, rows, table_grad = run_backward(
        patches, out_grad, kept, produced, slot_grad, wt, vec, table
    )
    weight_grad = weight_grad.reshape(devices, -1, width)
    small_grads = jnp.concatenate(
        [v.reshape(devices, -1) for v in (rows[:2], rows[2:6], table_grad, shift_grad)], axis=1
    )
    if by_hand:
        small_grads = jnp.pad(
            small_grads[:, None], ((0, 0), (0, 15), (0, width - small_grads.shape[1]))
        )
        total = run_scatter(jnp.concatenate([weight_grad, small_grads], axis=1))
        small_grads = total[weight_grad.shape[1]]
        weight_grad = total[: weight_grad.shape[1]].T
    else:
        weight_grad = scatter_sum(weight_grad).T
        small_grads = jnp.sum(lax.all_to_all(small_grads, AXES, 0, 0, tiled=True), axis=0)
    grads = []
    at = 0
    for length in lengths:
        grads.append(small_grads[at : at + length])
        at += length
    return (
        mixed_out,
        patch_grad,
        weight_grad,
        grads[0],
        grads[1],
        grads[2],
        expand_grad,
        inner_grad,
        contract_grad,
        grads[3],
    )


def solution(mesh):
    images = P(AXES, None, None)
    vector = P(AXES)
    second = P(None, AXES)
    return jax.shard_map(
        on_device,
        mesh=mesh,
        in_specs=(
            images, P(AXES, None), second, vector, vector, vector,
            P(None, None, AXES), second, P(None, AXES, None), vector, images,
        ),
        out_specs=(
            images, images, second, vector, vector, vector,
            P(None, None, AXES), second, P(None, AXES, None), vector,
        ),
        check_vma=False,
    )
```

```python
import functools

import jax
import jax.numpy as jnp
from jax import lax
from jax.experimental import pallas as pl
from jax.experimental.pallas import tpu as pltpu
from jax.sharding import PartitionSpec as P

HEAD_DIM = 64
PAIR = 2 * HEAD_DIM
MASKED = -1000000000.0
AXES = ("wide", "narrow")
BF16 = jnp.bfloat16
F32 = jnp.float32
MESH = pl.DeviceIdType.MESH
VMEM_LIMIT = 60 * 1024 * 1024
LAYER_LIMIT = 63 * 1024 * 1024
GAIN1, GAIN2, BIAS1, VBIAS, OBIAS, BIAS2 = range(6)


def dot(left, right, left_dim, right_dim):
    return lax.dot_general(
        left, right, (((left_dim,), (right_dim,)), ((), ())), preferred_element_type=F32
    )


def normalize(values):
    centred = values - jnp.mean(values, axis=-1, keepdims=True)
    factor = lax.rsqrt(jnp.mean(centred * centred, axis=-1, keepdims=True) + 1e-06)
    return (centred * factor, factor)


def norm_back(grad_hat, normed, factor):
    return factor * (
        grad_hat
        - jnp.mean(grad_hat, axis=-1, keepdims=True)
        - normed * jnp.mean(grad_hat * normed, axis=-1, keepdims=True)
    )


def smooth(values):
    return jax.nn.gelu(values, approximate=False)


def lower_half(shape):
    return lax.broadcasted_iota(jnp.int32, shape, 1) < HEAD_DIM


def own_half(low, head, own, other):
    return jnp.where(low, own, other) if head % 2 == 0 else jnp.where(low, other, own)


def forward_image(
    x, g, valid_row, wt, vec, table, q_ref, k_ref, v_ref, p_ref, att_ref, inv_ref,
    before_heads=None, after_head=None,
):
    patches, width = x.shape
    heads = width // HEAD_DIM
    images = x[...].astype(F32)
    normed, _ = normalize(images)
    first = (normed * vec[GAIN1 : GAIN1 + 1] + vec[BIAS1 : BIAS1 + 1]).astype(BF16)
    q_ref[...] = (dot(first, wt[:width], 1, 1) * HEAD_DIM ** (-0.5)).astype(BF16)
    k_ref[...] = dot(first, wt[width : 2 * width], 1, 1).astype(BF16)
    v_ref[...] = (dot(first, wt[2 * width : 3 * width], 1, 1) + vec[VBIAS : VBIAS + 1]).astype(BF16)
    if before_heads is not None:
        before_heads()
    bias_row = jnp.where(valid_row > 0, 0.0, MASKED).astype(F32)
    fill = jnp.broadcast_to(bias_row * (1.0 / HEAD_DIM), (PAIR, patches)).T.astype(BF16)
    low = lower_half((patches, PAIR))
    one = jnp.ones((patches, PAIR), BF16)
    scores = {}

    def pair_of(ref, head):
        at = head // 2 * PAIR
        return ref[:, at : at + PAIR]

    def score(head):
        scores[head] = dot(
            own_half(low, head, pair_of(q_ref, head), one),
            own_half(low, head, pair_of(k_ref, head), fill),
            1,
            1,
        )

    sums = {}
    score(0)
    for head in range(heads):
        if head + 1 < heads:
            score(head + 1)
        raw = scores.pop(head)
        prob = jnp.exp(raw - jnp.max(raw, axis=1, keepdims=True)).astype(BF16)
        p_ref[head] = prob
        sums[head] = dot(prob, own_half(low, head, pair_of(v_ref, head), one), 1, 0)
        if after_head is not None:
            after_head(head)
        if head % 2 == 1:
            even, odd = sums.pop(head - 1), sums.pop(head)
            inverse = 1.0 / pltpu.roll(jnp.where(low, odd, even), HEAD_DIM, 1)
            at = head // 2 * PAIR
            inv_ref[:, at : at + PAIR] = inverse.astype(inv_ref.dtype)
            att_ref[:, at : at + PAIR] = (jnp.where(low, even, odd) * inverse).astype(BF16)
    branch = dot(att_ref[...], wt[3 * width :], 1, 1)
    middle = images + branch + vec[OBIAS : OBIAS + 1]
    normed, _ = normalize(middle)
    second = (normed * vec[GAIN2 : GAIN2 + 1] + vec[BIAS2 : BIAS2 + 1]).astype(BF16)
    logits = dot(table, second, 1, 1)
    masked = jnp.where(valid_row > 0, logits, MASKED)
    dispatch = jnp.exp(masked - jnp.max(masked, axis=1, keepdims=True))
    dispatch = dispatch / jnp.sum(dispatch, axis=1, keepdims=True)
    combine = jnp.exp(logits - jnp.max(logits, axis=0, keepdims=True))
    combine = combine / jnp.sum(combine, axis=0, keepdims=True)
    slots = dot(dispatch.astype(BF16), second, 1, 0)
    produced_grad = dot(combine.astype(BF16), g[...], 1, 0)
    return middle, dispatch, combine, slots, produced_grad


def backward_image(
    x, g, middle_ref, dispatch, combine, produced, slot_grad, wt, vec, table,
    q_ref, k_ref, v_ref, p_ref, att_ref, inv_ref, ds_ref, grad_t_ref, dq_ref, dk_ref, dv_ref, mixed_ref,
    before_heads=None, before_head=None, after_heads=None,
):
    patches, width = x.shape
    heads = width // HEAD_DIM
    combine_low = combine.astype(BF16)
    dispatch_low = dispatch.astype(BF16)
    middle = middle_ref[...]
    normed, factor = normalize(middle)
    second = (normed * vec[GAIN2 : GAIN2 + 1] + vec[BIAS2 : BIAS2 + 1]).astype(BF16)
    upstream = g[...]
    mixed = (middle + dot(combine_low, produced, 0, 0)).astype(BF16)
    combine_grad = dot(produced, upstream, 1, 1)
    dispatch_grad = dot(slot_grad, second, 1, 1)
    logit_grad = dispatch * (
        dispatch_grad - jnp.sum(dispatch * dispatch_grad, axis=1, keepdims=True)
    ) + combine * (combine_grad - jnp.sum(combine * combine_grad, axis=0, keepdims=True))
    logit_grad = logit_grad.astype(BF16)
    table_grad = dot(logit_grad, second, 1, 0)
    second_grad = dot(
        jnp.concatenate([dispatch_low, logit_grad], axis=0),
        jnp.concatenate([slot_grad, table], axis=0),
        0,
        0,
    )
    gain_two = jnp.sum(second_grad * normed, axis=0, keepdims=True)
    shift_two = jnp.sum(second_grad, axis=0, keepdims=True)
    middle_grad = upstream.astype(F32) + norm_back(
        second_grad * vec[GAIN2 : GAIN2 + 1], normed, factor
    )
    mixed_ref[...] = mixed
    branch_grad = middle_grad.astype(BF16)
    branch_shift = jnp.sum(branch_grad.astype(F32), axis=0, keepdims=True)
    output_grad = dot(branch_grad.T, att_ref[...], 1, 0)
    attended_grad = dot(branch_grad, wt[3 * width :], 1, 0).astype(BF16).astype(F32)
    scaled = attended_grad * inv_ref[...].astype(F32)
    drop = (-(scaled * att_ref[...].astype(F32))).astype(BF16)
    scaled = scaled.astype(BF16)
    scaled_t = scaled.T
    query_t = q_ref[...].T
    if before_heads is not None:
        before_heads()
    low = lower_half((patches, PAIR))
    one = jnp.ones((patches, PAIR), BF16)
    prob_grads = {}

    def pair_of(ref, head):
        at = head // 2 * PAIR
        return ref[:, at : at + PAIR]

    def prob_grad(head):
        rolled = pltpu.roll(pair_of(drop, head).astype(F32), HEAD_DIM, 1).astype(BF16)
        prob_grads[head] = dot(
            own_half(low, head, pair_of(scaled, head), rolled),
            own_half(low, head, pair_of(v_ref, head), one),
            1,
            1,
        )

    query_grads = {}
    prob_grad(0)
    for head in range(heads):
        if head + 1 < heads:
            prob_grad(head + 1)
        if before_head is not None:
            before_head(head)
        rows = slice(head * HEAD_DIM, (head + 1) * HEAD_DIM)
        prob = p_ref[head]
        grad_t_ref[width + rows.start : width + rows.stop, :] = dot(
            scaled_t[rows], prob, 1, 0
        ).astype(BF16)
        score_grad = (prob.astype(F32) * prob_grads.pop(head)).astype(BF16)
        ds_ref[head % 2] = score_grad
        score_grad = ds_ref[head % 2]
        query_grads[head] = dot(score_grad, pair_of(k_ref, head), 1, 0)
        grad_t_ref[rows, :] = dot(query_t[rows], score_grad, 1, 0).astype(BF16)
        if head % 2 == 1:
            both = jnp.where(low, query_grads.pop(head - 1), query_grads.pop(head))
            at = head // 2 * PAIR
            dq_ref[:, at : at + PAIR] = (both * HEAD_DIM ** (-0.5)).astype(BF16)
    if after_heads is not None:
        after_heads()
    dk_ref[...] = grad_t_ref[:width, :].T
    dv_ref[...] = grad_t_ref[width:, :].T
    normed, factor = normalize(x[...].astype(F32))
    first = (normed * vec[GAIN1 : GAIN1 + 1] + vec[BIAS1 : BIAS1 + 1]).astype(BF16)
    query_front = dot(dq_ref[...].T, first, 1, 0)
    other_front = dot(grad_t_ref[...], first, 1, 0)
    value_shift = jnp.sum(dv_ref[...].astype(F32), axis=0, keepdims=True)
    project_grad = jnp.concatenate([dq_ref[...], dk_ref[...], dv_ref[...]], axis=1)
    first_grad = dot(project_grad, wt[: 3 * width], 1, 0)
    gain_one = jnp.sum(first_grad * normed, axis=0, keepdims=True)
    shift_one = jnp.sum(first_grad, axis=0, keepdims=True)
    patch_grad = middle_grad + norm_back(first_grad * vec[GAIN1 : GAIN1 + 1], normed, factor)
    sums = jnp.concatenate(
        [gain_one, gain_two, shift_one, value_shift, branch_shift, shift_two, jnp.zeros((2, width), F32)],
        axis=0,
    )
    return patch_grad.astype(BF16), query_front, other_front, output_grad, sums, table_grad


def forward_kernel(
    x, g, valid, wt, vec, table,
    q, k, v, p, att, inv, middle, dispatch, combine, slots, produced_grad,
):
    got = forward_image(
        x.at[0], g.at[0], valid[0], wt, vec[...], table[...],
        q.at[0], k.at[0], v.at[0], p.at[0], att.at[0], inv.at[0],
    )
    for ref, value in zip((middle, dispatch, combine, slots, produced_grad), got):
        ref[0] = value.astype(ref.dtype)


def add_grads(weight_grad, sums, table_grad, got):
    width = weight_grad.shape[1]
    for ref, at, value in (
        (weight_grad, 0, got[1]), (weight_grad, width, got[2]), (weight_grad, 3 * width, got[3]),
        (sums, 0, got[4]), (table_grad, 0, got[5]),
    ):
        ref[at : at + value.shape[0], :] += value


def backward_kernel(
    x, g, middle, dispatch, combine, produced, slot_grad, wt, vec, table,
    q, k, v, p, att, inv,
    mixed, patch_grad, weight_grad, sums, table_grad,
    ds, grad_t, dq, dk, dv,
):
    @pl.when(pl.program_id(0) == 0)
    def _():
        weight_grad[...] = jnp.zeros_like(weight_grad)
        sums[...] = jnp.zeros_like(sums)
        table_grad[...] = jnp.zeros_like(table_grad)

    got = backward_image(
        x.at[0], g.at[0], middle.at[0], dispatch[0], combine[0], produced[0], slot_grad[0],
        wt, vec[...], table[...],
        q.at[0], k.at[0], v.at[0], p.at[0], att.at[0], inv.at[0], ds, grad_t, dq, dk, dv, mixed.at[0],
    )
    patch_grad[0] = got[0]
    add_grads(weight_grad, sums, table_grad, got)


def per_image(*shape):
    return pl.BlockSpec((1,) + shape, lambda i: (i,) + (0,) * len(shape))


def whole(*shape):
    return pl.BlockSpec(shape, lambda i: (0,) * len(shape))


def run_forward(x, g, valid, wt, vec, table):
    count, patches, width = x.shape
    heads = width // HEAD_DIM
    experts = table.shape[0]
    flat = (patches, width)
    outs = [
        (flat, BF16), (flat, BF16), (flat, BF16), ((heads, patches, patches), BF16),
        (flat, BF16), (flat, F32), (flat, F32),
        ((experts, patches), F32), ((experts, patches), F32),
        ((experts, width), BF16), ((experts, width), BF16),
    ]
    return pl.pallas_call(
        forward_kernel,
        grid=(count,),
        in_specs=[
            per_image(*flat), per_image(*flat), per_image(1, patches),
            whole(*wt.shape), whole(*vec.shape), whole(*table.shape),
        ],
        out_specs=[per_image(*shape) for shape, _ in outs],
        out_shape=[jax.ShapeDtypeStruct((count,) + shape, kind) for shape, kind in outs],
        compiler_params=pltpu.CompilerParams(vmem_limit_bytes=VMEM_LIMIT),
        name="forward",
    )(x, g, valid, wt, vec, table)


def run_backward(x, g, kept, produced, slot_grad, wt, vec, table):
    count, patches, width = x.shape
    heads = width // HEAD_DIM
    experts = table.shape[0]
    flat = (patches, width)
    q, k, v, p, att, inv, middle, dispatch, combine = kept
    return pl.pallas_call(
        backward_kernel,
        grid=(count,),
        in_specs=[
            per_image(*flat), per_image(*flat), per_image(*flat),
            per_image(experts, patches), per_image(experts, patches),
            per_image(experts, width), per_image(experts, width),
            whole(*wt.shape), whole(*vec.shape), whole(*table.shape),
            per_image(*flat), per_image(*flat), per_image(*flat),
            per_image(heads, patches, patches), per_image(*flat), per_image(*flat),
        ],
        out_specs=[
            per_image(*flat), per_image(*flat),
            whole(4 * width, width), whole(8, width), whole(experts, width),
        ],
        out_shape=[
            jax.ShapeDtypeStruct(x.shape, BF16), jax.ShapeDtypeStruct(x.shape, BF16),
            jax.ShapeDtypeStruct((4 * width, width), F32), jax.ShapeDtypeStruct((8, width), F32),
            jax.ShapeDtypeStruct((experts, width), F32),
        ],
        scratch_shapes=[
            pltpu.VMEM((2, patches, patches), BF16),
            pltpu.VMEM((2 * width, patches), BF16),
            pltpu.VMEM(flat, BF16),
            pltpu.VMEM(flat, BF16),
            pltpu.VMEM(flat, BF16),
        ],
        compiler_params=pltpu.CompilerParams(vmem_limit_bytes=VMEM_LIMIT),
        name="backward",
    )(x, g, middle, dispatch, combine, produced, slot_grad, wt, vec, table, q, k, v, p, att, inv)


def here():
    return lax.axis_index("wide"), lax.axis_index("narrow")


def along_z(w, z):
    return [(w, lax.rem(z + step, 4)) for step in (1, 2, 3)]


def in_plane(w, z):
    x_flip = 2 - 4 * lax.rem(w // 2, 2)
    y_flip = 4 - 8 * (w // 4)
    return [(w + x_flip, z), (w + y_flip, z), (w + x_flip + y_flip, z)]


def other_core(w, z):
    return (w + 1 - 2 * lax.rem(w, 2), z)


def greet():
    w, z = here()
    barrier = pltpu.get_barrier_semaphore()
    peers = along_z(w, z) + in_plane(w, z) + [other_core(w, z)]
    for peer in peers:
        pl.semaphore_signal(barrier, inc=1, device_id=peer, device_id_type=MESH)
    pl.semaphore_wait(barrier, len(peers))


def remote(src, dst, send, recv, peer):
    return pltpu.make_async_remote_copy(
        src_ref=src, dst_ref=dst, send_sem=send, recv_sem=recv, device_id=peer, device_id_type=MESH
    )


class Gather:
    def __init__(self, every, send, recv):
        self.every, self.send, self.recv = every, send, recv
        self.w, self.z = here()

    def z_copies(self):
        own = self.every.at[self.w, self.z]
        return [
            remote(own, own, self.send.at[n], self.recv.at[n], peer)
            for n, peer in enumerate(along_z(self.w, self.z))
        ]

    def plane_copies(self):
        own = self.every.at[self.w]
        return [
            remote(own, own, self.send.at[3 + n], self.recv.at[3 + n], peer)
            for n, peer in enumerate(in_plane(self.w, self.z))
        ]

    def core_copies(self):
        peer = other_core(self.w, self.z)
        groups = [self.w] + [there for there, _ in in_plane(self.w, self.z)]
        return [
            remote(self.every.at[g], self.every.at[g], self.send.at[6 + n], self.recv.at[6 + n], peer)
            for n, g in enumerate(groups)
        ]

    def start_z(self):
        for copy in self.z_copies():
            copy.start()

    def start_plane(self):
        for copy in self.z_copies():
            copy.wait()
        for copy in self.plane_copies():
            copy.start()
        self.core_copies()[0].start()

    def start_core(self):
        for copy, onward in zip(self.plane_copies(), self.core_copies()[1:]):
            copy.wait()
            onward.start()

    def finish(self):
        for copy in self.core_copies():
            copy.wait()


class Scatter:
    def __init__(self, parts, from_core, chips, from_plane, column, from_z, send, recv):
        self.parts, self.from_core, self.chips = parts, from_core, chips
        self.from_plane, self.column, self.from_z = from_plane, column, from_z
        self.send, self.recv = send, recv
        self.w, self.z = here()
        self.core = lax.rem(self.w, 2)

    def core_copies(self):
        peer = other_core(self.w, self.z)
        return [
            remote(
                self.parts.at[2 * chip + 1 - self.core], self.from_core.at[chip],
                self.send.at[chip], self.recv.at[chip], peer,
            )
            for chip in range(4)
        ]

    def plane_copies(self):
        return [
            remote(
                self.chips.at[peer[0] // 2], self.from_plane.at[n],
                self.send.at[4 + n], self.recv.at[4 + n], peer,
            )
            for n, peer in enumerate(in_plane(self.w, self.z))
        ]

    def z_copies(self):
        return [
            remote(
                self.column.at[peer[1]], self.from_z.at[n],
                self.send.at[7 + n], self.recv.at[7 + n], peer,
            )
            for n, peer in enumerate(along_z(self.w, self.z))
        ]

    def start_core(self):
        for copy in self.core_copies():
            copy.start()

    def start_plane(self):
        for chip, copy in enumerate(self.core_copies()):
            copy.wait()
            own = self.parts[2 * chip + self.core].astype(F32)
            self.chips[chip] = (own + self.from_core[chip].astype(F32)).astype(BF16)
        for copy in self.plane_copies():
            copy.start()

    def start_z(self):
        for copy in self.plane_copies():
            copy.wait()
        total = self.chips[self.w // 2].astype(F32)
        for n in range(3):
            total = total + self.from_plane[n].astype(F32)
        self.column[...] = total.astype(BF16)
        for copy in self.z_copies():
            copy.start()

    def finish(self):
        for copy in self.z_copies():
            copy.wait()
        total = self.column[self.z].astype(F32)
        for n in range(3):
            total = total + self.from_z[n].astype(F32)
        return total


def gather_scratch(rows, width):
    return [
        pltpu.VMEM((8, 4, rows, width), BF16),
        pltpu.SemaphoreType.DMA((10,)),
        pltpu.SemaphoreType.DMA((10,)),
    ]


def scatter_scratch(rows, width):
    return [
        pltpu.VMEM((8, 4, rows, width), BF16),
        pltpu.VMEM((4, 4, rows, width), BF16),
        pltpu.VMEM((4, 4, rows, width), BF16),
        pltpu.VMEM((3, 4, rows, width), BF16),
        pltpu.VMEM((4, rows, width), BF16),
        pltpu.VMEM((3, rows, width), BF16),
        pltpu.SemaphoreType.DMA((10,)),
        pltpu.SemaphoreType.DMA((10,)),
    ]

def expert_rows(slots, grads, w_in, bias, w_out):
    rows, width = slots.shape
    units = w_in.shape[0]
    shape = (rows, units)
    own = lax.rem(lax.broadcasted_iota(jnp.int32, shape, 0), 8)
    start = own * (units // 8)
    lane = lax.broadcasted_iota(jnp.int32, shape, 1)
    keep = (lane >= start) & (lane < start + units // 8)
    hidden = dot(slots, w_in, 1, 1) + bias
    active_grad = dot(grads, w_out, 1, 1)
    half = 0.5 * (1.0 + lax.erf(hidden * 0.7071067811865476))
    active = jnp.where(keep, hidden * half, 0.0).astype(BF16)
    slope = half + hidden * jnp.exp(hidden * hidden * -0.5) * 0.3989422804014327
    hidden_grad = jnp.where(keep, active_grad * slope, 0.0).astype(BF16)
    produced = dot(active, w_out, 1, 0)
    slot_grad = dot(hidden_grad, w_in, 1, 0)
    in_grad = dot(hidden_grad, slots, 0, 0)
    out_grad = dot(active, grads, 0, 0)
    bias_grad = jnp.sum(hidden_grad.astype(F32), axis=0, keepdims=True)
    return produced, slot_grad, in_grad, out_grad, bias_grad


def lanes_of(length, offset, width, transposed=False):
    row = lax.broadcasted_iota(jnp.int32, (width, width), 1 if transposed else 0)
    column = lax.broadcasted_iota(jnp.int32, (width, width), 0 if transposed else 1)
    return (row == offset + lax.rem(column, length)).astype(BF16)


def spread(blocks, length, offset):
    width = blocks.shape[1]
    per_row = width // length
    wide = dot(blocks, lanes_of(length, offset, width), 1, 0)
    row = lax.broadcasted_iota(jnp.int32, wide.shape, 0)
    column = lax.broadcasted_iota(jnp.int32, wide.shape, 1)
    keep = (lax.rem(row, 16) == 0) & (lax.rem(row // 16, per_row) == column // length)
    wide = jnp.where(keep, wide, 0.0)
    return jnp.sum(wide.reshape(-1, per_row * 16, width), axis=1)


def gather_up(rows, length, offset):
    count, width = rows.shape
    per_row = width // length
    tall = jnp.broadcast_to(rows[:, None], (count, per_row, width)).reshape(32, width)
    row = lax.broadcasted_iota(jnp.int32, tall.shape, 0)
    column = lax.broadcasted_iota(jnp.int32, tall.shape, 1)
    tall = jnp.where(lax.rem(row, per_row) == column // length, tall, 0.0)
    return dot(tall.astype(BF16), lanes_of(length, offset, width, True), 1, 0)


def layer_kernel(
    lengths,
    x_hbm, g_hbm, valid, own_weights, own_vectors, w_in, own_bias, w_out,
    mixed_hbm, patch_grad_hbm, p_hbm, weight_out, vectors_out, in_grad, out_grad, bias_grad,
    x, g, q, k, v, att, inv, middle, dispatch, combine, p, ds, grad_t, wt, vec, table, shift, bias,
    weight_grad, sums, table_grad, shift_grad,
    x_sem, g_sem, p_out_sem, p_in_sem, mixed_sem, patch_sem,
    w_every, w_send, w_recv,
    every, g_send, g_recv,
    parts, from_core, chips, from_plane, column, from_z, s_send, s_recv,
    *last,
):
    count, patches, width = x.shape
    heads = width // HEAD_DIM
    rows = own_weights.shape[0]
    wide, narrow = here()

    for i in range(count):
        pltpu.make_async_copy(x_hbm.at[i], x.at[i], x_sem.at[i]).start()
        pltpu.make_async_copy(g_hbm.at[i], g.at[i], g_sem.at[i]).start()
    w_every[wide, narrow, :rows] = own_weights[...]
    row = lax.broadcasted_iota(jnp.int32, (16, width), 0)
    w_every[wide, narrow, rows:] = jnp.where(
        row == 0, jnp.broadcast_to(own_vectors[...].astype(F32), (16, width)), 0.0
    ).astype(BF16)
    greet()
    weights = Gather(w_every, w_send, w_recv)
    weights.start_z()
    for ref in (weight_grad, sums, table_grad, shift_grad, in_grad, out_grad, bias_grad):
        ref[...] = jnp.zeros_like(ref)
    units = w_in.shape[0] // 8
    spread_bias = dot(own_bias[...], lanes_of(units, 0, width)[:units], 1, 0)
    at = lax.broadcasted_iota(jnp.int32, spread_bias.shape, 0)
    lane = lax.broadcasted_iota(jnp.int32, spread_bias.shape, 1)
    bias[...] = jnp.sum(
        jnp.where(lane // units == at, spread_bias, 0.0), axis=0, keepdims=True
    )
    weights.start_plane()
    weights.start_core()
    weights.finish()
    wt[...] = w_every[:, :, :rows].reshape(4 * width, width)
    packed = w_every[:, :, rows:].reshape(32 * 16, width)
    offsets = [sum(lengths[:n]) for n in range(4)]
    gains, biases, slot_rows, shift_rows = (
        spread(packed, length, offset) for length, offset in zip(lengths, offsets)
    )
    vec[...] = jnp.concatenate([gains, biases, jnp.zeros((2, width), F32)], axis=0)
    table[...] = slot_rows
    shift[...] = shift_rows

    def slots_way(i):
        return Gather(every.at[i], g_send.at[i], g_recv.at[i])

    def results_way(i):
        ring = lax.rem(i, 3)
        return Scatter(
            parts.at[ring], from_core.at[ring], chips.at[ring], from_plane.at[ring],
            column.at[i], from_z.at[i], s_send.at[i], s_recv.at[i],
        )

    def for_image(i, action):
        @pl.when((i >= 0) & (i < count))
        def _():
            action(i)

    def experts(i):
        slots_way(i).finish()
        both = every[i].astype(F32).reshape(32, 2, 8, width)
        got = expert_rows(
            both[:, 0].reshape(32 * 8, width).astype(BF16),
            both[:, 1].reshape(32 * 8, width).astype(BF16),
            w_in[...], bias[...], w_out[...],
        )
        back = jnp.stack([got[0].reshape(32, 8, width), got[1].reshape(32, 8, width)], axis=1)
        parts[lax.rem(i, 3)] = back.reshape(8, 4, 16, width).astype(BF16)
        in_grad[...] += got[2]
        out_grad[...] += got[3]
        bias_grad[...] += got[4]
        results_way(i).start_core()

    def middle_of(step):
        for_image(step - 3, experts)

    def end_of(step):
        for_image(step - 4, lambda i: results_way(i).start_z())
        for_image(step - 3, lambda i: results_way(i).start_plane())
        for_image(step - 2, lambda i: slots_way(i).start_core())
        for_image(step - 1, lambda i: slots_way(i).start_plane())

    def p_out(i, head):
        return pltpu.make_async_copy(p.at[head], p_hbm.at[i, head], p_out_sem.at[head])

    def p_in(i, head):
        return pltpu.make_async_copy(p_hbm.at[i, head], p.at[head], p_in_sem.at[head])

    def forward(i, carry):
        pltpu.make_async_copy(x_hbm.at[i], x.at[i], x_sem.at[i]).wait()
        pltpu.make_async_copy(g_hbm.at[i], g.at[i], g_sem.at[i]).wait()

        def before_heads():
            middle_of(i)

            @pl.when(i > 0)
            def _():
                for head in range(heads):
                    p_out(i - 1, head).wait()

        got = forward_image(
            x.at[i], g.at[i], valid[pl.ds(i, 1)], wt, vec[...], table[...].astype(BF16),
            q.at[i], k.at[i], v.at[i], p, att.at[i], inv.at[i],
            before_heads, lambda head: p_out(i, head).start(),
        )
        middle[i], dispatch[i], combine[i] = got[:3]
        shift_grad[...] += got[4].astype(BF16).astype(F32)
        every[i, wide, narrow] = jnp.concatenate([got[3], got[4]], axis=0).astype(BF16)
        end_of(i)
        slots_way(i).start_z()
        return carry

    lax.fori_loop(0, count, forward, 0)
    for head in range(heads):
        p_out(count - 1, head).wait()
        p_in(0, head).start()

    def backward(i, carry):
        def after_heads():
            @pl.when(i + 1 < count)
            def _():
                for head in range(heads):
                    p_in(i + 1, head).start()

        total = results_way(i).finish()
        got = backward_image(
            x.at[i], g.at[i], middle.at[i], dispatch[i], combine[i],
            (total[:8] + shift[...]).astype(BF16), total[8:].astype(BF16),
            wt, vec[...], table[...].astype(BF16),
            q.at[i], k.at[i], v.at[i], p, att.at[i], inv.at[i], ds, grad_t,
            q.at[i], k.at[i], v.at[i], g.at[i],
            lambda: middle_of(count + i), lambda head: p_in(i, head).wait(), after_heads,
        )
        pltpu.make_async_copy(g.at[i], mixed_hbm.at[i], mixed_sem.at[i]).start()
        x[i] = got[0]
        pltpu.make_async_copy(x.at[i], patch_grad_hbm.at[i], patch_sem.at[i]).start()
        add_grads(weight_grad, sums, table_grad, got)
        end_of(count + i)
        return carry

    lax.fori_loop(0, count, backward, 0)

    sent = last[0]
    sent[:, :, :rows] = weight_grad[...].reshape(8, 4, rows, width).astype(BF16)
    sources = (sums[:2], sums[2:6], table_grad[...], shift_grad[...])
    pieces = [gather_up(s, length, offset) for s, length, offset in zip(sources, lengths, offsets)]
    total = pieces[0] + pieces[1] + pieces[2] + pieces[3]
    first_row = lax.broadcasted_iota(jnp.int32, (32, 16, width), 1) == 0
    total = jnp.where(first_row, jnp.broadcast_to(total[:, None], (32, 16, width)), 0.0)
    sent[:, :, rows:] = total.reshape(8, 4, 16, width).astype(BF16)
    scatter = Scatter(*last)
    scatter.start_core()
    scatter.start_plane()
    scatter.start_z()
    total = scatter.finish()
    weight_out[...] = total[:rows]
    vectors_out[...] = total[rows : rows + 1]
    for i in range(count):
        pltpu.make_async_copy(g.at[i], mixed_hbm.at[i], mixed_sem.at[i]).wait()
        pltpu.make_async_copy(x.at[i], patch_grad_hbm.at[i], patch_sem.at[i]).wait()


def run_layer(patches, valid, attn_weights, vectors, expert_in, expert_in_bias, expert_out, out_grad):
    count, length, width = patches.shape
    heads = width // HEAD_DIM
    experts, _, units = expert_in.shape
    rows = attn_weights.shape[1]
    lengths = [v.shape[0] for v in vectors]
    packed = jnp.concatenate(list(vectors) + [jnp.zeros((width - sum(lengths),), BF16)])
    flat = (length, width)
    dma = pltpu.SemaphoreType.DMA
    vmem = pltpu.VMEM
    anywhere = pl.BlockSpec(memory_space=pl.ANY)
    here_all = pl.BlockSpec(memory_space=pltpu.VMEM)
    mixed, patch_grad, _, weight_grad, vector_grads, in_grad, out_grads, bias_grad = pl.pallas_call(
        functools.partial(layer_kernel, lengths),
        in_specs=[anywhere] * 2 + [here_all] * 6,
        out_specs=[anywhere] * 3 + [here_all] * 5,
        out_shape=[
            jax.ShapeDtypeStruct(patches.shape, BF16), jax.ShapeDtypeStruct(patches.shape, BF16),
            jax.ShapeDtypeStruct((count, heads, length, length), BF16),
            jax.ShapeDtypeStruct((rows, width), F32), jax.ShapeDtypeStruct((1, width), F32),
            jax.ShapeDtypeStruct((experts * units, width), F32),
            jax.ShapeDtypeStruct((experts * units, width), F32),
            jax.ShapeDtypeStruct((1, experts * units), F32),
        ],
        scratch_shapes=[
            vmem((count,) + flat, BF16), vmem((count,) + flat, BF16),
            vmem((count,) + flat, BF16), vmem((count,) + flat, BF16), vmem((count,) + flat, BF16),
            vmem((count,) + flat, BF16), vmem((count,) + flat, BF16), vmem((count,) + flat, F32),
            vmem((count, experts, length), F32), vmem((count, experts, length), F32),
            vmem((heads, length, length), BF16), vmem((2, length, length), BF16),
            vmem((2 * width, length), BF16), vmem((4 * width, width), BF16),
            vmem((8, width), F32), vmem((experts, width), F32), vmem((experts, width), F32),
            vmem((1, experts * units), F32),
            vmem((4 * width, width), F32), vmem((8, width), F32), vmem((experts, width), F32),
            vmem((experts, width), F32),
            dma((count,)), dma((count,)), dma((heads,)), dma((heads,)), dma((count,)), dma((count,)),
        ]
        + gather_scratch(rows + 16, width)
        + [vmem((count, 8, 4, 16, width), BF16), dma((count, 10)), dma((count, 10))]
        + [
            vmem((3, 8, 4, 16, width), BF16), vmem((3, 4, 4, 16, width), BF16),
            vmem((3, 4, 4, 16, width), BF16), vmem((3, 3, 4, 16, width), BF16),
            vmem((count, 4, 16, width), BF16), vmem((count, 3, 16, width), BF16),
            dma((count, 10)), dma((count, 10)),
        ]
        + scatter_scratch(rows + 16, width),
        compiler_params=pltpu.CompilerParams(
            collective_id=0, has_side_effects=True, vmem_limit_bytes=LAYER_LIMIT
        ),
        name="layer",
    )(
        patches, out_grad, valid, attn_weights.T, packed.reshape(1, width),
        expert_in.transpose(0, 2, 1).reshape(experts * units, width), expert_in_bias,
        expert_out.reshape(experts * units, width),
    )
    grads = []
    at = 0
    for piece in lengths:
        grads.append(vector_grads[0, at : at + piece])
        at += piece
    return (
        mixed,
        patch_grad,
        weight_grad.T,
        grads[0],
        grads[1],
        grads[2],
        in_grad.reshape(experts, units, width).transpose(0, 2, 1),
        bias_grad.reshape(experts, units),
        out_grads.reshape(experts, units, width),
        grads[3],
    )


def scatter_sum(parts):
    got = lax.all_to_all(parts.astype(BF16), AXES, 0, 0, tiled=True)
    return jnp.sum(got.astype(F32), axis=0)


def experts_at_home(slots, produced_grad, expert_in, expert_in_bias, expert_out, devices):
    local_images, experts, width = slots.shape
    every = lax.all_gather(jnp.stack([slots, produced_grad]), AXES, axis=1, tiled=True)
    all_slots, all_grads = every[0], every[1]
    hidden = jnp.einsum(
        "bed,edf->bef", all_slots, expert_in, preferred_element_type=F32
    ) + expert_in_bias.astype(F32)
    active, gelu_back = jax.vjp(smooth, hidden)
    active = active.astype(BF16)
    partial = jnp.einsum("bef,efd->bed", active, expert_out, preferred_element_type=F32)
    active_grad = jnp.einsum("bed,efd->bef", all_grads, expert_out, preferred_element_type=F32)
    hidden_grad = gelu_back(active_grad)[0].astype(BF16)
    partial_back = jnp.einsum("bef,edf->bed", hidden_grad, expert_in, preferred_element_type=F32)
    contract_grad = jnp.einsum("bef,bed->efd", active, all_grads, preferred_element_type=F32)
    expand_grad = jnp.einsum("bed,bef->edf", all_slots, hidden_grad, preferred_element_type=F32)
    inner_grad = jnp.sum(hidden_grad.astype(F32), axis=0)
    both = jnp.stack([partial, partial_back]).reshape(2, devices, local_images, experts, width)
    both = scatter_sum(jnp.moveaxis(both, 1, 0))
    return (both[0], both[1], expand_grad, inner_grad, contract_grad)


def on_device(
    patches,
    valid,
    attn_weights,
    norm_gains,
    vec_biases,
    slot_params,
    expert_in,
    expert_in_bias,
    expert_out,
    expert_out_bias,
    out_grad,
):
    local_images, patch_count, width = patches.shape
    experts = expert_in.shape[0]
    devices = lax.axis_size("wide") * lax.axis_size("narrow")

    vectors = (norm_gains, vec_biases, slot_params, expert_out_bias)
    lengths = [v.shape[0] for v in vectors]
    if lax.axis_size("wide") == 8 and lax.axis_size("narrow") == 4:
        return run_layer(
            patches, valid, attn_weights, vectors, expert_in, expert_in_bias, expert_out, out_grad
        )
    wt = lax.all_gather(attn_weights.T, AXES, axis=0, tiled=True)
    small = lax.all_gather(jnp.concatenate(vectors), AXES)
    pieces = []
    at = 0
    for length in lengths:
        pieces.append(small[:, at : at + length].reshape(-1, width))
        at += length
    gains, biases, table, expert_shift = pieces
    vec = jnp.concatenate([gains, biases, jnp.zeros((2, width), BF16)]).astype(F32)

    *kept, slots, produced_grad = run_forward(
        patches, out_grad, valid.reshape(local_images, 1, patch_count), wt, vec, table
    )
    produced, slot_grad, expand_grad, inner_grad, contract_grad = experts_at_home(
        slots, produced_grad, expert_in, expert_in_bias, expert_out, devices
    )
    produced = (produced + expert_shift.astype(F32)).astype(BF16)
    slot_grad = slot_grad.astype(BF16)
    shift_grad = jnp.sum(produced_grad.astype(F32), axis=0)
    mixed_out, patch_grad, weight_grad, rows, table_grad = run_backward(
        patches, out_grad, kept, produced, slot_grad, wt, vec, table
    )
    weight_grad = weight_grad.reshape(devices, -1, width)
    small_grads = jnp.concatenate(
        [v.reshape(devices, -1) for v in (rows[:2], rows[2:6], table_grad, shift_grad)], axis=1
    )
    weight_grad = scatter_sum(weight_grad).T
    small_grads = jnp.sum(lax.all_to_all(small_grads, AXES, 0, 0, tiled=True), axis=0)
    grads = []
    at = 0
    for length in lengths:
        grads.append(small_grads[at : at + length])
        at += length
    return (
        mixed_out,
        patch_grad,
        weight_grad,
        grads[0],
        grads[1],
        grads[2],
        expand_grad,
        inner_grad,
        contract_grad,
        grads[3],
    )


def solution(mesh):
    images = P(AXES, None, None)
    vector = P(AXES)
    second = P(None, AXES)
    return jax.shard_map(
        on_device,
        mesh=mesh,
        in_specs=(
            images, P(AXES, None), second, vector, vector, vector,
            P(None, None, AXES), second, P(None, AXES, None), vector, images,
        ),
        out_specs=(
            images, images, second, vector, vector, vector,
            P(None, None, AXES), second, P(None, AXES, None), vector,
        ),
        check_vma=False,
    )
```

```python
import functools

import jax
import jax.numpy as jnp
from jax import lax
from jax.experimental import pallas as pl
from jax.experimental.pallas import tpu as pltpu
from jax.sharding import PartitionSpec as P

HEAD_DIM = 64
PAIR = 2 * HEAD_DIM
MASKED = -1000000000.0
AXES = ("wide", "narrow")
BF16 = jnp.bfloat16
F32 = jnp.float32
MESH = pl.DeviceIdType.MESH
VMEM_LIMIT = 60 * 1024 * 1024
LAYER_LIMIT = 63 * 1024 * 1024
GAIN1, GAIN2, BIAS1, VBIAS, OBIAS, BIAS2 = range(6)


def dot(left, right, left_dim, right_dim):
    return lax.dot_general(
        left, right, (((left_dim,), (right_dim,)), ((), ())), preferred_element_type=F32
    )


def normalize(values):
    centred = values - jnp.mean(values, axis=-1, keepdims=True)
    factor = lax.rsqrt(jnp.mean(centred * centred, axis=-1, keepdims=True) + 1e-06)
    return (centred * factor, factor)


def norm_back(grad_hat, normed, factor):
    return factor * (
        grad_hat
        - jnp.mean(grad_hat, axis=-1, keepdims=True)
        - normed * jnp.mean(grad_hat * normed, axis=-1, keepdims=True)
    )


def smooth(values):
    return jax.nn.gelu(values, approximate=False)


def lower_half(shape):
    return lax.broadcasted_iota(jnp.int32, shape, 1) < HEAD_DIM


def own_half(low, head, own, other):
    return jnp.where(low, own, other) if head % 2 == 0 else jnp.where(low, other, own)


def forward_image(
    x, g, valid_row, wt, vec, table, q_ref, k_ref, v_ref, p_ref, att_ref, inv_ref,
    before_heads=None, after_head=None,
):
    patches, width = x.shape
    heads = width // HEAD_DIM
    images = x[...].astype(F32)
    normed, _ = normalize(images)
    first = (normed * vec[GAIN1 : GAIN1 + 1] + vec[BIAS1 : BIAS1 + 1]).astype(BF16)
    q_ref[...] = (dot(first, wt[:width], 1, 1) * HEAD_DIM ** (-0.5)).astype(BF16)
    k_ref[...] = dot(first, wt[width : 2 * width], 1, 1).astype(BF16)
    v_ref[...] = (dot(first, wt[2 * width : 3 * width], 1, 1) + vec[VBIAS : VBIAS + 1]).astype(BF16)
    if before_heads is not None:
        before_heads()
    bias_row = jnp.where(valid_row > 0, 0.0, MASKED).astype(F32)
    fill = jnp.broadcast_to(bias_row * (1.0 / HEAD_DIM), (PAIR, patches)).T.astype(BF16)
    low = lower_half((patches, PAIR))
    one = jnp.ones((patches, PAIR), BF16)
    scores = {}

    def pair_of(ref, head):
        at = head // 2 * PAIR
        return ref[:, at : at + PAIR]

    def score(head):
        scores[head] = dot(
            own_half(low, head, pair_of(q_ref, head), one),
            own_half(low, head, pair_of(k_ref, head), fill),
            1,
            1,
        )

    sums = {}
    score(0)
    for head in range(heads):
        if head + 1 < heads:
            score(head + 1)
        raw = scores.pop(head)
        prob = jnp.exp(raw - jnp.max(raw, axis=1, keepdims=True)).astype(BF16)
        p_ref[head] = prob
        sums[head] = dot(prob, own_half(low, head, pair_of(v_ref, head), one), 1, 0)
        if after_head is not None:
            after_head(head)
        if head % 2 == 1:
            even, odd = sums.pop(head - 1), sums.pop(head)
            inverse = 1.0 / pltpu.roll(jnp.where(low, odd, even), HEAD_DIM, 1)
            at = head // 2 * PAIR
            inv_ref[:, at : at + PAIR] = inverse.astype(inv_ref.dtype)
            att_ref[:, at : at + PAIR] = (jnp.where(low, even, odd) * inverse).astype(BF16)
    branch = dot(att_ref[...], wt[3 * width :], 1, 1)
    middle = images + branch + vec[OBIAS : OBIAS + 1]
    normed, _ = normalize(middle)
    second = (normed * vec[GAIN2 : GAIN2 + 1] + vec[BIAS2 : BIAS2 + 1]).astype(BF16)
    logits = dot(table, second, 1, 1)
    masked = jnp.where(valid_row > 0, logits, MASKED)
    dispatch = jnp.exp(masked - jnp.max(masked, axis=1, keepdims=True))
    dispatch = dispatch / jnp.sum(dispatch, axis=1, keepdims=True)
    combine = jnp.exp(logits - jnp.max(logits, axis=0, keepdims=True))
    combine = combine / jnp.sum(combine, axis=0, keepdims=True)
    slots = dot(dispatch.astype(BF16), second, 1, 0)
    produced_grad = dot(combine.astype(BF16), g[...], 1, 0)
    return middle, dispatch, combine, slots, produced_grad


def backward_image(
    x, g, middle_ref, dispatch, combine, produced, slot_grad, wt, vec, table,
    q_ref, k_ref, v_ref, p_ref, att_ref, inv_ref, ds_ref, grad_t_ref, dq_ref, dk_ref, dv_ref,
    mixed_ref, grad_ref,
    before_heads=None, before_head=None, after_heads=None,
):
    patches, width = x.shape
    heads = width // HEAD_DIM
    combine_low = combine.astype(BF16)
    dispatch_low = dispatch.astype(BF16)
    middle = middle_ref[...]
    normed, factor = normalize(middle)
    second = (normed * vec[GAIN2 : GAIN2 + 1] + vec[BIAS2 : BIAS2 + 1]).astype(BF16)
    upstream = g[...]
    mixed = (middle + dot(combine_low, produced, 0, 0)).astype(BF16)
    combine_grad = dot(produced, upstream, 1, 1)
    dispatch_grad = dot(slot_grad, second, 1, 1)
    logit_grad = dispatch * (
        dispatch_grad - jnp.sum(dispatch * dispatch_grad, axis=1, keepdims=True)
    ) + combine * (combine_grad - jnp.sum(combine * combine_grad, axis=0, keepdims=True))
    logit_grad = logit_grad.astype(BF16)
    table_grad = dot(logit_grad, second, 1, 0)
    second_grad = dot(
        jnp.concatenate([dispatch_low, logit_grad], axis=0),
        jnp.concatenate([slot_grad, table], axis=0),
        0,
        0,
    )
    gain_two = jnp.sum(second_grad * normed, axis=0, keepdims=True)
    shift_two = jnp.sum(second_grad, axis=0, keepdims=True)
    middle_grad = upstream.astype(F32) + norm_back(
        second_grad * vec[GAIN2 : GAIN2 + 1], normed, factor
    )
    mixed_ref[...] = mixed
    grad_ref[...] = middle_grad
    branch_grad = middle_grad.astype(BF16)
    branch_shift = jnp.sum(branch_grad.astype(F32), axis=0, keepdims=True)
    output_grad = dot(branch_grad.T, att_ref[...], 1, 0)
    attended_grad = dot(branch_grad, wt[3 * width :], 1, 0).astype(BF16).astype(F32)
    scaled = attended_grad * inv_ref[...].astype(F32)
    drop = (-(scaled * att_ref[...].astype(F32))).astype(BF16)
    scaled = scaled.astype(BF16)
    scaled_t = scaled.T
    query_t = q_ref[...].T
    if before_heads is not None:
        before_heads()
    low = lower_half((patches, PAIR))
    one = jnp.ones((patches, PAIR), BF16)
    prob_grads = {}

    def pair_of(ref, head):
        at = head // 2 * PAIR
        return ref[:, at : at + PAIR]

    def prob_grad(head):
        rolled = pltpu.roll(pair_of(drop, head).astype(F32), HEAD_DIM, 1).astype(BF16)
        prob_grads[head] = dot(
            own_half(low, head, pair_of(scaled, head), rolled),
            own_half(low, head, pair_of(v_ref, head), one),
            1,
            1,
        )

    query_grads = {}
    prob_grad(0)
    for head in range(heads):
        if head + 1 < heads:
            prob_grad(head + 1)
        if before_head is not None:
            before_head(head)
        rows = slice(head * HEAD_DIM, (head + 1) * HEAD_DIM)
        prob = p_ref[head]
        grad_t_ref[width + rows.start : width + rows.stop, :] = dot(
            scaled_t[rows], prob, 1, 0
        ).astype(BF16)
        score_grad = (prob.astype(F32) * prob_grads.pop(head)).astype(BF16)
        ds_ref[head % 2] = score_grad
        score_grad = ds_ref[head % 2]
        query_grads[head] = dot(score_grad, pair_of(k_ref, head), 1, 0)
        grad_t_ref[rows, :] = dot(query_t[rows], score_grad, 1, 0).astype(BF16)
        if head % 2 == 1:
            both = jnp.where(low, query_grads.pop(head - 1), query_grads.pop(head))
            at = head // 2 * PAIR
            dq_ref[:, at : at + PAIR] = (both * HEAD_DIM ** (-0.5)).astype(BF16)
    if after_heads is not None:
        after_heads()
    dk_ref[...] = grad_t_ref[:width, :].T
    dv_ref[...] = grad_t_ref[width:, :].T
    normed, _ = normalize(x[...].astype(F32))
    first = (normed * vec[GAIN1 : GAIN1 + 1] + vec[BIAS1 : BIAS1 + 1]).astype(BF16)
    query_front = dot(dq_ref[...].T, first, 1, 0)
    other_front = dot(grad_t_ref[...], first, 1, 0)
    columns = [
        jnp.sum(ref[...].astype(F32), axis=0, keepdims=True) for ref in (dq_ref, dk_ref, dv_ref)
    ]
    sums = jnp.concatenate(
        columns + [gain_two, branch_shift, shift_two, jnp.zeros((2, width), F32)], axis=0
    )
    return query_front, other_front, output_grad, sums, table_grad


def finish_image(x, middle_grad, wt, vec, dq_ref, dk_ref, dv_ref):
    width = x.shape[1]
    normed, factor = normalize(x[...].astype(F32))
    project_grad = jnp.concatenate([dq_ref[...], dk_ref[...], dv_ref[...]], axis=1)
    first_grad = dot(project_grad, wt[: 3 * width], 1, 0)
    grad = middle_grad[...] + norm_back(first_grad * vec[GAIN1 : GAIN1 + 1], normed, factor)
    return grad.astype(BF16)


def norm_sums(sums, weight_grad, wt, vec):
    width = wt.shape[1]
    high = sums.astype(BF16)
    both = jnp.concatenate([high, (sums - high.astype(F32)).astype(BF16)], axis=0)
    shift_one = jnp.zeros((1, width), F32)
    for part in range(3):
        got = dot(both, wt[part * width : (part + 1) * width], 1, 0)
        shift_one += got[part : part + 1] + got[8 + part : 9 + part]
    product = jnp.sum(weight_grad * wt[: 3 * width].astype(F32), axis=0, keepdims=True)
    gain_one = (product - vec[BIAS1 : BIAS1 + 1] * shift_one) / vec[GAIN1 : GAIN1 + 1]
    gains = jnp.concatenate([gain_one, sums[3:4]], axis=0)
    return gains, jnp.concatenate([shift_one, sums[2:3], sums[4:5], sums[5:6]], axis=0)


def forward_kernel(
    x, g, valid, wt, vec, table,
    q, k, v, p, att, inv, middle, dispatch, combine, slots, produced_grad,
):
    got = forward_image(
        x.at[0], g.at[0], valid[0], wt, vec[...], table[...],
        q.at[0], k.at[0], v.at[0], p.at[0], att.at[0], inv.at[0],
    )
    for ref, value in zip((middle, dispatch, combine, slots, produced_grad), got):
        ref[0] = value.astype(ref.dtype)


def add_grads(weight_grad, sums, table_grad, got):
    width = weight_grad.shape[1]
    for ref, at, value in (
        (weight_grad, 0, got[0]), (weight_grad, width, got[1]), (weight_grad, 3 * width, got[2]),
        (sums, 0, got[3]), (table_grad, 0, got[4]),
    ):
        ref[at : at + value.shape[0], :] += value


def backward_kernel(
    x, g, middle, dispatch, combine, produced, slot_grad, wt, vec, table,
    q, k, v, p, att, inv,
    mixed, patch_grad, weight_grad, sums, table_grad,
    ds, grad_t, dq, dk, dv, middle_grad,
):
    @pl.when(pl.program_id(0) == 0)
    def _():
        weight_grad[...] = jnp.zeros_like(weight_grad)
        sums[...] = jnp.zeros_like(sums)
        table_grad[...] = jnp.zeros_like(table_grad)

    got = backward_image(
        x.at[0], g.at[0], middle.at[0], dispatch[0], combine[0], produced[0], slot_grad[0],
        wt, vec[...], table[...],
        q.at[0], k.at[0], v.at[0], p.at[0], att.at[0], inv.at[0], ds, grad_t, dq, dk, dv,
        mixed.at[0], middle_grad,
    )
    patch_grad[0] = finish_image(x.at[0], middle_grad, wt, vec[...], dq, dk, dv)
    add_grads(weight_grad, sums, table_grad, got)


def per_image(*shape):
    return pl.BlockSpec((1,) + shape, lambda i: (i,) + (0,) * len(shape))


def whole(*shape):
    return pl.BlockSpec(shape, lambda i: (0,) * len(shape))


def run_forward(x, g, valid, wt, vec, table):
    count, patches, width = x.shape
    heads = width // HEAD_DIM
    experts = table.shape[0]
    flat = (patches, width)
    outs = [
        (flat, BF16), (flat, BF16), (flat, BF16), ((heads, patches, patches), BF16),
        (flat, BF16), (flat, F32), (flat, F32),
        ((experts, patches), F32), ((experts, patches), F32),
        ((experts, width), BF16), ((experts, width), BF16),
    ]
    return pl.pallas_call(
        forward_kernel,
        grid=(count,),
        in_specs=[
            per_image(*flat), per_image(*flat), per_image(1, patches),
            whole(*wt.shape), whole(*vec.shape), whole(*table.shape),
        ],
        out_specs=[per_image(*shape) for shape, _ in outs],
        out_shape=[jax.ShapeDtypeStruct((count,) + shape, kind) for shape, kind in outs],
        compiler_params=pltpu.CompilerParams(vmem_limit_bytes=VMEM_LIMIT),
        name="forward",
    )(x, g, valid, wt, vec, table)


def run_backward(x, g, kept, produced, slot_grad, wt, vec, table):
    count, patches, width = x.shape
    heads = width // HEAD_DIM
    experts = table.shape[0]
    flat = (patches, width)
    q, k, v, p, att, inv, middle, dispatch, combine = kept
    return pl.pallas_call(
        backward_kernel,
        grid=(count,),
        in_specs=[
            per_image(*flat), per_image(*flat), per_image(*flat),
            per_image(experts, patches), per_image(experts, patches),
            per_image(experts, width), per_image(experts, width),
            whole(*wt.shape), whole(*vec.shape), whole(*table.shape),
            per_image(*flat), per_image(*flat), per_image(*flat),
            per_image(heads, patches, patches), per_image(*flat), per_image(*flat),
        ],
        out_specs=[
            per_image(*flat), per_image(*flat),
            whole(4 * width, width), whole(8, width), whole(experts, width),
        ],
        out_shape=[
            jax.ShapeDtypeStruct(x.shape, BF16), jax.ShapeDtypeStruct(x.shape, BF16),
            jax.ShapeDtypeStruct((4 * width, width), F32), jax.ShapeDtypeStruct((8, width), F32),
            jax.ShapeDtypeStruct((experts, width), F32),
        ],
        scratch_shapes=[
            pltpu.VMEM((2, patches, patches), BF16),
            pltpu.VMEM((2 * width, patches), BF16),
            pltpu.VMEM(flat, BF16),
            pltpu.VMEM(flat, BF16),
            pltpu.VMEM(flat, BF16),
            pltpu.VMEM(flat, F32),
        ],
        compiler_params=pltpu.CompilerParams(vmem_limit_bytes=VMEM_LIMIT),
        name="backward",
    )(x, g, middle, dispatch, combine, produced, slot_grad, wt, vec, table, q, k, v, p, att, inv)


def here():
    return lax.axis_index("wide"), lax.axis_index("narrow")


def along_z(w, z):
    return [(w, lax.rem(z + step, 4)) for step in (1, 2, 3)]


def in_plane(w, z):
    x_flip = 2 - 4 * lax.rem(w // 2, 2)
    y_flip = 4 - 8 * (w // 4)
    return [(w + x_flip, z), (w + y_flip, z), (w + x_flip + y_flip, z)]


def other_core(w, z):
    return (w + 1 - 2 * lax.rem(w, 2), z)


def greet():
    w, z = here()
    barrier = pltpu.get_barrier_semaphore()
    peers = along_z(w, z) + in_plane(w, z) + [other_core(w, z)]
    for peer in peers:
        pl.semaphore_signal(barrier, inc=1, device_id=peer, device_id_type=MESH)
    pl.semaphore_wait(barrier, len(peers))


def remote(src, dst, send, recv, peer):
    return pltpu.make_async_remote_copy(
        src_ref=src, dst_ref=dst, send_sem=send, recv_sem=recv, device_id=peer, device_id_type=MESH
    )


class Gather:
    def __init__(self, every, send, recv):
        self.every, self.send, self.recv = every, send, recv
        self.w, self.z = here()

    def z_copies(self):
        own = self.every.at[self.w, self.z]
        return [
            remote(own, own, self.send.at[n], self.recv.at[n], peer)
            for n, peer in enumerate(along_z(self.w, self.z))
        ]

    def plane_copies(self):
        own = self.every.at[self.w]
        return [
            remote(own, own, self.send.at[3 + n], self.recv.at[3 + n], peer)
            for n, peer in enumerate(in_plane(self.w, self.z))
        ]

    def core_copy(self, n, group):
        own = self.every.at[group]
        return remote(
            own, own, self.send.at[6 + n], self.recv.at[6 + n], other_core(self.w, self.z)
        )

    def start_z(self):
        for copy in self.z_copies():
            copy.start()

    def start_plane(self):
        for copy in self.z_copies():
            copy.wait()
        for copy in self.plane_copies():
            copy.start()
        self.core_copy(0, self.w).start()

    def start_core(self):
        peers = in_plane(self.w, self.z)
        for n, (copy, peer) in enumerate(zip(self.plane_copies(), peers)):
            copy.wait()
            self.core_copy(n + 1, peer[0]).start()

    def finish(self):
        for n in range(4):
            self.core_copy(n, self.w).wait()


class Scatter:
    def __init__(self, parts, from_core, chips, from_plane, column, from_z, send, recv):
        self.parts, self.from_core, self.chips = parts, from_core, chips
        self.from_plane, self.column, self.from_z = from_plane, column, from_z
        self.send, self.recv = send, recv
        self.w, self.z = here()
        self.core = lax.rem(self.w, 2)

    def core_copy(self, chip):
        return remote(
            self.parts.at[2 * chip + 1 - self.core], self.from_core.at[chip],
            self.send.at[chip], self.recv.at[chip], other_core(self.w, self.z),
        )

    def chip_order(self):
        return [there // 2 for there, _ in in_plane(self.w, self.z)] + [self.w // 2]

    def plane_copies(self):
        return [
            remote(
                self.chips.at[peer[0] // 2], self.from_plane.at[n],
                self.send.at[4 + n], self.recv.at[4 + n], peer,
            )
            for n, peer in enumerate(in_plane(self.w, self.z))
        ]

    def z_copies(self):
        return [
            remote(
                self.column.at[peer[1]], self.from_z.at[n],
                self.send.at[7 + n], self.recv.at[7 + n], peer,
            )
            for n, peer in enumerate(along_z(self.w, self.z))
        ]

    def start_core(self):
        for chip in self.chip_order():
            self.core_copy(chip).start()

    def start_plane(self):
        onward = self.plane_copies() + [None]
        for chip, copy in zip(self.chip_order(), onward):
            self.core_copy(chip).wait()
            own = self.parts[2 * chip + self.core].astype(F32)
            self.chips[chip] = (own + self.from_core[chip].astype(F32)).astype(BF16)
            if copy is not None:
                copy.start()

    def start_z(self):
        for copy in self.plane_copies():
            copy.wait()
        total = self.chips[self.w // 2].astype(F32)
        for n in range(3):
            total = total + self.from_plane[n].astype(F32)
        self.column[...] = total.astype(BF16)
        for copy in self.z_copies():
            copy.start()

    def finish(self):
        for copy in self.z_copies():
            copy.wait()
        total = self.column[self.z].astype(F32)
        for n in range(3):
            total = total + self.from_z[n].astype(F32)
        return total


class FineGather:
    def __init__(self, every, z_send, z_recv, p_send, p_recv, c_send, c_recv):
        self.every = every
        self.z_sems, self.p_sems, self.c_sems = (z_send, z_recv), (p_send, p_recv), (c_send, c_recv)
        self.w, self.z = here()
        self.plane = in_plane(self.w, self.z)

    def block(self, w, k):
        return self.every.at[w, lax.rem(self.z + 4 - k, 4)]

    def z_copy(self, n):
        own = self.block(self.w, 0)
        peer = along_z(self.w, self.z)[n]
        return remote(own, own, self.z_sems[0].at[n], self.z_sems[1].at[n], peer)

    def plane_copy(self, n, k):
        own = self.block(self.w, k)
        return remote(own, own, self.p_sems[0].at[n, k], self.p_sems[1].at[n, k], self.plane[n])

    def core_copy(self, group, k):
        own = self.block(self.w if group == 0 else self.plane[group - 1][0], k)
        return remote(
            own, own, self.c_sems[0].at[group, k], self.c_sems[1].at[group, k],
            other_core(self.w, self.z),
        )

    def pass_on(self, k):
        for n in range(3):
            self.plane_copy(n, k).start()
        self.core_copy(0, k).start()

    def start(self):
        for n in range(3):
            self.z_copy(n).start()
        self.pass_on(0)

    def start_plane(self):
        for n in range(3):
            self.z_copy(n).wait()
            self.pass_on(n + 1)

    def start_core(self):
        for k in range(4):
            for n in range(3):
                self.plane_copy(n, k).wait()
                self.core_copy(n + 1, k).start()

    def finish(self):
        for group in range(4):
            for k in range(4):
                self.core_copy(group, k).wait()


def fine_scratch(rows, width):
    dma = pltpu.SemaphoreType.DMA
    return [
        pltpu.VMEM((8, 4, rows, width), BF16),
        dma((3,)), dma((3,)), dma((3, 4)), dma((3, 4)), dma((4, 4)), dma((4, 4)),
    ]


def gather_scratch(rows, width):
    return [
        pltpu.VMEM((8, 4, rows, width), BF16),
        pltpu.SemaphoreType.DMA((10,)),
        pltpu.SemaphoreType.DMA((10,)),
    ]


def scatter_scratch(rows, width):
    return [
        pltpu.VMEM((8, 4, rows, width), BF16),
        pltpu.VMEM((4, 4, rows, width), BF16),
        pltpu.VMEM((4, 4, rows, width), BF16),
        pltpu.VMEM((3, 4, rows, width), BF16),
        pltpu.VMEM((4, rows, width), BF16),
        pltpu.VMEM((3, rows, width), BF16),
        pltpu.SemaphoreType.DMA((10,)),
        pltpu.SemaphoreType.DMA((10,)),
    ]

def expert_rows(slots, grads, w_in, bias, w_out):
    rows, width = slots.shape
    units = w_in.shape[0]
    shape = (rows, units)
    own = lax.rem(lax.broadcasted_iota(jnp.int32, shape, 0), 8)
    start = own * (units // 8)
    lane = lax.broadcasted_iota(jnp.int32, shape, 1)
    keep = (lane >= start) & (lane < start + units // 8)
    hidden = dot(slots, w_in, 1, 1) + bias
    active_grad = dot(grads, w_out, 1, 1)
    half = 0.5 * (1.0 + lax.erf(hidden * 0.7071067811865476))
    active = jnp.where(keep, hidden * half, 0.0).astype(BF16)
    slope = half + hidden * jnp.exp(hidden * hidden * -0.5) * 0.3989422804014327
    hidden_grad = jnp.where(keep, active_grad * slope, 0.0).astype(BF16)
    produced = dot(active, w_out, 1, 0)
    slot_grad = dot(hidden_grad, w_in, 1, 0)
    in_grad = dot(hidden_grad, slots, 0, 0)
    out_grad = dot(active, grads, 0, 0)
    bias_grad = jnp.sum(hidden_grad.astype(F32).reshape(-1, 8, units), axis=0)
    return produced, slot_grad, in_grad, out_grad, bias_grad


def one_hot(length, width):
    row = lax.broadcasted_iota(jnp.int32, (128, width), 0)
    column = lax.broadcasted_iota(jnp.int32, (128, width), 1)
    return (row == lax.rem(column, length)).astype(BF16)


def own_piece(shape, length):
    device = lax.broadcasted_iota(jnp.int32, shape, 0)
    column = lax.broadcasted_iota(jnp.int32, shape, 1)
    return lax.rem(device, shape[1] // length) == column // length


def spread(pieces, length, width):
    devices = pieces.shape[0]
    tall = dot(pieces.astype(BF16), one_hot(length, width), 1, 0)
    tall = jnp.where(own_piece(tall.shape, length), tall, 0.0).astype(BF16)
    row = lax.broadcasted_iota(jnp.int32, (8, devices), 0)
    device = lax.broadcasted_iota(jnp.int32, (8, devices), 1)
    return dot((device // (width // length) == row).astype(BF16), tall, 1, 0)


def pieces_of(rows, length, devices):
    count, width = rows.shape
    per_row = width // length
    tall = jnp.broadcast_to(rows[:, None], (count, per_row, width)).reshape(devices, width)
    tall = jnp.where(own_piece(tall.shape, length), tall, 0.0)
    return dot(tall.astype(BF16), one_hot(length, width), 1, 1)


def layer_kernel(
    lengths,
    x_hbm, g_hbm, valid, own_weights, own_gains, own_biases, own_table, own_shift, w_in, own_bias, w_out,
    mixed_hbm, patch_grad_hbm, p_hbm, weight_out, vectors_out, in_grad, out_grad, bias_grad,
    x, g, q, k, v, att, inv, middle, dispatch, combine, p, ds, grad_t, wt, vec, table, shift, bias,
    weight_grad, sums, table_grad, shift_grad, own_pieces,
    x_sem, g_sem, p_out_sem, p_in_sem, mixed_sem, patch_sem,
    every, g_send, g_recv,
    parts, from_core, chips, from_plane, column, from_z, s_send, s_recv,
    *rest,
):
    count, patches, width = x.shape
    heads = width // HEAD_DIM
    rows = own_weights.shape[0]
    wide, narrow = here()
    (w_every, *w_sems), (v_every, *v_sems) = rest[:7], rest[7:10]
    w_last, v_last = rest[10:18], rest[18:26]

    for i in range(count):
        pltpu.make_async_copy(x_hbm.at[i], x.at[i], x_sem.at[i]).start()
        pltpu.make_async_copy(g_hbm.at[i], g.at[i], g_sem.at[i]).start()
    w_every[wide, narrow] = own_weights[...]
    own_pieces[...] = jnp.zeros_like(own_pieces)
    for n, ref in enumerate((own_gains, own_biases, own_table, own_shift)):
        own_pieces[n : n + 1, : lengths[n]] = ref[...].astype(F32).reshape(1, lengths[n])
    v_every[wide, narrow] = own_pieces[...].astype(BF16)
    greet()
    weights = FineGather(w_every, *w_sems)
    vectors = Gather(v_every, *v_sems)
    vectors.start_z()
    weights.start()
    for ref in (weight_grad, sums, table_grad, shift_grad, in_grad, out_grad, bias_grad):
        ref[...] = jnp.zeros_like(ref)
    units = w_in.shape[0] // 8
    spread_bias = dot(own_bias[...], one_hot(units, 8 * units)[:units], 1, 0)
    at = lax.broadcasted_iota(jnp.int32, spread_bias.shape, 0)
    lane = lax.broadcasted_iota(jnp.int32, spread_bias.shape, 1)
    bias[...] = jnp.sum(jnp.where(lane // units == at, spread_bias, 0.0), axis=0, keepdims=True)
    vectors.start_plane()
    weights.start_plane()
    vectors.start_core()
    weights.start_core()
    vectors.finish()
    packed = v_every[...].astype(F32).reshape(32, 16, 128)
    gains, biases, slot_rows, shift_rows = (
        spread(packed[:, n], length, width) for n, length in enumerate(lengths)
    )
    vec[...] = jnp.concatenate([gains[:2], biases[:4], jnp.zeros((2, width), F32)], axis=0)
    table[...] = slot_rows
    shift[...] = shift_rows
    weights.finish()
    wt[...] = w_every[...].reshape(4 * width, width)

    def slots_way(i):
        return Gather(every.at[i], g_send.at[i], g_recv.at[i])

    def results_way(i):
        ring = lax.rem(i, 3)
        return Scatter(
            parts.at[ring], from_core.at[ring], chips.at[ring], from_plane.at[ring],
            column.at[i], from_z.at[i], s_send.at[i], s_recv.at[i],
        )

    def for_image(i, action):
        @pl.when((i >= 0) & (i < count))
        def _():
            action(i)

    def experts(i):
        slots_way(i).finish()
        both = every[i].astype(F32).reshape(32, 2, 8, width)
        got = expert_rows(
            both[:, 0].reshape(32 * 8, width).astype(BF16),
            both[:, 1].reshape(32 * 8, width).astype(BF16),
            w_in[...], bias[...], w_out[...],
        )
        back = jnp.stack([got[0].reshape(32, 8, width), got[1].reshape(32, 8, width)], axis=1)
        parts[lax.rem(i, 3)] = back.reshape(8, 4, 16, width).astype(BF16)
        in_grad[...] += got[2]
        out_grad[...] += got[3]
        bias_grad[...] += got[4]
        results_way(i).start_core()

    def middle_of(step):
        for_image(step - 3, experts)

    def end_of(step):
        for_image(step - 4, lambda i: results_way(i).start_z())
        for_image(step - 3, lambda i: results_way(i).start_plane())
        for_image(step - 2, lambda i: slots_way(i).start_core())
        for_image(step - 1, lambda i: slots_way(i).start_plane())

    def p_out(i, head):
        return pltpu.make_async_copy(p.at[head], p_hbm.at[i, head], p_out_sem.at[head])

    def p_in(i, head):
        return pltpu.make_async_copy(p_hbm.at[i, head], p.at[head], p_in_sem.at[head])

    def forward(i, carry):
        pltpu.make_async_copy(x_hbm.at[i], x.at[i], x_sem.at[i]).wait()
        pltpu.make_async_copy(g_hbm.at[i], g.at[i], g_sem.at[i]).wait()

        def before_heads():
            middle_of(i)

            @pl.when(i > 0)
            def _():
                for head in range(heads):
                    p_out(i - 1, head).wait()

        got = forward_image(
            x.at[i], g.at[i], valid[pl.ds(i, 1)], wt, vec[...], table[...].astype(BF16),
            q.at[i], k.at[i], v.at[i], p, att.at[i], inv.at[i],
            before_heads, lambda head: p_out(i, head).start(),
        )
        middle[i], dispatch[i], combine[i] = got[:3]
        shift_grad[...] += got[4].astype(BF16).astype(F32)
        every[i, wide, narrow] = jnp.concatenate([got[3], got[4]], axis=0).astype(BF16)
        end_of(i)
        slots_way(i).start_z()
        return carry

    lax.fori_loop(0, count, forward, 0)
    for head in range(heads):
        p_out(count - 1, head).wait()
        p_in(0, head).start()

    def backward(i, carry):
        def after_heads():
            @pl.when(i + 1 < count)
            def _():
                for head in range(heads):
                    p_in(i + 1, head).start()

        total = results_way(i).finish()
        got = backward_image(
            x.at[i], g.at[i], middle.at[i], dispatch[i], combine[i],
            (total[:8] + shift[...]).astype(BF16), total[8:].astype(BF16),
            wt, vec[...], table[...].astype(BF16),
            q.at[i], k.at[i], v.at[i], p, att.at[i], inv.at[i], ds, grad_t,
            q.at[i], k.at[i], v.at[i], g.at[i], middle.at[i],
            lambda: middle_of(count + i), lambda head: p_in(i, head).wait(), after_heads,
        )
        pltpu.make_async_copy(g.at[i], mixed_hbm.at[i], mixed_sem.at[i]).start()
        add_grads(weight_grad, sums, table_grad, got)
        end_of(count + i)
        return carry

    lax.fori_loop(0, count, backward, 0)

    w_last[0][...] = weight_grad[...].reshape(8, 4, rows, width).astype(BF16)
    weights = Scatter(*w_last)
    weights.start_core()
    gains, biases = norm_sums(sums[...], weight_grad[: 3 * width, :], wt, vec[...])
    pieces = [
        pieces_of(value, length, 32)
        for value, length in zip((gains, biases, table_grad[...], shift_grad[...]), lengths)
    ]
    pieces.append(jnp.zeros((32, 128), F32))
    pieces = jnp.stack([pieces[min(n, 4)] for n in range(16)], axis=1)
    v_last[0][...] = pieces.reshape(8, 4, 16, 128).astype(BF16)
    vectors = Scatter(*v_last)
    vectors.start_core()
    weights.start_plane()
    vectors.start_plane()

    def finish(i, carry):
        x[i] = finish_image(x.at[i], middle.at[i], wt, vec[...], q.at[i], k.at[i], v.at[i])
        pltpu.make_async_copy(x.at[i], patch_grad_hbm.at[i], patch_sem.at[i]).start()

        @pl.when(i == count // 2)
        def _():
            weights.start_z()
            vectors.start_z()

        return carry

    lax.fori_loop(0, count, finish, 0)
    weight_out[...] = weights.finish()
    vectors_out[...] = vectors.finish()
    for i in range(count):
        pltpu.make_async_copy(g.at[i], mixed_hbm.at[i], mixed_sem.at[i]).wait()
        pltpu.make_async_copy(x.at[i], patch_grad_hbm.at[i], patch_sem.at[i]).wait()


def hand_over_kernel(
    mixed, patch_grad, weight_grad, in_grad, out_grad, vectors, bias_grad,
    mixed_out, patch_grad_out, weight_out, in_out, out_out, gains, biases, table, shift, bias_out,
    images, weights, arrived, left,
):
    count = mixed.shape[0]
    moves = []
    for n, (src, dst) in enumerate(((mixed, mixed_out), (patch_grad, patch_grad_out))):
        moves += [(src.at[i], images.at[n, i], dst.at[i]) for i in range(count)]
    at = 0
    for src, dst in ((weight_grad, weight_out), (in_grad, in_out), (out_grad, out_out)):
        moves.append((src, weights.at[pl.ds(at, src.shape[0])], dst))
        at += src.shape[0]
    copies = [
        (
            pltpu.make_async_copy(src, stage, arrived.at[n]),
            pltpu.make_async_copy(stage, dst, left.at[n]),
        )
        for n, (src, stage, dst) in enumerate(moves)
    ]
    for come, _ in copies:
        come.start()
    for n, ref in enumerate((gains, biases, table, shift)):
        ref[...] = vectors[n : n + 1, : ref.shape[0]].reshape(ref.shape[0])
    experts, units = bias_out.shape
    for e in range(experts):
        bias_out[e : e + 1, :] = bias_grad[e : e + 1, e * units : (e + 1) * units]
    for come, go in copies:
        come.wait()
        go.start()
    for _, go in copies:
        go.wait()


def run_layer(patches, valid, attn_weights, vectors, expert_in, expert_in_bias, expert_out, out_grad):
    count, length, width = patches.shape
    heads = width // HEAD_DIM
    experts, _, units = expert_in.shape
    rows = attn_weights.shape[1]
    lengths = [v.shape[0] for v in vectors]
    flat = (length, width)
    dma = pltpu.SemaphoreType.DMA
    vmem = pltpu.VMEM
    anywhere = pl.BlockSpec(memory_space=pl.ANY)
    here_all = pl.BlockSpec(memory_space=pltpu.VMEM)
    mixed, patch_grad, _, weight_grad, vector_grads, in_grad, out_grads, bias_grad = pl.pallas_call(
        functools.partial(layer_kernel, lengths),
        in_specs=[anywhere] * 2 + [here_all] * 9,
        out_specs=[anywhere] * 3 + [here_all] * 5,
        out_shape=[
            jax.ShapeDtypeStruct(patches.shape, BF16), jax.ShapeDtypeStruct(patches.shape, BF16),
            jax.ShapeDtypeStruct((count, heads, length, length), BF16),
            jax.ShapeDtypeStruct((rows, width), F32), jax.ShapeDtypeStruct((16, 128), F32),
            jax.ShapeDtypeStruct((experts * units, width), F32),
            jax.ShapeDtypeStruct((experts * units, width), F32),
            jax.ShapeDtypeStruct((experts, experts * units), F32),
        ],
        scratch_shapes=[
            vmem((count,) + flat, BF16), vmem((count,) + flat, BF16),
            vmem((count,) + flat, BF16), vmem((count,) + flat, BF16), vmem((count,) + flat, BF16),
            vmem((count,) + flat, BF16), vmem((count,) + flat, BF16), vmem((count,) + flat, F32),
            vmem((count, experts, length), F32), vmem((count, experts, length), F32),
            vmem((heads, length, length), BF16), vmem((2, length, length), BF16),
            vmem((2 * width, length), BF16), vmem((4 * width, width), BF16),
            vmem((8, width), F32), vmem((experts, width), F32), vmem((experts, width), F32),
            vmem((1, experts * units), F32),
            vmem((4 * width, width), F32), vmem((8, width), F32), vmem((experts, width), F32),
            vmem((experts, width), F32), vmem((16, 128), F32),
            dma((count,)), dma((count,)), dma((heads,)), dma((heads,)), dma((count,)), dma((count,)),
        ]
        + [vmem((count, 8, 4, 16, width), BF16), dma((count, 10)), dma((count, 10))]
        + [
            vmem((3, 8, 4, 16, width), BF16), vmem((3, 4, 4, 16, width), BF16),
            vmem((3, 4, 4, 16, width), BF16), vmem((3, 3, 4, 16, width), BF16),
            vmem((count, 4, 16, width), BF16), vmem((count, 3, 16, width), BF16),
            dma((count, 10)), dma((count, 10)),
        ]
        + fine_scratch(rows, width) + gather_scratch(16, 128)
        + scatter_scratch(rows, width) + scatter_scratch(16, 128),
        compiler_params=pltpu.CompilerParams(
            collective_id=0, has_side_effects=True, vmem_limit_bytes=LAYER_LIMIT
        ),
        name="layer",
    )(
        patches, out_grad, valid, attn_weights.T, *vectors,
        expert_in.transpose(0, 2, 1).reshape(experts * units, width), expert_in_bias,
        expert_out.reshape(experts * units, width),
    )
    results = pl.pallas_call(
        hand_over_kernel,
        in_specs=[anywhere] * 5 + [here_all] * 2,
        out_specs=[anywhere] * 5 + [here_all] * 5,
        out_shape=[
            jax.ShapeDtypeStruct(value.shape, value.dtype)
            for value in (mixed, patch_grad, weight_grad, in_grad, out_grads)
        ]
        + [jax.ShapeDtypeStruct((piece,), F32) for piece in lengths]
        + [jax.ShapeDtypeStruct((experts, units), F32)],
        scratch_shapes=[
            vmem((2,) + patches.shape, BF16), vmem((rows + 2 * experts * units, width), F32),
            dma((2 * count + 3,)), dma((2 * count + 3,)),
        ],
        compiler_params=pltpu.CompilerParams(vmem_limit_bytes=VMEM_LIMIT),
        name="hand_over",
    )(mixed, patch_grad, weight_grad, in_grad, out_grads, vector_grads, bias_grad)
    mixed, patch_grad, weight_grad, in_grad, out_grads, gains, biases, table, shift, bias_grad = results
    return (
        mixed,
        patch_grad,
        weight_grad.T,
        gains,
        biases,
        table,
        in_grad.reshape(experts, units, width).transpose(0, 2, 1),
        bias_grad,
        out_grads.reshape(experts, units, width),
        shift,
    )


def scatter_sum(parts):
    got = lax.all_to_all(parts.astype(BF16), AXES, 0, 0, tiled=True)
    return jnp.sum(got.astype(F32), axis=0)


def experts_at_home(slots, produced_grad, expert_in, expert_in_bias, expert_out, devices):
    local_images, experts, width = slots.shape
    every = lax.all_gather(jnp.stack([slots, produced_grad]), AXES, axis=1, tiled=True)
    all_slots, all_grads = every[0], every[1]
    hidden = jnp.einsum(
        "bed,edf->bef", all_slots, expert_in, preferred_element_type=F32
    ) + expert_in_bias.astype(F32)
    active, gelu_back = jax.vjp(smooth, hidden)
    active = active.astype(BF16)
    partial = jnp.einsum("bef,efd->bed", active, expert_out, preferred_element_type=F32)
    active_grad = jnp.einsum("bed,efd->bef", all_grads, expert_out, preferred_element_type=F32)
    hidden_grad = gelu_back(active_grad)[0].astype(BF16)
    partial_back = jnp.einsum("bef,edf->bed", hidden_grad, expert_in, preferred_element_type=F32)
    contract_grad = jnp.einsum("bef,bed->efd", active, all_grads, preferred_element_type=F32)
    expand_grad = jnp.einsum("bed,bef->edf", all_slots, hidden_grad, preferred_element_type=F32)
    inner_grad = jnp.sum(hidden_grad.astype(F32), axis=0)
    both = jnp.stack([partial, partial_back]).reshape(2, devices, local_images, experts, width)
    both = scatter_sum(jnp.moveaxis(both, 1, 0))
    return (both[0], both[1], expand_grad, inner_grad, contract_grad)


def on_device(
    patches,
    valid,
    attn_weights,
    norm_gains,
    vec_biases,
    slot_params,
    expert_in,
    expert_in_bias,
    expert_out,
    expert_out_bias,
    out_grad,
):
    local_images, patch_count, width = patches.shape
    experts = expert_in.shape[0]
    devices = lax.axis_size("wide") * lax.axis_size("narrow")

    vectors = (norm_gains, vec_biases, slot_params, expert_out_bias)
    lengths = [v.shape[0] for v in vectors]
    if lax.axis_size("wide") == 8 and lax.axis_size("narrow") == 4:
        return run_layer(
            patches, valid, attn_weights, vectors, expert_in, expert_in_bias, expert_out, out_grad
        )
    wt = lax.all_gather(attn_weights.T, AXES, axis=0, tiled=True)
    small = lax.all_gather(jnp.concatenate(vectors), AXES)
    pieces = []
    at = 0
    for length in lengths:
        pieces.append(small[:, at : at + length].reshape(-1, width))
        at += length
    gains, biases, table, expert_shift = pieces
    vec = jnp.concatenate([gains, biases, jnp.zeros((2, width), BF16)]).astype(F32)

    *kept, slots, produced_grad = run_forward(
        patches, out_grad, valid.reshape(local_images, 1, patch_count), wt, vec, table
    )
    produced, slot_grad, expand_grad, inner_grad, contract_grad = experts_at_home(
        slots, produced_grad, expert_in, expert_in_bias, expert_out, devices
    )
    produced = (produced + expert_shift.astype(F32)).astype(BF16)
    slot_grad = slot_grad.astype(BF16)
    shift_grad = jnp.sum(produced_grad.astype(F32), axis=0)
    mixed_out, patch_grad, weight_grad, rows, table_grad = run_backward(
        patches, out_grad, kept, produced, slot_grad, wt, vec, table
    )
    weight_front = weight_grad[: 3 * width]
    weight_grad = weight_grad.reshape(devices, -1, width)
    gain_grads, bias_grads = norm_sums(rows, weight_front, wt, vec)
    small_grads = jnp.concatenate(
        [v.reshape(devices, -1) for v in (gain_grads, bias_grads, table_grad, shift_grad)], axis=1
    )
    weight_grad = scatter_sum(weight_grad).T
    small_grads = jnp.sum(lax.all_to_all(small_grads, AXES, 0, 0, tiled=True), axis=0)
    grads = []
    at = 0
    for length in lengths:
        grads.append(small_grads[at : at + length])
        at += length
    return (
        mixed_out,
        patch_grad,
        weight_grad,
        grads[0],
        grads[1],
        grads[2],
        expand_grad,
        inner_grad,
        contract_grad,
        grads[3],
    )


def solution(mesh):
    images = P(AXES, None, None)
    vector = P(AXES)
    second = P(None, AXES)
    return jax.shard_map(
        on_device,
        mesh=mesh,
        in_specs=(
            images, P(AXES, None), second, vector, vector, vector,
            P(None, None, AXES), second, P(None, AXES, None), vector, images,
        ),
        out_specs=(
            images, images, second, vector, vector, vector,
            P(None, None, AXES), second, P(None, AXES, None), vector,
        ),
        check_vma=False,
    )
```

```python
import functools

import jax
import jax.numpy as jnp
from jax import lax
from jax.experimental import pallas as pl
from jax.experimental.pallas import tpu as pltpu
from jax.sharding import PartitionSpec as P

HEAD_DIM = 64
PAIR = 2 * HEAD_DIM
MASKED = -1000000000.0
AXES = ("wide", "narrow")
BF16 = jnp.bfloat16
F32 = jnp.float32
MESH = pl.DeviceIdType.MESH
VMEM_LIMIT = 60 * 1024 * 1024
LAYER_LIMIT = 63 * 1024 * 1024
GAIN1, GAIN2, BIAS1, VBIAS, OBIAS, BIAS2 = range(6)


def dot(left, right, left_dim, right_dim):
    return lax.dot_general(
        left, right, (((left_dim,), (right_dim,)), ((), ())), preferred_element_type=F32
    )


def normalize(values):
    centred = values - jnp.mean(values, axis=-1, keepdims=True)
    factor = lax.rsqrt(jnp.mean(centred * centred, axis=-1, keepdims=True) + 1e-06)
    return (centred * factor, factor)


def norm_back(grad_hat, normed, factor):
    return factor * (
        grad_hat
        - jnp.mean(grad_hat, axis=-1, keepdims=True)
        - normed * jnp.mean(grad_hat * normed, axis=-1, keepdims=True)
    )


def smooth(values):
    return jax.nn.gelu(values, approximate=False)


def lower_half(shape):
    return lax.broadcasted_iota(jnp.int32, shape, 1) < HEAD_DIM


def own_half(low, head, own, other):
    return jnp.where(low, own, other) if head % 2 == 0 else jnp.where(low, other, own)


def projections(x, wt, vec, q_ref, k_ref, v_ref):
    width = x.shape[1]
    kept = []

    def start():
        normed, _ = normalize(x[...].astype(F32))
        kept.append((normed * vec[GAIN1 : GAIN1 + 1] + vec[BIAS1 : BIAS1 + 1]).astype(BF16))

    def query():
        q_ref[...] = (dot(kept[0], wt[:width], 1, 1) * HEAD_DIM ** (-0.5)).astype(BF16)

    def key():
        k_ref[...] = dot(kept[0], wt[width : 2 * width], 1, 1).astype(BF16)

    def value():
        got = dot(kept[0], wt[2 * width : 3 * width], 1, 1)
        v_ref[...] = (got + vec[VBIAS : VBIAS + 1]).astype(BF16)

    return [start, query, key, value]


def forward_image(
    x, g, valid_row, wt, vec, table, q_ref, k_ref, v_ref, p_ref, att_ref, inv_ref,
    after_head=None,
):
    patches, width = x.shape
    heads = width // HEAD_DIM
    bias_row = jnp.where(valid_row > 0, 0.0, MASKED).astype(F32)
    fill = jnp.broadcast_to(bias_row * (1.0 / HEAD_DIM), (PAIR, patches)).T.astype(BF16)
    low = lower_half((patches, PAIR))
    one = jnp.ones((patches, PAIR), BF16)
    scores = {}

    def pair_of(ref, head):
        at = head // 2 * PAIR
        return ref[:, at : at + PAIR]

    def score(head):
        scores[head] = dot(
            own_half(low, head, pair_of(q_ref, head), one),
            own_half(low, head, pair_of(k_ref, head), fill),
            1,
            1,
        )

    sums = {}
    score(0)
    for head in range(heads):
        if head + 1 < heads:
            score(head + 1)
        raw = scores.pop(head)
        prob = jnp.exp(raw - jnp.max(raw, axis=1, keepdims=True)).astype(BF16)
        p_ref[head] = prob
        sums[head] = dot(prob, own_half(low, head, pair_of(v_ref, head), one), 1, 0)
        if after_head is not None:
            after_head(head)
        if head % 2 == 1:
            even, odd = sums.pop(head - 1), sums.pop(head)
            inverse = 1.0 / pltpu.roll(jnp.where(low, odd, even), HEAD_DIM, 1)
            at = head // 2 * PAIR
            inv_ref[:, at : at + PAIR] = inverse.astype(inv_ref.dtype)
            att_ref[:, at : at + PAIR] = (jnp.where(low, even, odd) * inverse).astype(BF16)
    branch = dot(att_ref[...], wt[3 * width :], 1, 1)
    middle = x[...].astype(F32) + branch + vec[OBIAS : OBIAS + 1]
    normed, _ = normalize(middle)
    second = (normed * vec[GAIN2 : GAIN2 + 1] + vec[BIAS2 : BIAS2 + 1]).astype(BF16)
    logits = dot(table, second, 1, 1)
    masked = jnp.where(valid_row > 0, logits, MASKED)
    dispatch = jnp.exp(masked - jnp.max(masked, axis=1, keepdims=True))
    dispatch = dispatch / jnp.sum(dispatch, axis=1, keepdims=True)
    combine = jnp.exp(logits - jnp.max(logits, axis=0, keepdims=True))
    combine = combine / jnp.sum(combine, axis=0, keepdims=True)
    slots = dot(dispatch.astype(BF16), second, 1, 0)
    produced_grad = dot(combine.astype(BF16), g[...], 1, 0)
    return middle, dispatch, combine, slots, produced_grad


def backward_image(
    x, g, middle_ref, dispatch, combine, produced, slot_grad, wt, vec, table,
    q_ref, k_ref, v_ref, p_ref, att_ref, inv_ref, ds_ref, grad_t_ref, dq_ref, dk_ref, dv_ref,
    mixed_ref, grad_ref,
    before_heads=None, after_heads=None,
):
    patches, width = x.shape
    heads = width // HEAD_DIM
    combine_low = combine.astype(BF16)
    dispatch_low = dispatch.astype(BF16)
    middle = middle_ref[...]
    normed, factor = normalize(middle)
    second = (normed * vec[GAIN2 : GAIN2 + 1] + vec[BIAS2 : BIAS2 + 1]).astype(BF16)
    upstream = g[...]
    mixed = (middle + dot(combine_low, produced, 0, 0)).astype(BF16)
    combine_grad = dot(produced, upstream, 1, 1)
    dispatch_grad = dot(slot_grad, second, 1, 1)
    logit_grad = dispatch * (
        dispatch_grad - jnp.sum(dispatch * dispatch_grad, axis=1, keepdims=True)
    ) + combine * (combine_grad - jnp.sum(combine * combine_grad, axis=0, keepdims=True))
    logit_grad = logit_grad.astype(BF16)
    table_grad = dot(logit_grad, second, 1, 0)
    second_grad = dot(
        jnp.concatenate([dispatch_low, logit_grad], axis=0),
        jnp.concatenate([slot_grad, table], axis=0),
        0,
        0,
    )
    gain_two = jnp.sum(second_grad * normed, axis=0, keepdims=True)
    shift_two = jnp.sum(second_grad, axis=0, keepdims=True)
    middle_grad = upstream.astype(F32) + norm_back(
        second_grad * vec[GAIN2 : GAIN2 + 1], normed, factor
    )
    mixed_ref[...] = mixed
    grad_ref[...] = middle_grad
    branch_grad = middle_grad.astype(BF16)
    branch_shift = jnp.sum(branch_grad.astype(F32), axis=0, keepdims=True)
    output_grad = dot(branch_grad.T, att_ref[...], 1, 0)
    attended_grad = dot(branch_grad, wt[3 * width :], 1, 0).astype(BF16).astype(F32)
    scaled = attended_grad * inv_ref[...].astype(F32)
    drop = (-(scaled * att_ref[...].astype(F32))).astype(BF16)
    scaled = scaled.astype(BF16)
    scaled_t = scaled.T
    query_t = q_ref[...].T
    if before_heads is not None:
        before_heads()
    low = lower_half((patches, PAIR))
    one = jnp.ones((patches, PAIR), BF16)
    prob_grads = {}

    def pair_of(ref, head):
        at = head // 2 * PAIR
        return ref[:, at : at + PAIR]

    def prob_grad(head):
        rolled = pltpu.roll(pair_of(drop, head).astype(F32), HEAD_DIM, 1).astype(BF16)
        prob_grads[head] = dot(
            own_half(low, head, pair_of(scaled, head), rolled),
            own_half(low, head, pair_of(v_ref, head), one),
            1,
            1,
        )

    query_grads = {}
    prob_grad(0)
    for head in range(heads):
        if head + 1 < heads:
            prob_grad(head + 1)
        rows = slice(head * HEAD_DIM, (head + 1) * HEAD_DIM)
        prob = p_ref[head]
        grad_t_ref[width + rows.start : width + rows.stop, :] = dot(
            scaled_t[rows], prob, 1, 0
        ).astype(BF16)
        score_grad = (prob.astype(F32) * prob_grads.pop(head)).astype(BF16)
        ds_ref[head % 2] = score_grad
        score_grad = ds_ref[head % 2]
        query_grads[head] = dot(score_grad, pair_of(k_ref, head), 1, 0)
        grad_t_ref[rows, :] = dot(query_t[rows], score_grad, 1, 0).astype(BF16)
        if head % 2 == 1:
            both = jnp.where(low, query_grads.pop(head - 1), query_grads.pop(head))
            at = head // 2 * PAIR
            dq_ref[:, at : at + PAIR] = (both * HEAD_DIM ** (-0.5)).astype(BF16)
    if after_heads is not None:
        after_heads()
    dk_ref[...] = grad_t_ref[:width, :].T
    dv_ref[...] = grad_t_ref[width:, :].T
    normed, _ = normalize(x[...].astype(F32))
    first = (normed * vec[GAIN1 : GAIN1 + 1] + vec[BIAS1 : BIAS1 + 1]).astype(BF16)
    query_front = dot(dq_ref[...].T, first, 1, 0)
    other_front = dot(grad_t_ref[...], first, 1, 0)
    columns = [
        jnp.sum(ref[...].astype(F32), axis=0, keepdims=True) for ref in (dq_ref, dk_ref, dv_ref)
    ]
    sums = jnp.concatenate(
        columns + [gain_two, branch_shift, shift_two, jnp.zeros((2, width), F32)], axis=0
    )
    return query_front, other_front, output_grad, sums, table_grad


def finish_image(x, middle_grad, wt, vec, dq_ref, dk_ref, dv_ref):
    width = x.shape[1]
    normed, factor = normalize(x[...].astype(F32))
    project_grad = jnp.concatenate([dq_ref[...], dk_ref[...], dv_ref[...]], axis=1)
    first_grad = dot(project_grad, wt[: 3 * width], 1, 0)
    grad = middle_grad[...] + norm_back(first_grad * vec[GAIN1 : GAIN1 + 1], normed, factor)
    return grad.astype(BF16)


def norm_sums(sums, weight_grad, wt, vec):
    width = wt.shape[1]
    high = sums.astype(BF16)
    both = jnp.concatenate([high, (sums - high.astype(F32)).astype(BF16)], axis=0)
    shift_one = jnp.zeros((1, width), F32)
    for part in range(3):
        got = dot(both, wt[part * width : (part + 1) * width], 1, 0)
        shift_one += got[part : part + 1] + got[8 + part : 9 + part]
    product = jnp.sum(weight_grad * wt[: 3 * width].astype(F32), axis=0, keepdims=True)
    gain_one = (product - vec[BIAS1 : BIAS1 + 1] * shift_one) / vec[GAIN1 : GAIN1 + 1]
    gains = jnp.concatenate([gain_one, sums[3:4]], axis=0)
    return gains, jnp.concatenate([shift_one, sums[2:3], sums[4:5], sums[5:6]], axis=0)


def forward_kernel(
    x, g, valid, wt, vec, table,
    q, k, v, p, att, inv, middle, dispatch, combine, slots, produced_grad,
):
    for step in projections(x.at[0], wt, vec[...], q.at[0], k.at[0], v.at[0]):
        step()
    got = forward_image(
        x.at[0], g.at[0], valid[0], wt, vec[...], table[...],
        q.at[0], k.at[0], v.at[0], p.at[0], att.at[0], inv.at[0],
    )
    for ref, value in zip((middle, dispatch, combine, slots, produced_grad), got):
        ref[0] = value.astype(ref.dtype)


def add_grads(weight_grad, sums, table_grad, got):
    width = weight_grad.shape[1]
    for ref, at, value in (
        (weight_grad, 0, got[0]), (weight_grad, width, got[1]), (weight_grad, 3 * width, got[2]),
        (sums, 0, got[3]), (table_grad, 0, got[4]),
    ):
        ref[at : at + value.shape[0], :] += value


def backward_kernel(
    x, g, middle, dispatch, combine, produced, slot_grad, wt, vec, table,
    q, k, v, p, att, inv,
    mixed, patch_grad, weight_grad, sums, table_grad,
    ds, grad_t, dq, dk, dv, middle_grad,
):
    @pl.when(pl.program_id(0) == 0)
    def _():
        weight_grad[...] = jnp.zeros_like(weight_grad)
        sums[...] = jnp.zeros_like(sums)
        table_grad[...] = jnp.zeros_like(table_grad)

    got = backward_image(
        x.at[0], g.at[0], middle.at[0], dispatch[0], combine[0], produced[0], slot_grad[0],
        wt, vec[...], table[...],
        q.at[0], k.at[0], v.at[0], p.at[0], att.at[0], inv.at[0], ds, grad_t, dq, dk, dv,
        mixed.at[0], middle_grad,
    )
    patch_grad[0] = finish_image(x.at[0], middle_grad, wt, vec[...], dq, dk, dv)
    add_grads(weight_grad, sums, table_grad, got)


def per_image(*shape):
    return pl.BlockSpec((1,) + shape, lambda i: (i,) + (0,) * len(shape))


def whole(*shape):
    return pl.BlockSpec(shape, lambda i: (0,) * len(shape))


def run_forward(x, g, valid, wt, vec, table):
    count, patches, width = x.shape
    heads = width // HEAD_DIM
    experts = table.shape[0]
    flat = (patches, width)
    outs = [
        (flat, BF16), (flat, BF16), (flat, BF16), ((heads, patches, patches), BF16),
        (flat, BF16), (flat, F32), (flat, F32),
        ((experts, patches), F32), ((experts, patches), F32),
        ((experts, width), BF16), ((experts, width), BF16),
    ]
    return pl.pallas_call(
        forward_kernel,
        grid=(count,),
        in_specs=[
            per_image(*flat), per_image(*flat), per_image(1, patches),
            whole(*wt.shape), whole(*vec.shape), whole(*table.shape),
        ],
        out_specs=[per_image(*shape) for shape, _ in outs],
        out_shape=[jax.ShapeDtypeStruct((count,) + shape, kind) for shape, kind in outs],
        compiler_params=pltpu.CompilerParams(vmem_limit_bytes=VMEM_LIMIT),
        name="forward",
    )(x, g, valid, wt, vec, table)


def run_backward(x, g, kept, produced, slot_grad, wt, vec, table):
    count, patches, width = x.shape
    heads = width // HEAD_DIM
    experts = table.shape[0]
    flat = (patches, width)
    q, k, v, p, att, inv, middle, dispatch, combine = kept
    return pl.pallas_call(
        backward_kernel,
        grid=(count,),
        in_specs=[
            per_image(*flat), per_image(*flat), per_image(*flat),
            per_image(experts, patches), per_image(experts, patches),
            per_image(experts, width), per_image(experts, width),
            whole(*wt.shape), whole(*vec.shape), whole(*table.shape),
            per_image(*flat), per_image(*flat), per_image(*flat),
            per_image(heads, patches, patches), per_image(*flat), per_image(*flat),
        ],
        out_specs=[
            per_image(*flat), per_image(*flat),
            whole(4 * width, width), whole(8, width), whole(experts, width),
        ],
        out_shape=[
            jax.ShapeDtypeStruct(x.shape, BF16), jax.ShapeDtypeStruct(x.shape, BF16),
            jax.ShapeDtypeStruct((4 * width, width), F32), jax.ShapeDtypeStruct((8, width), F32),
            jax.ShapeDtypeStruct((experts, width), F32),
        ],
        scratch_shapes=[
            pltpu.VMEM((2, patches, patches), BF16),
            pltpu.VMEM((2 * width, patches), BF16),
            pltpu.VMEM(flat, BF16),
            pltpu.VMEM(flat, BF16),
            pltpu.VMEM(flat, BF16),
            pltpu.VMEM(flat, F32),
        ],
        compiler_params=pltpu.CompilerParams(vmem_limit_bytes=VMEM_LIMIT),
        name="backward",
    )(x, g, middle, dispatch, combine, produced, slot_grad, wt, vec, table, q, k, v, p, att, inv)


def here():
    return lax.axis_index("wide"), lax.axis_index("narrow")


def along_z(w, z):
    return [(w, lax.rem(z + step, 4)) for step in (1, 2, 3)]


def in_plane(w, z):
    x_flip = 2 - 4 * lax.rem(w // 2, 2)
    y_flip = 4 - 8 * (w // 4)
    return [(w + x_flip, z), (w + y_flip, z), (w + x_flip + y_flip, z)]


def other_core(w, z):
    return (w + 1 - 2 * lax.rem(w, 2), z)


def greet():
    w, z = here()
    barrier = pltpu.get_barrier_semaphore()
    peers = along_z(w, z) + in_plane(w, z) + [other_core(w, z)]
    for peer in peers:
        pl.semaphore_signal(barrier, inc=1, device_id=peer, device_id_type=MESH)
    pl.semaphore_wait(barrier, len(peers))


def remote(src, dst, send, recv, peer):
    return pltpu.make_async_remote_copy(
        src_ref=src, dst_ref=dst, send_sem=send, recv_sem=recv, device_id=peer, device_id_type=MESH
    )


class Gather:
    def __init__(self, every, send, recv):
        self.every, self.send, self.recv = every, send, recv
        self.w, self.z = here()
        self.core, self.chip = lax.rem(self.w, 2), self.w // 2

    def z_copies(self):
        own = self.every.at[self.core, self.chip, self.z]
        return [
            remote(own, own, self.send.at[n], self.recv.at[n], peer)
            for n, peer in enumerate(along_z(self.w, self.z))
        ]

    def plane_copies(self):
        own = self.every.at[self.core, self.chip]
        return [
            remote(own, own, self.send.at[3 + n], self.recv.at[3 + n], peer)
            for n, peer in enumerate(in_plane(self.w, self.z))
        ]

    def core_copy(self):
        own = self.every.at[self.core]
        return remote(own, own, self.send.at[6], self.recv.at[6], other_core(self.w, self.z))

    def start_z(self):
        for copy in self.z_copies():
            copy.start()

    def start_plane(self):
        for copy in self.z_copies():
            copy.wait()
        for copy in self.plane_copies():
            copy.start()

    def start_core(self):
        for copy in self.plane_copies():
            copy.wait()
        self.core_copy().start()

    def finish(self):
        self.core_copy().wait()


class FineGather:
    def __init__(self, every, z_send, z_recv, p_send, p_recv, c_send, c_recv):
        self.every = every
        self.z_sems, self.p_sems, self.c_sems = (z_send, z_recv), (p_send, p_recv), (c_send, c_recv)
        self.w, self.z = here()
        self.plane = in_plane(self.w, self.z)

    def block(self, w, k):
        return self.every.at[lax.rem(w, 2), w // 2, lax.rem(self.z + 4 - k, 4)]

    def z_copy(self, n):
        own = self.block(self.w, 0)
        peer = along_z(self.w, self.z)[n]
        return remote(own, own, self.z_sems[0].at[n], self.z_sems[1].at[n], peer)

    def plane_copy(self, n, k):
        own = self.block(self.w, k)
        return remote(own, own, self.p_sems[0].at[n, k], self.p_sems[1].at[n, k], self.plane[n])

    def core_copy(self, group, k):
        own = self.block(self.w if group == 0 else self.plane[group - 1][0], k)
        return remote(
            own, own, self.c_sems[0].at[group, k], self.c_sems[1].at[group, k],
            other_core(self.w, self.z),
        )

    def pass_on(self, k):
        for n in range(3):
            self.plane_copy(n, k).start()
        self.core_copy(0, k).start()

    def start(self):
        for n in range(3):
            self.z_copy(n).start()
        self.pass_on(0)

    def start_plane(self):
        for n in range(3):
            self.z_copy(n).wait()
            self.pass_on(n + 1)

    def start_core(self):
        for k in range(4):
            for n in range(3):
                self.plane_copy(n, k).wait()
                self.core_copy(n + 1, k).start()

    def finish(self):
        for group in range(4):
            for k in range(4):
                self.core_copy(group, k).wait()


class Scatter:
    def __init__(
        self, parts, from_core, chips, from_plane, column, from_z, send, recv, by_chip=False
    ):
        self.parts, self.from_core, self.chips = parts, from_core, chips
        self.from_plane, self.column, self.from_z = from_plane, column, from_z
        self.send, self.recv, self.by_chip = send, recv, by_chip
        self.w, self.z = here()
        self.core = lax.rem(self.w, 2)

    def core_copy(self, chip=None):
        src, dst = self.parts.at[1 - self.core], self.from_core
        if chip is not None:
            src, dst = src.at[chip], dst.at[chip]
        at = 0 if chip is None else chip
        return remote(src, dst, self.send.at[at], self.recv.at[at], other_core(self.w, self.z))

    def chip_order(self):
        return [there // 2 for there, _ in in_plane(self.w, self.z)] + [self.w // 2]

    def plane_copies(self):
        return [
            remote(
                self.chips.at[peer[0] // 2], self.from_plane.at[n],
                self.send.at[4 + n], self.recv.at[4 + n], peer,
            )
            for n, peer in enumerate(in_plane(self.w, self.z))
        ]

    def z_copies(self):
        return [
            remote(
                self.column.at[peer[1]], self.from_z.at[n],
                self.send.at[7 + n], self.recv.at[7 + n], peer,
            )
            for n, peer in enumerate(along_z(self.w, self.z))
        ]

    def start_core(self):
        if not self.by_chip:
            self.core_copy().start()
            return
        for chip in self.chip_order():
            self.core_copy(chip).start()

    def start_plane(self):
        if not self.by_chip:
            self.core_copy().wait()
            total = self.parts[self.core].astype(F32) + self.from_core[...].astype(F32)
            self.chips[...] = total.astype(BF16)
            for copy in self.plane_copies():
                copy.start()
            return
        for chip, copy in zip(self.chip_order(), self.plane_copies() + [None]):
            self.core_copy(chip).wait()
            own = self.parts[self.core, chip].astype(F32)
            self.chips[chip] = (own + self.from_core[chip].astype(F32)).astype(BF16)
            if copy is not None:
                copy.start()

    def start_z(self):
        for copy in self.plane_copies():
            copy.wait()
        total = self.chips[self.w // 2].astype(F32)
        for n in range(3):
            total = total + self.from_plane[n].astype(F32)
        self.column[...] = total.astype(BF16)
        for copy in self.z_copies():
            copy.start()

    def finish(self):
        for copy in self.z_copies():
            copy.wait()

    def total(self):
        total = self.column[self.z].astype(F32)
        for n in range(3):
            total = total + self.from_z[n].astype(F32)
        return total


def by_device(blocks):
    return jnp.concatenate([blocks[core, chip] for chip in range(4) for core in range(2)], axis=0)


def fill_blocks(blocks, values):
    for chip in range(4):
        for core in range(2):
            at = (2 * chip + core) * 4
            blocks[core, chip] = values[at : at + 4].astype(blocks.dtype)


def gather_scratch(rows, width):
    dma = pltpu.SemaphoreType.DMA
    return [pltpu.VMEM((2, 4, 4, rows, width), BF16), dma((7,)), dma((7,))]


def fine_scratch(rows, width):
    dma = pltpu.SemaphoreType.DMA
    return [
        pltpu.VMEM((2, 4, 4, rows, width), BF16),
        dma((3,)), dma((3,)), dma((3, 4)), dma((3, 4)), dma((4, 4)), dma((4, 4)),
    ]


def scatter_scratch(rows, width):
    return [
        pltpu.VMEM((2, 4, 4, rows, width), BF16),
        pltpu.VMEM((4, 4, rows, width), BF16),
        pltpu.VMEM((4, 4, rows, width), BF16),
        pltpu.VMEM((3, 4, rows, width), BF16),
        pltpu.VMEM((4, rows, width), BF16),
        pltpu.VMEM((3, rows, width), BF16),
        pltpu.SemaphoreType.DMA((10,)),
        pltpu.SemaphoreType.DMA((10,)),
    ]


def expert_rows(slots, grads, w_in, bias, w_out):
    rows, width = slots.shape
    units = w_in.shape[0]
    shape = (rows, units)
    own = lax.rem(lax.broadcasted_iota(jnp.int32, shape, 0), 8)
    start = own * (units // 8)
    lane = lax.broadcasted_iota(jnp.int32, shape, 1)
    keep = (lane >= start) & (lane < start + units // 8)
    hidden = dot(slots, w_in, 1, 1) + bias
    active_grad = dot(grads, w_out, 1, 1)
    half = 0.5 * (1.0 + lax.erf(hidden * 0.7071067811865476))
    active = jnp.where(keep, hidden * half, 0.0).astype(BF16)
    slope = half + hidden * jnp.exp(hidden * hidden * -0.5) * 0.3989422804014327
    hidden_grad = jnp.where(keep, active_grad * slope, 0.0).astype(BF16)
    produced = dot(active, w_out, 1, 0)
    slot_grad = dot(hidden_grad, w_in, 1, 0)
    in_grad = dot(hidden_grad, slots, 0, 0)
    out_grad = dot(active, grads, 0, 0)
    bias_grad = jnp.sum(hidden_grad.astype(F32).reshape(-1, 8, units), axis=0)
    return produced, slot_grad, in_grad, out_grad, bias_grad


def one_hot(length, width):
    row = lax.broadcasted_iota(jnp.int32, (128, width), 0)
    column = lax.broadcasted_iota(jnp.int32, (128, width), 1)
    return (row == lax.rem(column, length)).astype(BF16)


def own_piece(shape, length):
    device = lax.broadcasted_iota(jnp.int32, shape, 0)
    column = lax.broadcasted_iota(jnp.int32, shape, 1)
    return lax.rem(device, shape[1] // length) == column // length


def spread(pieces, length, width):
    devices = pieces.shape[0]
    tall = dot(pieces.astype(BF16), one_hot(length, width), 1, 0)
    tall = jnp.where(own_piece(tall.shape, length), tall, 0.0).astype(BF16)
    row = lax.broadcasted_iota(jnp.int32, (8, devices), 0)
    device = lax.broadcasted_iota(jnp.int32, (8, devices), 1)
    return dot((device // (width // length) == row).astype(BF16), tall, 1, 0)


def pieces_of(rows, length, devices):
    count, width = rows.shape
    per_row = width // length
    tall = jnp.broadcast_to(rows[:, None], (count, per_row, width)).reshape(devices, width)
    tall = jnp.where(own_piece(tall.shape, length), tall, 0.0)
    return dot(tall.astype(BF16), one_hot(length, width), 1, 1)


def layer_kernel(
    lengths,
    x_hbm, g_hbm, valid, own_weights, own_gains, own_biases, own_table, own_shift, w_in, own_bias, w_out,
    mixed_hbm, patch_grad_hbm, p_hbm, weight_out, vectors_out, in_grad, out_grad, bias_grad,
    x, g, q, k, v, att, inv, middle, dispatch, combine, p, ds, grad_t, wt, vec, table, shift, bias,
    weight_grad, sums, table_grad, shift_grad, own_pieces,
    x_sem, g_sem, p_out_sem, p_in_sem, mixed_sem, patch_sem,
    every, g_send, g_recv,
    parts, from_core, chips, from_plane, column, from_z, s_send, s_recv,
    *rest,
):
    count, patches, width = x.shape
    heads = width // HEAD_DIM
    rows = own_weights.shape[0]
    wide, narrow = here()
    me = (lax.rem(wide, 2), wide // 2, narrow)
    (w_every, *w_sems), (v_every, *v_sems) = rest[:7], rest[7:10]
    w_last, v_last = rest[10:18], rest[18:26]

    for i in range(count):
        pltpu.make_async_copy(x_hbm.at[i], x.at[i], x_sem.at[i]).start()
        pltpu.make_async_copy(g_hbm.at[i], g.at[i], g_sem.at[i]).start()
    w_every[me] = own_weights[...]
    own_pieces[...] = jnp.zeros_like(own_pieces)
    for n, ref in enumerate((own_gains, own_biases, own_table, own_shift)):
        own_pieces[n : n + 1, : lengths[n]] = ref[...].astype(F32).reshape(1, lengths[n])
    v_every[me] = own_pieces[...].astype(BF16)
    greet()
    weights = FineGather(w_every, *w_sems)
    vectors = Gather(v_every, *v_sems)
    vectors.start_z()
    weights.start()
    for ref in (weight_grad, sums, table_grad, shift_grad, in_grad, out_grad, bias_grad):
        ref[...] = jnp.zeros_like(ref)
    units = w_in.shape[0] // 8
    spread_bias = dot(own_bias[...], one_hot(units, 8 * units)[:units], 1, 0)
    at = lax.broadcasted_iota(jnp.int32, spread_bias.shape, 0)
    lane = lax.broadcasted_iota(jnp.int32, spread_bias.shape, 1)
    bias[...] = jnp.sum(jnp.where(lane // units == at, spread_bias, 0.0), axis=0, keepdims=True)
    vectors.start_plane()
    weights.start_plane()
    vectors.start_core()
    weights.start_core()
    vectors.finish()
    packed = by_device(v_every).astype(F32)
    gains, biases, slot_rows, shift_rows = (
        spread(packed[:, n], length, width) for n, length in enumerate(lengths)
    )
    vec[...] = jnp.concatenate([gains[:2], biases[:4], jnp.zeros((2, width), F32)], axis=0)
    table[...] = slot_rows
    shift[...] = shift_rows
    weights.finish()
    wt[...] = by_device(w_every).reshape(4 * width, width)

    def slots_way(i):
        return Gather(every.at[i], g_send.at[i], g_recv.at[i])

    def results_way(i):
        ring = lax.rem(i, 2)
        return Scatter(
            parts.at[ring], from_core.at[ring], chips.at[ring], from_plane.at[i], column.at[i],
            from_z.at[i], s_send.at[i], s_recv.at[i],
        )

    def for_image(i, action):
        @pl.when((i >= 0) & (i < count))
        def _():
            action(i)

    def experts(i):
        slots_way(i).finish()
        both = every[i].astype(F32).reshape(32, 2, 8, width)
        got = expert_rows(
            both[:, 0].reshape(32 * 8, width).astype(BF16),
            both[:, 1].reshape(32 * 8, width).astype(BF16),
            w_in[...], bias[...], w_out[...],
        )
        back = jnp.stack([got[0].reshape(32, 8, width), got[1].reshape(32, 8, width)], axis=1)
        parts[lax.rem(i, 2)] = back.reshape(2, 4, 4, 16, width).astype(BF16)
        in_grad[...] += got[2]
        out_grad[...] += got[3]
        bias_grad[...] += got[4]
        results_way(i).start_core()

    def middle_of(step):
        for_image(step - 3, experts)

    def end_of(step):
        for_image(step - 4, lambda i: results_way(i).start_z())
        for_image(step - 3, lambda i: results_way(i).start_plane())
        for_image(step - 2, lambda i: slots_way(i).start_core())
        for_image(step - 1, lambda i: slots_way(i).start_plane())

    def p_out(i, head):
        return pltpu.make_async_copy(p.at[head], p_hbm.at[i, head], p_out_sem.at[head])

    def p_in(i, head):
        return pltpu.make_async_copy(p_hbm.at[i, head], p.at[head], p_in_sem.at[head])

    def arrive(hbm, ref, sem, i):
        pltpu.make_async_copy(hbm.at[i], ref.at[i], sem.at[i]).wait()

    def forward(i, carry):
        arrive(x_hbm, x, x_sem, i)
        for step in projections(x.at[i], wt, vec[...], q.at[i], k.at[i], v.at[i]):
            step()
        arrive(g_hbm, g, g_sem, i)
        middle_of(i)

        @pl.when(i > 0)
        def _():
            for head in range(heads):
                p_out(i - 1, head).wait()

        got = forward_image(
            x.at[i], g.at[i], valid[pl.ds(i, 1)], wt, vec[...], table[...].astype(BF16),
            q.at[i], k.at[i], v.at[i], p, att.at[i], inv.at[i], lambda head: p_out(i, head).start(),
        )
        middle[i], dispatch[i], combine[i] = got[:3]
        shift_grad[...] += got[4].astype(BF16).astype(F32)
        every[(i,) + me] = jnp.concatenate([got[3], got[4]], axis=0).astype(BF16)
        end_of(i)
        slots_way(i).start_z()
        return carry

    lax.fori_loop(0, count, forward, 0)
    for head in range(heads):
        p_out(count - 1, head).wait()
        p_in(0, head).start()

    def backward(i, carry):
        def before_heads():
            middle_of(count + i)
            for head in range(heads):
                p_in(i, head).wait()

        def after_heads():
            @pl.when(i + 1 < count)
            def _():
                for head in range(heads):
                    p_in(i + 1, head).start()

        results_way(i).finish()
        total = results_way(i).total()
        got = backward_image(
            x.at[i], g.at[i], middle.at[i], dispatch[i], combine[i],
            (total[:8] + shift[...]).astype(BF16), total[8:].astype(BF16),
            wt, vec[...], table[...].astype(BF16),
            q.at[i], k.at[i], v.at[i], p, att.at[i], inv.at[i], ds, grad_t,
            q.at[i], k.at[i], v.at[i], g.at[i], middle.at[i],
            before_heads, after_heads,
        )
        pltpu.make_async_copy(g.at[i], mixed_hbm.at[i], mixed_sem.at[i]).start()
        add_grads(weight_grad, sums, table_grad, got)
        end_of(count + i)
        return carry

    lax.fori_loop(0, count, backward, 0)

    fill_blocks(w_last[0], weight_grad[...].reshape(32, rows, width))
    weights = Scatter(*w_last, by_chip=True)
    weights.start_core()
    gains, biases = norm_sums(sums[...], weight_grad[: 3 * width, :], wt, vec[...])
    pieces = [
        pieces_of(value, length, 32)
        for value, length in zip((gains, biases, table_grad[...], shift_grad[...]), lengths)
    ]
    pieces.append(jnp.zeros((32, 128), F32))
    pieces = jnp.stack([pieces[min(n, 4)] for n in range(16)], axis=1)
    fill_blocks(v_last[0], pieces)
    vectors = Scatter(*v_last)
    vectors.start_core()
    weights.start_plane()
    vectors.start_plane()

    def finish(i, carry):
        x[i] = finish_image(x.at[i], middle.at[i], wt, vec[...], q.at[i], k.at[i], v.at[i])
        pltpu.make_async_copy(x.at[i], patch_grad_hbm.at[i], patch_sem.at[i]).start()

        @pl.when(i == count // 2)
        def _():
            weights.start_z()
            vectors.start_z()

        return carry

    lax.fori_loop(0, count, finish, 0)
    weights.finish()
    weight_out[...] = weights.total()
    vectors.finish()
    vectors_out[...] = vectors.total()
    for i in range(count):
        pltpu.make_async_copy(g.at[i], mixed_hbm.at[i], mixed_sem.at[i]).wait()
        pltpu.make_async_copy(x.at[i], patch_grad_hbm.at[i], patch_sem.at[i]).wait()


def hand_over_kernel(
    mixed, patch_grad, weight_grad, in_grad, out_grad, vectors, bias_grad,
    mixed_out, patch_grad_out, weight_out, in_out, out_out, gains, biases, table, shift, bias_out,
    images, weights, arrived, left,
):
    count = mixed.shape[0]
    moves = []
    for n, (src, dst) in enumerate(((mixed, mixed_out), (patch_grad, patch_grad_out))):
        moves += [(src.at[i], images.at[n, i], dst.at[i]) for i in range(count)]
    at = 0
    for src, dst in ((weight_grad, weight_out), (in_grad, in_out), (out_grad, out_out)):
        moves.append((src, weights.at[pl.ds(at, src.shape[0])], dst))
        at += src.shape[0]
    copies = [
        (
            pltpu.make_async_copy(src, stage, arrived.at[n]),
            pltpu.make_async_copy(stage, dst, left.at[n]),
        )
        for n, (src, stage, dst) in enumerate(moves)
    ]
    for come, _ in copies:
        come.start()
    for n, ref in enumerate((gains, biases, table, shift)):
        ref[...] = vectors[n : n + 1, : ref.shape[0]].reshape(ref.shape[0])
    experts, units = bias_out.shape
    for e in range(experts):
        bias_out[e : e + 1, :] = bias_grad[e : e + 1, e * units : (e + 1) * units]
    for come, go in copies:
        come.wait()
        go.start()
    for _, go in copies:
        go.wait()


def run_layer(patches, valid, attn_weights, vectors, expert_in, expert_in_bias, expert_out, out_grad):
    count, length, width = patches.shape
    heads = width // HEAD_DIM
    experts, _, units = expert_in.shape
    rows = attn_weights.shape[1]
    lengths = [v.shape[0] for v in vectors]
    flat = (length, width)
    dma = pltpu.SemaphoreType.DMA
    vmem = pltpu.VMEM
    anywhere = pl.BlockSpec(memory_space=pl.ANY)
    here_all = pl.BlockSpec(memory_space=pltpu.VMEM)
    mixed, patch_grad, _, weight_grad, vector_grads, in_grad, out_grads, bias_grad = pl.pallas_call(
        functools.partial(layer_kernel, lengths),
        in_specs=[anywhere] * 2 + [here_all] * 9,
        out_specs=[anywhere] * 3 + [here_all] * 5,
        out_shape=[
            jax.ShapeDtypeStruct(patches.shape, BF16), jax.ShapeDtypeStruct(patches.shape, BF16),
            jax.ShapeDtypeStruct((count, heads, length, length), BF16),
            jax.ShapeDtypeStruct((rows, width), F32), jax.ShapeDtypeStruct((16, 128), F32),
            jax.ShapeDtypeStruct((experts * units, width), F32),
            jax.ShapeDtypeStruct((experts * units, width), F32),
            jax.ShapeDtypeStruct((experts, experts * units), F32),
        ],
        scratch_shapes=[
            vmem((count,) + flat, BF16), vmem((count,) + flat, BF16),
            vmem((count,) + flat, BF16), vmem((count,) + flat, BF16), vmem((count,) + flat, BF16),
            vmem((count,) + flat, BF16), vmem((count,) + flat, BF16), vmem((count,) + flat, F32),
            vmem((count, experts, length), F32), vmem((count, experts, length), F32),
            vmem((heads, length, length), BF16), vmem((2, length, length), BF16),
            vmem((2 * width, length), BF16), vmem((4 * width, width), BF16),
            vmem((8, width), F32), vmem((experts, width), F32), vmem((experts, width), F32),
            vmem((1, experts * units), F32),
            vmem((4 * width, width), F32), vmem((8, width), F32), vmem((experts, width), F32),
            vmem((experts, width), F32), vmem((16, 128), F32),
            dma((count,)), dma((count,)), dma((heads,)), dma((heads,)), dma((count,)), dma((count,)),
        ]
        + [vmem((count, 2, 4, 4, 16, width), BF16), dma((count, 7)), dma((count, 7))]
        + [
            vmem((2, 2, 4, 4, 16, width), BF16), vmem((2, 4, 4, 16, width), BF16),
            vmem((2, 4, 4, 16, width), BF16), vmem((count, 3, 4, 16, width), BF16),
            vmem((count, 4, 16, width), BF16), vmem((count, 3, 16, width), BF16),
            dma((count, 10)), dma((count, 10)),
        ]
        + fine_scratch(rows, width) + gather_scratch(16, 128)
        + scatter_scratch(rows, width) + scatter_scratch(16, 128),
        compiler_params=pltpu.CompilerParams(
            collective_id=0, has_side_effects=True, vmem_limit_bytes=LAYER_LIMIT
        ),
        name="layer",
    )(
        patches, out_grad, valid, attn_weights.T, *vectors,
        expert_in.transpose(0, 2, 1).reshape(experts * units, width), expert_in_bias,
        expert_out.reshape(experts * units, width),
    )
    results = pl.pallas_call(
        hand_over_kernel,
        in_specs=[anywhere] * 5 + [here_all] * 2,
        out_specs=[anywhere] * 5 + [here_all] * 5,
        out_shape=[
            jax.ShapeDtypeStruct(value.shape, value.dtype)
            for value in (mixed, patch_grad, weight_grad, in_grad, out_grads)
        ]
        + [jax.ShapeDtypeStruct((piece,), F32) for piece in lengths]
        + [jax.ShapeDtypeStruct((experts, units), F32)],
        scratch_shapes=[
            vmem((2,) + patches.shape, BF16), vmem((rows + 2 * experts * units, width), F32),
            dma((2 * count + 3,)), dma((2 * count + 3,)),
        ],
        compiler_params=pltpu.CompilerParams(vmem_limit_bytes=VMEM_LIMIT),
        name="hand_over",
    )(mixed, patch_grad, weight_grad, in_grad, out_grads, vector_grads, bias_grad)
    mixed, patch_grad, weight_grad, in_grad, out_grads, gains, biases, table, shift, bias_grad = results
    return (
        mixed,
        patch_grad,
        weight_grad.T,
        gains,
        biases,
        table,
        in_grad.reshape(experts, units, width).transpose(0, 2, 1),
        bias_grad,
        out_grads.reshape(experts, units, width),
        shift,
    )


def scatter_sum(parts):
    got = lax.all_to_all(parts.astype(BF16), AXES, 0, 0, tiled=True)
    return jnp.sum(got.astype(F32), axis=0)


def experts_at_home(slots, produced_grad, expert_in, expert_in_bias, expert_out, devices):
    local_images, experts, width = slots.shape
    every = lax.all_gather(jnp.stack([slots, produced_grad]), AXES, axis=1, tiled=True)
    all_slots, all_grads = every[0], every[1]
    hidden = jnp.einsum(
        "bed,edf->bef", all_slots, expert_in, preferred_element_type=F32
    ) + expert_in_bias.astype(F32)
    active, gelu_back = jax.vjp(smooth, hidden)
    active = active.astype(BF16)
    partial = jnp.einsum("bef,efd->bed", active, expert_out, preferred_element_type=F32)
    active_grad = jnp.einsum("bed,efd->bef", all_grads, expert_out, preferred_element_type=F32)
    hidden_grad = gelu_back(active_grad)[0].astype(BF16)
    partial_back = jnp.einsum("bef,edf->bed", hidden_grad, expert_in, preferred_element_type=F32)
    contract_grad = jnp.einsum("bef,bed->efd", active, all_grads, preferred_element_type=F32)
    expand_grad = jnp.einsum("bed,bef->edf", all_slots, hidden_grad, preferred_element_type=F32)
    inner_grad = jnp.sum(hidden_grad.astype(F32), axis=0)
    both = jnp.stack([partial, partial_back]).reshape(2, devices, local_images, experts, width)
    both = scatter_sum(jnp.moveaxis(both, 1, 0))
    return (both[0], both[1], expand_grad, inner_grad, contract_grad)


def on_device(
    patches,
    valid,
    attn_weights,
    norm_gains,
    vec_biases,
    slot_params,
    expert_in,
    expert_in_bias,
    expert_out,
    expert_out_bias,
    out_grad,
):
    local_images, patch_count, width = patches.shape
    experts = expert_in.shape[0]
    devices = lax.axis_size("wide") * lax.axis_size("narrow")

    vectors = (norm_gains, vec_biases, slot_params, expert_out_bias)
    lengths = [v.shape[0] for v in vectors]
    if lax.axis_size("wide") == 8 and lax.axis_size("narrow") == 4:
        return run_layer(
            patches, valid, attn_weights, vectors, expert_in, expert_in_bias, expert_out, out_grad
        )
    wt = lax.all_gather(attn_weights.T, AXES, axis=0, tiled=True)
    small = lax.all_gather(jnp.concatenate(vectors), AXES)
    pieces = []
    at = 0
    for length in lengths:
        pieces.append(small[:, at : at + length].reshape(-1, width))
        at += length
    gains, biases, table, expert_shift = pieces
    vec = jnp.concatenate([gains, biases, jnp.zeros((2, width), BF16)]).astype(F32)

    *kept, slots, produced_grad = run_forward(
        patches, out_grad, valid.reshape(local_images, 1, patch_count), wt, vec, table
    )
    produced, slot_grad, expand_grad, inner_grad, contract_grad = experts_at_home(
        slots, produced_grad, expert_in, expert_in_bias, expert_out, devices
    )
    produced = (produced + expert_shift.astype(F32)).astype(BF16)
    slot_grad = slot_grad.astype(BF16)
    shift_grad = jnp.sum(produced_grad.astype(F32), axis=0)
    mixed_out, patch_grad, weight_grad, rows, table_grad = run_backward(
        patches, out_grad, kept, produced, slot_grad, wt, vec, table
    )
    weight_front = weight_grad[: 3 * width]
    weight_grad = weight_grad.reshape(devices, -1, width)
    gain_grads, bias_grads = norm_sums(rows, weight_front, wt, vec)
    small_grads = jnp.concatenate(
        [v.reshape(devices, -1) for v in (gain_grads, bias_grads, table_grad, shift_grad)], axis=1
    )
    weight_grad = scatter_sum(weight_grad).T
    small_grads = jnp.sum(lax.all_to_all(small_grads, AXES, 0, 0, tiled=True), axis=0)
    grads = []
    at = 0
    for length in lengths:
        grads.append(small_grads[at : at + length])
        at += length
    return (
        mixed_out,
        patch_grad,
        weight_grad,
        grads[0],
        grads[1],
        grads[2],
        expand_grad,
        inner_grad,
        contract_grad,
        grads[3],
    )


def solution(mesh):
    images = P(AXES, None, None)
    vector = P(AXES)
    second = P(None, AXES)
    return jax.shard_map(
        on_device,
        mesh=mesh,
        in_specs=(
            images, P(AXES, None), second, vector, vector, vector,
            P(None, None, AXES), second, P(None, AXES, None), vector, images,
        ),
        out_specs=(
            images, images, second, vector, vector, vector,
            P(None, None, AXES), second, P(None, AXES, None), vector,
        ),
        check_vma=False,
    )
```

```python
import functools

import jax
import jax.numpy as jnp
from jax import lax
from jax.experimental import pallas as pl
from jax.experimental.pallas import tpu as pltpu
from jax.sharding import PartitionSpec as P

HEAD_DIM = 64
PAIR = 2 * HEAD_DIM
MASKED = -1000000000.0
AXES = ("wide", "narrow")
BF16 = jnp.bfloat16
F32 = jnp.float32
MESH = pl.DeviceIdType.MESH
VMEM_LIMIT = 60 * 1024 * 1024
LAYER_LIMIT = 56 * 1024 * 1024
GAIN1, GAIN2, BIAS1, VBIAS, OBIAS, BIAS2 = range(6)


def dot(left, right, left_dim, right_dim):
    return lax.dot_general(
        left, right, (((left_dim,), (right_dim,)), ((), ())), preferred_element_type=F32
    )


def normalize(values):
    centred = values - jnp.mean(values, axis=-1, keepdims=True)
    factor = lax.rsqrt(jnp.mean(centred * centred, axis=-1, keepdims=True) + 1e-06)
    return (centred * factor, factor)


def norm_back(grad_hat, normed, factor):
    return factor * (
        grad_hat
        - jnp.mean(grad_hat, axis=-1, keepdims=True)
        - normed * jnp.mean(grad_hat * normed, axis=-1, keepdims=True)
    )


def smooth(values):
    return jax.nn.gelu(values, approximate=False)


def lower_half(shape):
    return lax.broadcasted_iota(jnp.int32, shape, 1) < HEAD_DIM


def own_half(low, head, own, other):
    return jnp.where(low, own, other) if head % 2 == 0 else jnp.where(low, other, own)


def projections(normed, wt, vec, q_ref, k_ref, v_ref):
    width = wt.shape[1]
    first = (normed[...] * vec[GAIN1 : GAIN1 + 1] + vec[BIAS1 : BIAS1 + 1]).astype(BF16)
    got = dot(first, wt[: 3 * width], 1, 1)
    q_ref[...] = (got[:, :width] * HEAD_DIM ** (-0.5)).astype(BF16)
    k_ref[...] = got[:, width : 2 * width].astype(BF16)
    v_ref[...] = (got[:, 2 * width :] + vec[VBIAS : VBIAS + 1]).astype(BF16)


def forward_image(
    x, g, valid_row, wt, vec, table, q_ref, k_ref, v_ref, p_ref, att_ref, inv_ref,
    after_head=None,
):
    patches, width = x.shape
    heads = width // HEAD_DIM
    bias_row = jnp.where(valid_row > 0, 0.0, MASKED).astype(F32)
    fill = jnp.broadcast_to(bias_row * (1.0 / HEAD_DIM), (PAIR, patches)).T.astype(BF16)
    low = lower_half((patches, PAIR))
    one = jnp.ones((patches, PAIR), BF16)
    scores = {}

    def pair_of(ref, head):
        at = head // 2 * PAIR
        return ref[:, at : at + PAIR]

    def score(head):
        scores[head] = dot(
            own_half(low, head, pair_of(q_ref, head), one),
            own_half(low, head, pair_of(k_ref, head), fill),
            1,
            1,
        )

    sums = {}
    score(0)
    for head in range(heads):
        if head + 1 < heads:
            score(head + 1)
        raw = scores.pop(head)
        prob = jnp.exp(raw - jnp.max(raw, axis=1, keepdims=True)).astype(BF16)
        p_ref[head] = prob
        sums[head] = dot(prob, own_half(low, head, pair_of(v_ref, head), one), 1, 0)
        if after_head is not None:
            after_head(head)
        if head % 2 == 1:
            even, odd = sums.pop(head - 1), sums.pop(head)
            inverse = 1.0 / pltpu.roll(jnp.where(low, odd, even), HEAD_DIM, 1)
            at = head // 2 * PAIR
            inv_ref[:, at : at + PAIR] = inverse.astype(inv_ref.dtype)
            att_ref[:, at : at + PAIR] = (jnp.where(low, even, odd) * inverse).astype(BF16)
    branch = dot(att_ref[...], wt[3 * width :], 1, 1)
    middle = x[...].astype(F32) + branch + vec[OBIAS : OBIAS + 1]
    normed, _ = normalize(middle)
    second = (normed * vec[GAIN2 : GAIN2 + 1] + vec[BIAS2 : BIAS2 + 1]).astype(BF16)
    logits = dot(table, second, 1, 1)
    masked = jnp.where(valid_row > 0, logits, MASKED)
    dispatch = jnp.exp(masked - jnp.max(masked, axis=1, keepdims=True))
    dispatch = dispatch / jnp.sum(dispatch, axis=1, keepdims=True)
    combine = jnp.exp(logits - jnp.max(logits, axis=0, keepdims=True))
    combine = combine / jnp.sum(combine, axis=0, keepdims=True)
    slots = dot(dispatch.astype(BF16), second, 1, 0)
    produced_grad = dot(combine.astype(BF16), g[...], 1, 0)
    return middle, dispatch, combine, slots, produced_grad


def backward_image(
    x, g, middle_ref, dispatch, combine, produced, slot_grad, wt, vec, table,
    q_ref, k_ref, v_ref, p_ref, att_ref, inv_ref, ds_ref, grad_t_ref, dq_ref, dk_ref, dv_ref, grad_ref,
    before_heads=None, after_heads=None,
):
    patches, width = x.shape
    heads = width // HEAD_DIM
    dispatch_low = dispatch.astype(BF16)
    middle = middle_ref[...]
    normed, factor = normalize(middle)
    second = (normed * vec[GAIN2 : GAIN2 + 1] + vec[BIAS2 : BIAS2 + 1]).astype(BF16)
    upstream = g[...]
    combine_grad = dot(produced, upstream, 1, 1)
    dispatch_grad = dot(slot_grad, second, 1, 1)
    logit_grad = dispatch * (
        dispatch_grad - jnp.sum(dispatch * dispatch_grad, axis=1, keepdims=True)
    ) + combine * (combine_grad - jnp.sum(combine * combine_grad, axis=0, keepdims=True))
    logit_grad = logit_grad.astype(BF16)
    table_grad = dot(logit_grad, second, 1, 0)
    second_grad = dot(
        jnp.concatenate([dispatch_low, logit_grad], axis=0),
        jnp.concatenate([slot_grad, table], axis=0),
        0,
        0,
    )
    gain_two = jnp.sum(second_grad * normed, axis=0, keepdims=True)
    shift_two = jnp.sum(second_grad, axis=0, keepdims=True)
    middle_grad = upstream.astype(F32) + norm_back(
        second_grad * vec[GAIN2 : GAIN2 + 1], normed, factor
    )
    grad_ref[...] = middle_grad
    branch_grad = middle_grad.astype(BF16)
    branch_shift = jnp.sum(branch_grad.astype(F32), axis=0, keepdims=True)
    output_grad = dot(branch_grad.T, att_ref[...], 1, 0)
    attended_grad = dot(branch_grad, wt[3 * width :], 1, 0).astype(BF16).astype(F32)
    scaled = attended_grad * inv_ref[...].astype(F32)
    drop = (-(scaled * att_ref[...].astype(F32))).astype(BF16)
    scaled = scaled.astype(BF16)
    scaled_t = scaled.T
    query_t = q_ref[...].T
    if before_heads is not None:
        before_heads()
    low = lower_half((patches, PAIR))
    one = jnp.ones((patches, PAIR), BF16)
    prob_grads = {}

    def pair_of(ref, head):
        at = head // 2 * PAIR
        return ref[:, at : at + PAIR]

    def prob_grad(head):
        rolled = pltpu.roll(pair_of(drop, head).astype(F32), HEAD_DIM, 1).astype(BF16)
        prob_grads[head] = dot(
            own_half(low, head, pair_of(scaled, head), rolled),
            own_half(low, head, pair_of(v_ref, head), one),
            1,
            1,
        )

    query_grads = {}
    prob_grad(0)
    for head in range(heads):
        if head + 1 < heads:
            prob_grad(head + 1)
        rows = slice(head * HEAD_DIM, (head + 1) * HEAD_DIM)
        prob = p_ref[head]
        grad_t_ref[width + rows.start : width + rows.stop, :] = dot(
            scaled_t[rows], prob, 1, 0
        ).astype(BF16)
        score_grad = (prob.astype(F32) * prob_grads.pop(head)).astype(BF16)
        ds_ref[head % 2] = score_grad
        score_grad = ds_ref[head % 2]
        query_grads[head] = dot(score_grad, pair_of(k_ref, head), 1, 0)
        grad_t_ref[rows, :] = dot(query_t[rows], score_grad, 1, 0).astype(BF16)
        if head % 2 == 1:
            both = jnp.where(low, query_grads.pop(head - 1), query_grads.pop(head))
            at = head // 2 * PAIR
            dq_ref[:, at : at + PAIR] = (both * HEAD_DIM ** (-0.5)).astype(BF16)
    if after_heads is not None:
        after_heads()
    dk_ref[...] = grad_t_ref[:width, :].T
    dv_ref[...] = grad_t_ref[width:, :].T
    normed, _ = normalize(x[...].astype(F32))
    first = (normed * vec[GAIN1 : GAIN1 + 1] + vec[BIAS1 : BIAS1 + 1]).astype(BF16)
    query_front = dot(dq_ref[...].T, first, 1, 0)
    other_front = dot(grad_t_ref[...], first, 1, 0)
    columns = [
        jnp.sum(ref[...].astype(F32), axis=0, keepdims=True) for ref in (dq_ref, dk_ref, dv_ref)
    ]
    sums = jnp.concatenate(
        columns + [gain_two, branch_shift, shift_two, jnp.zeros((2, width), F32)], axis=0
    )
    return query_front, other_front, output_grad, sums, table_grad


def finish_image(x, middle, middle_grad, combine, produced, wt, vec, dq_ref, dk_ref, dv_ref):
    width = x.shape[1]
    mixed = middle[...] + dot(combine.astype(BF16), produced, 0, 0)
    normed, factor = normalize(x[...].astype(F32))
    project_grad = jnp.concatenate([dq_ref[...], dk_ref[...], dv_ref[...]], axis=1)
    first_grad = dot(project_grad, wt[: 3 * width], 1, 0)
    grad = middle_grad[...] + norm_back(first_grad * vec[GAIN1 : GAIN1 + 1], normed, factor)
    return mixed.astype(BF16), grad.astype(BF16)


def norm_sums(sums, weight_grad, wt, vec):
    width = wt.shape[1]
    high = sums.astype(BF16)
    both = jnp.concatenate([high, (sums - high.astype(F32)).astype(BF16)], axis=0)
    shift_one = jnp.zeros((1, width), F32)
    for part in range(3):
        got = dot(both, wt[part * width : (part + 1) * width], 1, 0)
        shift_one += got[part : part + 1] + got[8 + part : 9 + part]
    product = jnp.sum(weight_grad * wt[: 3 * width].astype(F32), axis=0, keepdims=True)
    gain_one = (product - vec[BIAS1 : BIAS1 + 1] * shift_one) / vec[GAIN1 : GAIN1 + 1]
    gains = jnp.concatenate([gain_one, sums[3:4]], axis=0)
    return gains, jnp.concatenate([shift_one, sums[2:3], sums[4:5], sums[5:6]], axis=0)


def forward_kernel(
    x, g, valid, wt, vec, table,
    q, k, v, p, att, inv, middle, dispatch, combine, slots, produced_grad,
):
    middle[0] = normalize(x[0].astype(F32))[0]
    projections(middle.at[0], wt, vec[...], q.at[0], k.at[0], v.at[0])
    got = forward_image(
        x.at[0], g.at[0], valid[0], wt, vec[...], table[...],
        q.at[0], k.at[0], v.at[0], p.at[0], att.at[0], inv.at[0],
    )
    for ref, value in zip((middle, dispatch, combine, slots, produced_grad), got):
        ref[0] = value.astype(ref.dtype)


def add_grads(weight_grad, sums, table_grad, got):
    width = weight_grad.shape[1]
    for ref, at, value in (
        (weight_grad, 0, got[0]), (weight_grad, width, got[1]), (weight_grad, 3 * width, got[2]),
        (sums, 0, got[3]), (table_grad, 0, got[4]),
    ):
        ref[at : at + value.shape[0], :] += value


def backward_kernel(
    x, g, middle, dispatch, combine, produced, slot_grad, wt, vec, table,
    q, k, v, p, att, inv,
    mixed, patch_grad, weight_grad, sums, table_grad,
    ds, grad_t, dq, dk, dv, middle_grad,
):
    @pl.when(pl.program_id(0) == 0)
    def _():
        weight_grad[...] = jnp.zeros_like(weight_grad)
        sums[...] = jnp.zeros_like(sums)
        table_grad[...] = jnp.zeros_like(table_grad)

    got = backward_image(
        x.at[0], g.at[0], middle.at[0], dispatch[0], combine[0], produced[0], slot_grad[0],
        wt, vec[...], table[...],
        q.at[0], k.at[0], v.at[0], p.at[0], att.at[0], inv.at[0], ds, grad_t, dq, dk, dv,
        middle_grad,
    )
    mixed[0], patch_grad[0] = finish_image(
        x.at[0], middle.at[0], middle_grad, combine[0], produced[0], wt, vec[...], dq, dk, dv
    )
    add_grads(weight_grad, sums, table_grad, got)


def per_image(*shape):
    return pl.BlockSpec((1,) + shape, lambda i: (i,) + (0,) * len(shape))


def whole(*shape):
    return pl.BlockSpec(shape, lambda i: (0,) * len(shape))


def run_forward(x, g, valid, wt, vec, table):
    count, patches, width = x.shape
    heads = width // HEAD_DIM
    experts = table.shape[0]
    flat = (patches, width)
    outs = [
        (flat, BF16), (flat, BF16), (flat, BF16), ((heads, patches, patches), BF16),
        (flat, BF16), (flat, F32), (flat, F32),
        ((experts, patches), F32), ((experts, patches), F32),
        ((experts, width), BF16), ((experts, width), BF16),
    ]
    return pl.pallas_call(
        forward_kernel,
        grid=(count,),
        in_specs=[
            per_image(*flat), per_image(*flat), per_image(1, patches),
            whole(*wt.shape), whole(*vec.shape), whole(*table.shape),
        ],
        out_specs=[per_image(*shape) for shape, _ in outs],
        out_shape=[jax.ShapeDtypeStruct((count,) + shape, kind) for shape, kind in outs],
        compiler_params=pltpu.CompilerParams(vmem_limit_bytes=VMEM_LIMIT),
        name="forward",
    )(x, g, valid, wt, vec, table)


def run_backward(x, g, kept, produced, slot_grad, wt, vec, table):
    count, patches, width = x.shape
    heads = width // HEAD_DIM
    experts = table.shape[0]
    flat = (patches, width)
    q, k, v, p, att, inv, middle, dispatch, combine = kept
    return pl.pallas_call(
        backward_kernel,
        grid=(count,),
        in_specs=[
            per_image(*flat), per_image(*flat), per_image(*flat),
            per_image(experts, patches), per_image(experts, patches),
            per_image(experts, width), per_image(experts, width),
            whole(*wt.shape), whole(*vec.shape), whole(*table.shape),
            per_image(*flat), per_image(*flat), per_image(*flat),
            per_image(heads, patches, patches), per_image(*flat), per_image(*flat),
        ],
        out_specs=[
            per_image(*flat), per_image(*flat),
            whole(4 * width, width), whole(8, width), whole(experts, width),
        ],
        out_shape=[
            jax.ShapeDtypeStruct(x.shape, BF16), jax.ShapeDtypeStruct(x.shape, BF16),
            jax.ShapeDtypeStruct((4 * width, width), F32), jax.ShapeDtypeStruct((8, width), F32),
            jax.ShapeDtypeStruct((experts, width), F32),
        ],
        scratch_shapes=[
            pltpu.VMEM((2, patches, patches), BF16),
            pltpu.VMEM((2 * width, patches), BF16),
            pltpu.VMEM(flat, BF16),
            pltpu.VMEM(flat, BF16),
            pltpu.VMEM(flat, BF16),
            pltpu.VMEM(flat, F32),
        ],
        compiler_params=pltpu.CompilerParams(vmem_limit_bytes=VMEM_LIMIT),
        name="backward",
    )(x, g, middle, dispatch, combine, produced, slot_grad, wt, vec, table, q, k, v, p, att, inv)


def here():
    return lax.axis_index("wide"), lax.axis_index("narrow")


def along_z(w, z):
    return [(w, lax.rem(z + step, 4)) for step in (1, 2, 3)]


def in_plane(w, z):
    x_flip = 2 - 4 * lax.rem(w // 2, 2)
    y_flip = 4 - 8 * (w // 4)
    return [(w + x_flip, z), (w + y_flip, z), (w + x_flip + y_flip, z)]


def other_core(w, z):
    return (w + 1 - 2 * lax.rem(w, 2), z)


def greet():
    w, z = here()
    barrier = pltpu.get_barrier_semaphore()
    peers = along_z(w, z) + in_plane(w, z) + [other_core(w, z)]
    for peer in peers:
        pl.semaphore_signal(barrier, inc=1, device_id=peer, device_id_type=MESH)
    pl.semaphore_wait(barrier, len(peers))


def remote(src, dst, send, recv, peer):
    return pltpu.make_async_remote_copy(
        src_ref=src, dst_ref=dst, send_sem=send, recv_sem=recv, device_id=peer, device_id_type=MESH
    )


class Gather:
    def __init__(self, every, send, recv):
        self.every, self.send, self.recv = every, send, recv
        self.w, self.z = here()
        self.core, self.chip = lax.rem(self.w, 2), self.w // 2

    def z_copies(self):
        own = self.every.at[self.core, self.chip, self.z]
        return [
            remote(own, own, self.send.at[n], self.recv.at[n], peer)
            for n, peer in enumerate(along_z(self.w, self.z))
        ]

    def plane_copies(self):
        own = self.every.at[self.core, self.chip]
        return [
            remote(own, own, self.send.at[3 + n], self.recv.at[3 + n], peer)
            for n, peer in enumerate(in_plane(self.w, self.z))
        ]

    def core_copy(self):
        own = self.every.at[self.core]
        return remote(own, own, self.send.at[6], self.recv.at[6], other_core(self.w, self.z))

    def start_z(self):
        for copy in self.z_copies():
            copy.start()

    def start_plane(self):
        for copy in self.z_copies():
            copy.wait()
        for copy in self.plane_copies():
            copy.start()

    def start_core(self):
        for copy in self.plane_copies():
            copy.wait()
        self.core_copy().start()

    def finish(self):
        self.core_copy().wait()


class FineGather:
    def __init__(self, every, z_send, z_recv, p_send, p_recv, c_send, c_recv):
        self.every = every
        self.z_sems, self.p_sems, self.c_sems = (z_send, z_recv), (p_send, p_recv), (c_send, c_recv)
        self.w, self.z = here()
        self.plane = in_plane(self.w, self.z)

    def block(self, w, k):
        return self.every.at[lax.rem(w, 2), w // 2, lax.rem(self.z + 4 - k, 4)]

    def z_copy(self, n):
        own = self.block(self.w, 0)
        peer = along_z(self.w, self.z)[n]
        return remote(own, own, self.z_sems[0].at[n], self.z_sems[1].at[n], peer)

    def plane_copy(self, n, k):
        own = self.block(self.w, k)
        return remote(own, own, self.p_sems[0].at[n, k], self.p_sems[1].at[n, k], self.plane[n])

    def core_copy(self, group, k):
        own = self.block(self.w if group == 0 else self.plane[group - 1][0], k)
        return remote(
            own, own, self.c_sems[0].at[group, k], self.c_sems[1].at[group, k],
            other_core(self.w, self.z),
        )

    def pass_on(self, k):
        for n in range(3):
            self.plane_copy(n, k).start()
        self.core_copy(0, k).start()

    def start(self):
        for n in range(3):
            self.z_copy(n).start()
        self.pass_on(0)

    def start_plane(self):
        for n in range(3):
            self.z_copy(n).wait()
            self.pass_on(n + 1)

    def start_core(self):
        for k in range(4):
            for n in range(3):
                self.plane_copy(n, k).wait()
                self.core_copy(n + 1, k).start()

    def finish(self):
        for group in range(4):
            for k in range(4):
                self.core_copy(group, k).wait()


class Scatter:
    def __init__(self, parts, from_core, chips, from_plane, column, from_z, send, recv):
        self.parts, self.from_core, self.chips = parts, from_core, chips
        self.from_plane, self.column, self.from_z = from_plane, column, from_z
        self.send, self.recv = send, recv
        self.w, self.z = here()
        self.core = lax.rem(self.w, 2)

    def core_copy(self):
        return remote(
            self.parts.at[1 - self.core], self.from_core, self.send.at[0], self.recv.at[0],
            other_core(self.w, self.z),
        )

    def plane_copies(self):
        return [
            remote(
                self.chips.at[peer[0] // 2], self.from_plane.at[n],
                self.send.at[1 + n], self.recv.at[1 + n], peer,
            )
            for n, peer in enumerate(in_plane(self.w, self.z))
        ]

    def z_copies(self):
        return [
            remote(
                self.column.at[peer[1]], self.from_z.at[n],
                self.send.at[4 + n], self.recv.at[4 + n], peer,
            )
            for n, peer in enumerate(along_z(self.w, self.z))
        ]

    def start_core(self):
        self.core_copy().start()

    def start_plane(self):
        self.core_copy().wait()
        total = self.parts[self.core].astype(F32) + self.from_core[...].astype(F32)
        self.chips[...] = total.astype(BF16)
        for copy in self.plane_copies():
            copy.start()

    def start_z(self):
        for copy in self.plane_copies():
            copy.wait()
        total = self.chips[self.w // 2].astype(F32)
        for n in range(3):
            total = total + self.from_plane[n].astype(F32)
        self.column[...] = total.astype(BF16)
        for copy in self.z_copies():
            copy.start()

    def finish(self):
        for copy in self.z_copies():
            copy.wait()

    def total(self):
        total = self.column[self.z].astype(F32)
        for n in range(3):
            total = total + self.from_z[n].astype(F32)
        return total


class FineScatter:
    def __init__(
        self, parts, from_core, chips, from_plane, column, from_z,
        c_send, c_recv, p_send, p_recv, z_send, z_recv,
    ):
        self.parts, self.from_core, self.chips = parts, from_core, chips
        self.from_plane, self.column, self.from_z = from_plane, column, from_z
        self.c_sems, self.p_sems, self.z_sems = (c_send, c_recv), (p_send, p_recv), (z_send, z_recv)
        self.w, self.z = here()
        self.core = lax.rem(self.w, 2)
        self.plane = in_plane(self.w, self.z)

    def goal(self, k):
        return lax.rem(self.z + k, 4)

    def core_copy(self, chip):
        return remote(
            self.parts.at[1 - self.core, chip], self.from_core.at[chip],
            self.c_sems[0].at[chip], self.c_sems[1].at[chip], other_core(self.w, self.z),
        )

    def plane_copy(self, n, k):
        z = self.goal(k)
        return remote(
            self.chips.at[self.plane[n][0] // 2, z], self.from_plane.at[n, z],
            self.p_sems[0].at[n, k], self.p_sems[1].at[n, k], self.plane[n],
        )

    def z_copy(self, k):
        return remote(
            self.column.at[self.goal(k)], self.from_z.at[k - 1],
            self.z_sems[0].at[k - 1], self.z_sems[1].at[k - 1], (self.w, self.goal(k)),
        )

    def start_core(self):
        for chip in [there // 2 for there, _ in self.plane] + [self.w // 2]:
            self.core_copy(chip).start()

    def start_plane(self):
        for n, chip in enumerate([there // 2 for there, _ in self.plane] + [self.w // 2]):
            self.core_copy(chip).wait()
            own = self.parts[self.core, chip].astype(F32)
            self.chips[chip] = (own + self.from_core[chip].astype(F32)).astype(BF16)
        for k in (1, 2, 3, 0):
            for n in range(3):
                self.plane_copy(n, k).start()

    def plane_sum(self, k):
        z = self.goal(k)
        total = self.chips[self.w // 2, z].astype(F32)
        for n in range(3):
            self.plane_copy(n, k).wait()
            total = total + self.from_plane[n, z].astype(F32)
        return total

    def start_z(self, k):
        self.column[self.goal(k)] = self.plane_sum(k).astype(BF16)
        self.z_copy(k).start()

    def total(self):
        total = self.plane_sum(0)
        for k in (1, 2, 3):
            self.z_copy(k).wait()
            total = total + self.from_z[k - 1].astype(F32)
        return total


def by_device(blocks):
    return jnp.concatenate([blocks[core, chip] for chip in range(4) for core in range(2)], axis=0)


def fill_blocks(blocks, values):
    for chip in range(4):
        for core in range(2):
            at = (2 * chip + core) * 4
            blocks[core, chip] = values[at : at + 4].astype(blocks.dtype)


def gather_scratch(rows, width):
    dma = pltpu.SemaphoreType.DMA
    return [pltpu.VMEM((2, 4, 4, rows, width), BF16), dma((7,)), dma((7,))]


def fine_scratch(rows, width):
    dma = pltpu.SemaphoreType.DMA
    return [
        pltpu.VMEM((2, 4, 4, rows, width), BF16),
        dma((3,)), dma((3,)), dma((3, 4)), dma((3, 4)), dma((4, 4)), dma((4, 4)),
    ]


def scatter_scratch(rows, width):
    return [
        pltpu.VMEM((2, 4, 4, rows, width), BF16),
        pltpu.VMEM((4, 4, rows, width), BF16),
        pltpu.VMEM((4, 4, rows, width), BF16),
        pltpu.VMEM((3, 4, rows, width), BF16),
        pltpu.VMEM((4, rows, width), BF16),
        pltpu.VMEM((3, rows, width), BF16),
        pltpu.SemaphoreType.DMA((7,)),
        pltpu.SemaphoreType.DMA((7,)),
    ]


def expert_rows(slots, grads, w_in, bias, w_out):
    rows, width = slots.shape
    units = w_in.shape[0]
    shape = (rows, units)
    own = lax.rem(lax.broadcasted_iota(jnp.int32, shape, 0), 8)
    start = own * (units // 8)
    lane = lax.broadcasted_iota(jnp.int32, shape, 1)
    keep = (lane >= start) & (lane < start + units // 8)
    hidden = dot(slots, w_in, 1, 1) + bias
    active_grad = dot(grads, w_out, 1, 1)
    half = 0.5 * (1.0 + lax.erf(hidden * 0.7071067811865476))
    active = jnp.where(keep, hidden * half, 0.0).astype(BF16)
    slope = half + hidden * jnp.exp(hidden * hidden * -0.5) * 0.3989422804014327
    hidden_grad = jnp.where(keep, active_grad * slope, 0.0).astype(BF16)
    produced = dot(active, w_out, 1, 0)
    slot_grad = dot(hidden_grad, w_in, 1, 0)
    return produced, slot_grad, active, hidden_grad


def one_hot(length, width):
    row = lax.broadcasted_iota(jnp.int32, (128, width), 0)
    column = lax.broadcasted_iota(jnp.int32, (128, width), 1)
    return (row == lax.rem(column, length)).astype(BF16)


def own_piece(shape, length):
    device = lax.broadcasted_iota(jnp.int32, shape, 0)
    column = lax.broadcasted_iota(jnp.int32, shape, 1)
    return lax.rem(device, shape[1] // length) == column // length


def spread(pieces, length, width):
    devices = pieces.shape[0]
    tall = dot(pieces.astype(BF16), one_hot(length, width), 1, 0)
    tall = jnp.where(own_piece(tall.shape, length), tall, 0.0).astype(BF16)
    row = lax.broadcasted_iota(jnp.int32, (8, devices), 0)
    device = lax.broadcasted_iota(jnp.int32, (8, devices), 1)
    return dot((device // (width // length) == row).astype(BF16), tall, 1, 0)


def pieces_of(rows, length, devices):
    count, width = rows.shape
    per_row = width // length
    tall = jnp.broadcast_to(rows[:, None], (count, per_row, width)).reshape(devices, width)
    tall = jnp.where(own_piece(tall.shape, length), tall, 0.0)
    return dot(tall.astype(BF16), one_hot(length, width), 1, 1)


def layer_kernel(
    lengths,
    x_hbm, g_hbm, valid, own_weights, own_gains, own_biases, own_table, own_shift, w_in, own_bias, w_out,
    g, x, p_hbm, weight_out, vectors_out, in_grad, out_grad, bias_grad,
    q, k, v, att, inv, middle, dispatch, combine, p, ds, grad_t, wt, vec, table, shift, bias,
    weight_grad, sums, table_grad, shift_grad, own_pieces,
    middle_grad, produced, active, hidden_grad,
    x_sem, g_sem, p_out_sem, p_in_sem,
    every, g_send, g_recv,
    parts, from_core, chips, from_plane, column, from_z, s_send, s_recv,
    *rest,
):
    count, patches, width = x.shape
    heads = width // HEAD_DIM
    rows = own_weights.shape[0]
    wide, narrow = here()
    me = (lax.rem(wide, 2), wide // 2, narrow)
    (w_every, *w_sems), (v_every, *v_sems) = rest[:7], rest[7:10]
    w_last, v_last = rest[10:22], rest[22:30]

    for i in range(count):
        pltpu.make_async_copy(x_hbm.at[i], x.at[i], x_sem.at[i]).start()
        pltpu.make_async_copy(g_hbm.at[i], g.at[i], g_sem.at[i]).start()
    w_every[me] = own_weights[...]
    own_pieces[...] = jnp.zeros_like(own_pieces)
    for n, ref in enumerate((own_gains, own_biases, own_table, own_shift)):
        own_pieces[n : n + 1, : lengths[n]] = ref[...].astype(F32).reshape(1, lengths[n])
    v_every[me] = own_pieces[...].astype(BF16)
    greet()
    weights = FineGather(w_every, *w_sems)
    vectors = Gather(v_every, *v_sems)
    vectors.start_z()
    weights.start()
    for ref in (weight_grad, sums, table_grad, shift_grad, in_grad, out_grad, bias_grad):
        ref[...] = jnp.zeros_like(ref)
    units = w_in.shape[0] // 8
    spread_bias = dot(own_bias[...], one_hot(units, 8 * units)[:units], 1, 0)
    at = lax.broadcasted_iota(jnp.int32, spread_bias.shape, 0)
    lane = lax.broadcasted_iota(jnp.int32, spread_bias.shape, 1)
    bias[...] = jnp.sum(jnp.where(lane // units == at, spread_bias, 0.0), axis=0, keepdims=True)
    def arrive(hbm, ref, sem, i):
        pltpu.make_async_copy(hbm.at[i], ref.at[i], sem.at[i]).wait()

    def first_norm(i, carry):
        arrive(x_hbm, x, x_sem, i)
        middle[i] = normalize(x[i].astype(F32))[0]
        return carry

    lax.fori_loop(0, count, first_norm, 0)
    vectors.start_plane()
    weights.start_plane()
    vectors.start_core()
    weights.start_core()
    vectors.finish()
    packed = by_device(v_every).astype(F32)
    gains, biases, slot_rows, shift_rows = (
        spread(packed[:, n], length, width) for n, length in enumerate(lengths)
    )
    vec[...] = jnp.concatenate([gains[:2], biases[:4], jnp.zeros((2, width), F32)], axis=0)
    table[...] = slot_rows
    shift[...] = shift_rows
    weights.finish()
    wt[...] = by_device(w_every).reshape(4 * width, width)

    def slots_way(i):
        return Gather(every.at[i], g_send.at[i], g_recv.at[i])

    def results_way(i):
        ring = lax.rem(i, 2)
        return Scatter(
            parts.at[ring], from_core.at[ring], chips.at[ring], from_plane.at[i], column.at[i],
            from_z.at[i], s_send.at[i], s_recv.at[i],
        )

    def for_image(i, action):
        @pl.when((i >= 0) & (i < count))
        def _():
            action(i)

    def arrived_rows(i):
        both = every[i].astype(F32).reshape(32, 2, 8, width)
        return [both[:, n].reshape(32 * 8, width).astype(BF16) for n in range(2)]

    def experts(i):
        slots_way(i).finish()
        got = expert_rows(*arrived_rows(i), w_in[...], bias[...], w_out[...])
        back = jnp.stack([got[0].reshape(32, 8, width), got[1].reshape(32, 8, width)], axis=1)
        parts[lax.rem(i, 2)] = back.reshape(2, 4, 4, 16, width).astype(BF16)
        active[i], hidden_grad[i] = got[2:]
        results_way(i).start_core()

    def middle_of(step):
        for_image(step - 3, experts)

    def end_of(step):
        for_image(step - 4, lambda i: results_way(i).start_z())
        for_image(step - 3, lambda i: results_way(i).start_plane())
        for_image(step - 2, lambda i: slots_way(i).start_core())
        for_image(step - 1, lambda i: slots_way(i).start_plane())

    def p_out(i, head):
        return pltpu.make_async_copy(p.at[head], p_hbm.at[i, head], p_out_sem.at[head])

    def p_in(i, head):
        return pltpu.make_async_copy(p_hbm.at[i, head], p.at[head], p_in_sem.at[head])

    def forward(i, carry):
        projections(middle.at[i], wt, vec[...], q.at[i], k.at[i], v.at[i])
        arrive(g_hbm, g, g_sem, i)
        middle_of(i)

        @pl.when(i > 0)
        def _():
            for head in range(heads):
                p_out(i - 1, head).wait()

        got = forward_image(
            x.at[i], g.at[i], valid[pl.ds(i, 1)], wt, vec[...], table[...].astype(BF16),
            q.at[i], k.at[i], v.at[i], p, att.at[i], inv.at[i], lambda head: p_out(i, head).start(),
        )
        middle[i], dispatch[i], combine[i] = got[:3]
        shift_grad[...] += got[4].astype(BF16).astype(F32)
        every[(i,) + me] = jnp.concatenate([got[3], got[4]], axis=0).astype(BF16)
        end_of(i)
        slots_way(i).start_z()
        return carry

    lax.fori_loop(0, count, forward, 0)
    for head in range(heads):
        p_out(count - 1, head).wait()
        p_in(0, head).start()

    def backward(i, carry):
        def before_heads():
            middle_of(count + i)
            for head in range(heads):
                p_in(i, head).wait()

        def after_heads():
            @pl.when(i + 1 < count)
            def _():
                for head in range(heads):
                    p_in(i + 1, head).start()

        results_way(i).finish()
        total = results_way(i).total()
        produced[i] = total[:8] + shift[...]
        got = backward_image(
            x.at[i], g.at[i], middle.at[i], dispatch[i], combine[i],
            produced[i].astype(BF16), total[8:].astype(BF16),
            wt, vec[...], table[...].astype(BF16),
            q.at[i], k.at[i], v.at[i], p, att.at[i], inv.at[i], ds, grad_t,
            q.at[i], k.at[i], v.at[i], middle_grad.at[i],
            before_heads, after_heads,
        )
        add_grads(weight_grad, sums, table_grad, got)
        end_of(count + i)
        return carry

    lax.fori_loop(0, count, backward, 0)

    fill_blocks(w_last[0], weight_grad[...].reshape(32, rows, width))
    weights = FineScatter(*w_last)
    weights.start_core()
    gains, biases = norm_sums(sums[...], weight_grad[: 3 * width, :], wt, vec[...])
    pieces = [
        pieces_of(value, length, 32)
        for value, length in zip((gains, biases, table_grad[...], shift_grad[...]), lengths)
    ]
    pieces.append(jnp.zeros((32, 128), F32))
    pieces = jnp.stack([pieces[min(n, 4)] for n in range(16)], axis=1)
    fill_blocks(v_last[0], pieces)
    vectors = Scatter(*v_last)
    vectors.start_core()
    weights.start_plane()
    vectors.start_plane()

    def finish(i, carry):
        g[i], x[i] = finish_image(
            x.at[i], middle.at[i], middle_grad.at[i], combine[i], produced[i].astype(BF16),
            wt, vec[...], q.at[i], k.at[i], v.at[i],
        )
        all_slots, all_grads = arrived_rows(i)
        in_grad[...] += dot(hidden_grad[i], all_slots, 0, 0)
        out_grad[...] += dot(active[i], all_grads, 0, 0)
        bias_grad[...] += jnp.sum(hidden_grad[i].astype(F32).reshape(32, 8, -1), axis=0)

        for block in (1, 2, 3):

            @pl.when(i == block)
            def _(block=block):
                weights.start_z(block)

        @pl.when(i == 3)
        def _():
            vectors.start_z()

        return carry

    lax.fori_loop(0, count, finish, 0)
    weight_out[...] = weights.total()
    vectors.finish()
    vectors_out[...] = vectors.total()


def hand_over_kernel(
    mixed, patch_grad, weight_grad, in_grad, out_grad, vectors, bias_grad,
    mixed_out, patch_grad_out, weight_out, in_out, out_out, gains, biases, table, shift, bias_out, sems,
):
    moves = (
        (mixed, mixed_out), (patch_grad, patch_grad_out), (weight_grad, weight_out),
        (in_grad, in_out), (out_grad, out_out),
    )
    copies = [pltpu.make_async_copy(src, dst, sems.at[n]) for n, (src, dst) in enumerate(moves)]
    for copy in copies:
        copy.start()
    for n, ref in enumerate((gains, biases, table, shift)):
        ref[...] = vectors[n : n + 1, : ref.shape[0]].reshape(ref.shape[0])
    experts, units = bias_out.shape
    for e in range(experts):
        bias_out[e : e + 1, :] = bias_grad[e : e + 1, e * units : (e + 1) * units]
    for copy in copies:
        copy.wait()


def run_layer(patches, valid, attn_weights, vectors, expert_in, expert_in_bias, expert_out, out_grad):
    count, length, width = patches.shape
    heads = width // HEAD_DIM
    experts, _, units = expert_in.shape
    rows = attn_weights.shape[1]
    lengths = [v.shape[0] for v in vectors]
    flat = (length, width)
    dma = pltpu.SemaphoreType.DMA
    vmem = pltpu.VMEM
    anywhere = pl.BlockSpec(memory_space=pl.ANY)
    here_all = pl.BlockSpec(memory_space=pltpu.VMEM)
    mixed, patch_grad, _, weight_grad, vector_grads, in_grad, out_grads, bias_grad = pl.pallas_call(
        functools.partial(layer_kernel, lengths),
        in_specs=[anywhere] * 2 + [here_all] * 9,
        out_specs=[here_all] * 2 + [anywhere] + [here_all] * 5,
        out_shape=[
            vmem(patches.shape, BF16), vmem(patches.shape, BF16),
            jax.ShapeDtypeStruct((count, heads, length, length), BF16),
            vmem((rows, width), F32), vmem((16, 128), F32),
            vmem((experts * units, width), F32), vmem((experts * units, width), F32),
            vmem((experts, experts * units), F32),
        ],
        scratch_shapes=[
            vmem((count,) + flat, BF16), vmem((count,) + flat, BF16), vmem((count,) + flat, BF16),
            vmem((count,) + flat, BF16), vmem((count,) + flat, BF16), vmem((count,) + flat, F32),
            vmem((count, experts, length), F32), vmem((count, experts, length), F32),
            vmem((heads, length, length), BF16), vmem((2, length, length), BF16),
            vmem((2 * width, length), BF16), vmem((4 * width, width), BF16),
            vmem((8, width), F32), vmem((experts, width), F32), vmem((experts, width), F32),
            vmem((1, experts * units), F32),
            vmem((4 * width, width), F32), vmem((8, width), F32), vmem((experts, width), F32),
            vmem((experts, width), F32), vmem((16, 128), F32),
            vmem((count,) + flat, F32), vmem((count, experts, width), F32),
            vmem((count, 32 * experts, experts * units), BF16),
            vmem((count, 32 * experts, experts * units), BF16),
            dma((count,)), dma((count,)), dma((heads,)), dma((heads,)),
        ]
        + [vmem((count, 2, 4, 4, 16, width), BF16), dma((count, 7)), dma((count, 7))]
        + [
            vmem((2, 2, 4, 4, 16, width), BF16), vmem((2, 4, 4, 16, width), BF16),
            vmem((2, 4, 4, 16, width), BF16), vmem((count, 3, 4, 16, width), BF16),
            vmem((count, 4, 16, width), BF16), vmem((count, 3, 16, width), BF16),
            dma((count, 7)), dma((count, 7)),
        ]
        + fine_scratch(rows, width) + gather_scratch(16, 128)
        + scatter_scratch(rows, width)[:6]
        + [dma((4,)), dma((4,)), dma((3, 4)), dma((3, 4)), dma((3,)), dma((3,))]
        + scatter_scratch(16, 128),
        compiler_params=pltpu.CompilerParams(
            collective_id=0, has_side_effects=True, vmem_limit_bytes=LAYER_LIMIT
        ),
        name="layer",
    )(
        patches, out_grad, valid, attn_weights.T, *vectors,
        expert_in.transpose(0, 2, 1).reshape(experts * units, width), expert_in_bias,
        expert_out.reshape(experts * units, width),
    )
    results = pl.pallas_call(
        hand_over_kernel,
        in_specs=[here_all] * 7,
        out_specs=[anywhere] * 5 + [here_all] * 5,
        out_shape=[
            jax.ShapeDtypeStruct(value.shape, value.dtype)
            for value in (mixed, patch_grad, weight_grad, in_grad, out_grads)
        ]
        + [jax.ShapeDtypeStruct((piece,), F32) for piece in lengths]
        + [jax.ShapeDtypeStruct((experts, units), F32)],
        scratch_shapes=[dma((5,))],
        compiler_params=pltpu.CompilerParams(vmem_limit_bytes=8 * 1024 * 1024),
        name="hand_over",
    )(mixed, patch_grad, weight_grad, in_grad, out_grads, vector_grads, bias_grad)
    mixed, patch_grad, weight_grad, in_grad, out_grads, gains, biases, table, shift, bias_grad = results
    return (
        mixed,
        patch_grad,
        weight_grad.T,
        gains,
        biases,
        table,
        in_grad.reshape(experts, units, width).transpose(0, 2, 1),
        bias_grad,
        out_grads.reshape(experts, units, width),
        shift,
    )


def scatter_sum(parts):
    got = lax.all_to_all(parts.astype(BF16), AXES, 0, 0, tiled=True)
    return jnp.sum(got.astype(F32), axis=0)


def experts_at_home(slots, produced_grad, expert_in, expert_in_bias, expert_out, devices):
    local_images, experts, width = slots.shape
    every = lax.all_gather(jnp.stack([slots, produced_grad]), AXES, axis=1, tiled=True)
    all_slots, all_grads = every[0], every[1]
    hidden = jnp.einsum(
        "bed,edf->bef", all_slots, expert_in, preferred_element_type=F32
    ) + expert_in_bias.astype(F32)
    active, gelu_back = jax.vjp(smooth, hidden)
    active = active.astype(BF16)
    partial = jnp.einsum("bef,efd->bed", active, expert_out, preferred_element_type=F32)
    active_grad = jnp.einsum("bed,efd->bef", all_grads, expert_out, preferred_element_type=F32)
    hidden_grad = gelu_back(active_grad)[0].astype(BF16)
    partial_back = jnp.einsum("bef,edf->bed", hidden_grad, expert_in, preferred_element_type=F32)
    contract_grad = jnp.einsum("bef,bed->efd", active, all_grads, preferred_element_type=F32)
    expand_grad = jnp.einsum("bed,bef->edf", all_slots, hidden_grad, preferred_element_type=F32)
    inner_grad = jnp.sum(hidden_grad.astype(F32), axis=0)
    both = jnp.stack([partial, partial_back]).reshape(2, devices, local_images, experts, width)
    both = scatter_sum(jnp.moveaxis(both, 1, 0))
    return (both[0], both[1], expand_grad, inner_grad, contract_grad)


def on_device(
    patches,
    valid,
    attn_weights,
    norm_gains,
    vec_biases,
    slot_params,
    expert_in,
    expert_in_bias,
    expert_out,
    expert_out_bias,
    out_grad,
):
    local_images, patch_count, width = patches.shape
    experts = expert_in.shape[0]
    devices = lax.axis_size("wide") * lax.axis_size("narrow")

    vectors = (norm_gains, vec_biases, slot_params, expert_out_bias)
    lengths = [v.shape[0] for v in vectors]
    if lax.axis_size("wide") == 8 and lax.axis_size("narrow") == 4:
        return run_layer(
            patches, valid, attn_weights, vectors, expert_in, expert_in_bias, expert_out, out_grad
        )
    wt = lax.all_gather(attn_weights.T, AXES, axis=0, tiled=True)
    small = lax.all_gather(jnp.concatenate(vectors), AXES)
    pieces = []
    at = 0
    for length in lengths:
        pieces.append(small[:, at : at + length].reshape(-1, width))
        at += length
    gains, biases, table, expert_shift = pieces
    vec = jnp.concatenate([gains, biases, jnp.zeros((2, width), BF16)]).astype(F32)

    *kept, slots, produced_grad = run_forward(
        patches, out_grad, valid.reshape(local_images, 1, patch_count), wt, vec, table
    )
    produced, slot_grad, expand_grad, inner_grad, contract_grad = experts_at_home(
        slots, produced_grad, expert_in, expert_in_bias, expert_out, devices
    )
    produced = (produced + expert_shift.astype(F32)).astype(BF16)
    slot_grad = slot_grad.astype(BF16)
    shift_grad = jnp.sum(produced_grad.astype(F32), axis=0)
    mixed_out, patch_grad, weight_grad, rows, table_grad = run_backward(
        patches, out_grad, kept, produced, slot_grad, wt, vec, table
    )
    weight_front = weight_grad[: 3 * width]
    weight_grad = weight_grad.reshape(devices, -1, width)
    gain_grads, bias_grads = norm_sums(rows, weight_front, wt, vec)
    small_grads = jnp.concatenate(
        [v.reshape(devices, -1) for v in (gain_grads, bias_grads, table_grad, shift_grad)], axis=1
    )
    weight_grad = scatter_sum(weight_grad).T
    small_grads = jnp.sum(lax.all_to_all(small_grads, AXES, 0, 0, tiled=True), axis=0)
    grads = []
    at = 0
    for length in lengths:
        grads.append(small_grads[at : at + length])
        at += length
    return (
        mixed_out,
        patch_grad,
        weight_grad,
        grads[0],
        grads[1],
        grads[2],
        expand_grad,
        inner_grad,
        contract_grad,
        grads[3],
    )


def solution(mesh):
    images = P(AXES, None, None)
    vector = P(AXES)
    second = P(None, AXES)
    return jax.shard_map(
        on_device,
        mesh=mesh,
        in_specs=(
            images, P(AXES, None), second, vector, vector, vector,
            P(None, None, AXES), second, P(None, AXES, None), vector, images,
        ),
        out_specs=(
            images, images, second, vector, vector, vector,
            P(None, None, AXES), second, P(None, AXES, None), vector,
        ),
        check_vma=False,
    )
```

```python
import functools

import jax
import jax.numpy as jnp
from jax import lax
from jax.experimental import pallas as pl
from jax.experimental.pallas import tpu as pltpu
from jax.sharding import PartitionSpec as P

HEAD_DIM = 64
PAIR = 2 * HEAD_DIM
MASKED = -1000000000.0
AXES = ("wide", "narrow")
BF16 = jnp.bfloat16
F32 = jnp.float32
MESH = pl.DeviceIdType.MESH
VMEM_LIMIT = 60 * 1024 * 1024
LAYER_LIMIT = 56 * 1024 * 1024
GAIN1, GAIN2, BIAS1, VBIAS, OBIAS, BIAS2 = range(6)


def dot(left, right, left_dim, right_dim):
    return lax.dot_general(
        left, right, (((left_dim,), (right_dim,)), ((), ())), preferred_element_type=F32
    )


def normalize(values):
    centred = values - jnp.mean(values, axis=-1, keepdims=True)
    factor = lax.rsqrt(jnp.mean(centred * centred, axis=-1, keepdims=True) + 1e-06)
    return (centred * factor, factor)


def norm_back(grad_hat, normed, factor):
    return factor * (
        grad_hat
        - jnp.mean(grad_hat, axis=-1, keepdims=True)
        - normed * jnp.mean(grad_hat * normed, axis=-1, keepdims=True)
    )


def smooth(values):
    return jax.nn.gelu(values, approximate=False)


def lower_half(shape):
    return lax.broadcasted_iota(jnp.int32, shape, 1) < HEAD_DIM


def own_half(low, head, own, other):
    return jnp.where(low, own, other) if head % 2 == 0 else jnp.where(low, other, own)


def projections(normed, wt, vec, h1_ref, q_ref, k_ref, v_ref):
    width = wt.shape[1]
    first = (normed[...] * vec[GAIN1 : GAIN1 + 1] + vec[BIAS1 : BIAS1 + 1]).astype(BF16)
    h1_ref[...] = first
    got = dot(first, wt[: 3 * width], 1, 1)
    q_ref[...] = (got[:, :width] * HEAD_DIM ** (-0.5)).astype(BF16)
    k_ref[...] = got[:, width : 2 * width].astype(BF16)
    v_ref[...] = (got[:, 2 * width :] + vec[VBIAS : VBIAS + 1]).astype(BF16)


def forward_image(
    x, g, valid_row, wt, vec, table, q_ref, k_ref, v_ref, p_ref, att_ref, inv_ref,
    after_head=None,
):
    patches, width = x.shape
    heads = width // HEAD_DIM
    bias_row = jnp.where(valid_row > 0, 0.0, MASKED).astype(F32)
    fill = jnp.broadcast_to(bias_row * (1.0 / HEAD_DIM), (PAIR, patches)).T.astype(BF16)
    low = lower_half((patches, PAIR))
    one = jnp.ones((patches, PAIR), BF16)
    scores = {}

    def pair_of(ref, head):
        at = head // 2 * PAIR
        return ref[:, at : at + PAIR]

    def score(head):
        scores[head] = dot(
            own_half(low, head, pair_of(q_ref, head), one),
            own_half(low, head, pair_of(k_ref, head), fill),
            1,
            1,
        )

    sums = {}

    def product(head):
        sums[head] = dot(p_ref[head], own_half(low, head, pair_of(v_ref, head), one), 1, 0)
        if after_head is not None:
            after_head(head)
        if head % 2 == 1:
            even, odd = sums.pop(head - 1), sums.pop(head)
            inverse = 1.0 / pltpu.roll(jnp.where(low, odd, even), HEAD_DIM, 1)
            at = head // 2 * PAIR
            inv_ref[:, at : at + PAIR] = inverse.astype(inv_ref.dtype)
            att_ref[:, at : at + PAIR] = (jnp.where(low, even, odd) * inverse).astype(BF16)

    score(0)
    for head in range(heads):
        if head + 1 < heads:
            score(head + 1)
        if head > 0:
            product(head - 1)
        raw = scores.pop(head)
        p_ref[head] = jnp.exp(raw - jnp.max(raw, axis=1, keepdims=True)).astype(BF16)
    product(heads - 1)
    branch = dot(att_ref[...], wt[3 * width :], 1, 1)
    middle = x[...].astype(F32) + branch + vec[OBIAS : OBIAS + 1]
    normed, _ = normalize(middle)
    second = (normed * vec[GAIN2 : GAIN2 + 1] + vec[BIAS2 : BIAS2 + 1]).astype(BF16)
    logits = dot(table, second, 1, 1)
    masked = jnp.where(valid_row > 0, logits, MASKED)
    dispatch = jnp.exp(masked - jnp.max(masked, axis=1, keepdims=True))
    dispatch = dispatch / jnp.sum(dispatch, axis=1, keepdims=True)
    combine = jnp.exp(logits - jnp.max(logits, axis=0, keepdims=True))
    combine = combine / jnp.sum(combine, axis=0, keepdims=True)
    slots = dot(dispatch.astype(BF16), second, 1, 0)
    produced_grad = dot(combine.astype(BF16), g[...], 1, 0)
    return middle, dispatch, combine, slots, produced_grad


def backward_image(
    x, g, middle_ref, dispatch, combine, produced, slot_grad, wt, vec, table,
    q_ref, k_ref, v_ref, p_ref, att_ref, inv_ref, ds_ref, grad_t_ref, dq_ref,
    mixed_ref, grad_ref,
    before_heads=None, after_heads=None, between=(),
):
    patches, width = x.shape
    heads = width // HEAD_DIM
    dispatch_low = dispatch.astype(BF16)
    middle = middle_ref[...]
    normed, factor = normalize(middle)
    second = (normed * vec[GAIN2 : GAIN2 + 1] + vec[BIAS2 : BIAS2 + 1]).astype(BF16)
    upstream = g[...]
    other_work = list(between)

    def other():
        if other_work:
            other_work.pop(0)()

    other()
    mixed = (middle + dot(combine.astype(BF16), produced, 0, 0)).astype(BF16)
    combine_grad = dot(produced, upstream, 1, 1)
    dispatch_grad = dot(slot_grad, second, 1, 1)
    logit_grad = dispatch * (
        dispatch_grad - jnp.sum(dispatch * dispatch_grad, axis=1, keepdims=True)
    ) + combine * (combine_grad - jnp.sum(combine * combine_grad, axis=0, keepdims=True))
    logit_grad = logit_grad.astype(BF16)
    other()
    table_grad = dot(logit_grad, second, 1, 0)
    second_grad = dot(
        jnp.concatenate([dispatch_low, logit_grad], axis=0),
        jnp.concatenate([slot_grad, table], axis=0),
        0,
        0,
    )
    gain_two = jnp.sum(second_grad * normed, axis=0, keepdims=True)
    shift_two = jnp.sum(second_grad, axis=0, keepdims=True)
    middle_grad = upstream.astype(F32) + norm_back(
        second_grad * vec[GAIN2 : GAIN2 + 1], normed, factor
    )
    mixed_ref[...] = mixed
    grad_ref[...] = middle_grad
    other()
    branch_grad = middle_grad.astype(BF16)
    branch_shift = jnp.sum(branch_grad.astype(F32), axis=0, keepdims=True)
    attended_grad = dot(branch_grad, wt[3 * width :], 1, 0).astype(BF16).astype(F32)
    scaled = attended_grad * inv_ref[...].astype(F32)
    drop = (-(scaled * att_ref[...].astype(F32))).astype(BF16)
    scaled = scaled.astype(BF16)
    scaled_t = scaled.T
    query_t = q_ref[...].T
    if before_heads is not None:
        before_heads()
    low = lower_half((patches, PAIR))
    one = jnp.ones((patches, PAIR), BF16)
    prob_grads = {}

    def pair_of(ref, head):
        at = head // 2 * PAIR
        return ref[:, at : at + PAIR]

    def prob_grad(head):
        rolled = pltpu.roll(pair_of(drop, head).astype(F32), HEAD_DIM, 1).astype(BF16)
        prob_grads[head] = dot(
            own_half(low, head, pair_of(scaled, head), rolled),
            own_half(low, head, pair_of(v_ref, head), one),
            1,
            1,
        )

    query_grads = {}
    prob_grad(0)
    for head in range(heads):
        if head + 1 < heads:
            prob_grad(head + 1)
        rows = slice(head * HEAD_DIM, (head + 1) * HEAD_DIM)
        prob = p_ref[head]
        grad_t_ref[width + rows.start : width + rows.stop, :] = dot(
            scaled_t[rows], prob, 1, 0
        ).astype(BF16)
        score_grad = (prob.astype(F32) * prob_grads.pop(head)).astype(BF16)
        ds_ref[head % 2] = score_grad
        score_grad = ds_ref[head % 2]
        query_grads[head] = dot(score_grad, pair_of(k_ref, head), 1, 0)
        grad_t_ref[rows, :] = dot(query_t[rows], score_grad, 1, 0).astype(BF16)
        if head % 2 == 1:
            both = jnp.where(low, query_grads.pop(head - 1), query_grads.pop(head))
            at = head // 2 * PAIR
            dq_ref[:, at : at + PAIR] = (both * HEAD_DIM ** (-0.5)).astype(BF16)
    if after_heads is not None:
        after_heads()
    sums = jnp.concatenate(
        [jnp.zeros((3, width), F32), gain_two, branch_shift, shift_two, jnp.zeros((2, width), F32)],
        axis=0,
    )
    return sums, table_grad


def front_grads(first, grad_t_ref, dq_ref, dk_ref, dv_ref, weight_grad, sums):
    width = first.shape[1]

    def turn():
        dk_ref[...] = grad_t_ref[:width, :].T
        dv_ref[...] = grad_t_ref[width:, :].T

    def key_and_value():
        weight_grad[width : 3 * width, :] += dot(grad_t_ref[...], first[...], 1, 0)

    def query():
        weight_grad[:width, :] += dot(dq_ref[...].T, first[...], 1, 0)
        for n, ref in enumerate((dq_ref, dk_ref, dv_ref)):
            sums[n : n + 1, :] += jnp.sum(ref[...].astype(F32), axis=0, keepdims=True)

    return [turn, key_and_value, query]


def finish_image(x, middle_grad, wt, vec, dq_ref, dk_ref, dv_ref):
    width = x.shape[1]
    normed, factor = normalize(x[...].astype(F32))
    project_grad = jnp.concatenate([dq_ref[...], dk_ref[...], dv_ref[...]], axis=1)
    first_grad = dot(project_grad, wt[: 3 * width], 1, 0)
    grad = middle_grad[...] + norm_back(first_grad * vec[GAIN1 : GAIN1 + 1], normed, factor)
    return grad.astype(BF16)


def norm_sums(sums, weight_grad, wt, vec):
    width = wt.shape[1]
    high = sums.astype(BF16)
    both = jnp.concatenate([high, (sums - high.astype(F32)).astype(BF16)], axis=0)
    shift_one = jnp.zeros((1, width), F32)
    for part in range(3):
        got = dot(both, wt[part * width : (part + 1) * width], 1, 0)
        shift_one += got[part : part + 1] + got[8 + part : 9 + part]
    product = jnp.sum(weight_grad * wt[: 3 * width].astype(F32), axis=0, keepdims=True)
    gain_one = (product - vec[BIAS1 : BIAS1 + 1] * shift_one) / vec[GAIN1 : GAIN1 + 1]
    gains = jnp.concatenate([gain_one, sums[3:4]], axis=0)
    return gains, jnp.concatenate([shift_one, sums[2:3], sums[4:5], sums[5:6]], axis=0)


def forward_kernel(
    x, g, valid, wt, vec, table,
    h1, q, k, v, p, att, inv, middle, dispatch, combine, slots, produced_grad,
):
    middle[0] = normalize(x[0].astype(F32))[0]
    projections(middle.at[0], wt, vec[...], h1.at[0], q.at[0], k.at[0], v.at[0])
    got = forward_image(
        x.at[0], g.at[0], valid[0], wt, vec[...], table[...],
        q.at[0], k.at[0], v.at[0], p.at[0], att.at[0], inv.at[0],
    )
    for ref, value in zip((middle, dispatch, combine, slots, produced_grad), got):
        ref[0] = value.astype(ref.dtype)


def add_output_grad(weight_grad, middle_grad, att):
    width = weight_grad.shape[1]
    branch_grad = middle_grad.astype(BF16).reshape(-1, width)
    weight_grad[3 * width :, :] += dot(branch_grad.T, att.reshape(-1, width), 1, 0)


def backward_kernel(
    x, g, middle, dispatch, combine, produced, slot_grad, wt, vec, table,
    h1, q, k, v, p, att, inv,
    mixed, patch_grad, weight_grad, sums, table_grad,
    ds, grad_t, dq, dk, dv, middle_grad,
):
    @pl.when(pl.program_id(0) == 0)
    def _():
        weight_grad[...] = jnp.zeros_like(weight_grad)
        sums[...] = jnp.zeros_like(sums)
        table_grad[...] = jnp.zeros_like(table_grad)

    got = backward_image(
        x.at[0], g.at[0], middle.at[0], dispatch[0], combine[0], produced[0], slot_grad[0],
        wt, vec[...], table[...],
        q.at[0], k.at[0], v.at[0], p.at[0], att.at[0], inv.at[0], ds, grad_t, dq,
        mixed.at[0], middle_grad,
    )
    sums[...] += got[0]
    table_grad[...] += got[1]
    for step in front_grads(h1.at[0], grad_t, dq, dk, dv, weight_grad, sums):
        step()
    add_output_grad(weight_grad, middle_grad[...], att[0])
    patch_grad[0] = finish_image(x.at[0], middle_grad, wt, vec[...], dq, dk, dv)


def per_image(*shape):
    return pl.BlockSpec((1,) + shape, lambda i: (i,) + (0,) * len(shape))


def whole(*shape):
    return pl.BlockSpec(shape, lambda i: (0,) * len(shape))


def run_forward(x, g, valid, wt, vec, table):
    count, patches, width = x.shape
    heads = width // HEAD_DIM
    experts = table.shape[0]
    flat = (patches, width)
    outs = [
        (flat, BF16), (flat, BF16), (flat, BF16), (flat, BF16), ((heads, patches, patches), BF16),
        (flat, BF16), (flat, F32), (flat, F32),
        ((experts, patches), F32), ((experts, patches), F32),
        ((experts, width), BF16), ((experts, width), BF16),
    ]
    return pl.pallas_call(
        forward_kernel,
        grid=(count,),
        in_specs=[
            per_image(*flat), per_image(*flat), per_image(1, patches),
            whole(*wt.shape), whole(*vec.shape), whole(*table.shape),
        ],
        out_specs=[per_image(*shape) for shape, _ in outs],
        out_shape=[jax.ShapeDtypeStruct((count,) + shape, kind) for shape, kind in outs],
        compiler_params=pltpu.CompilerParams(vmem_limit_bytes=VMEM_LIMIT),
        name="forward",
    )(x, g, valid, wt, vec, table)


def run_backward(x, g, kept, produced, slot_grad, wt, vec, table):
    count, patches, width = x.shape
    heads = width // HEAD_DIM
    experts = table.shape[0]
    flat = (patches, width)
    h1, q, k, v, p, att, inv, middle, dispatch, combine = kept
    return pl.pallas_call(
        backward_kernel,
        grid=(count,),
        in_specs=[
            per_image(*flat), per_image(*flat), per_image(*flat),
            per_image(experts, patches), per_image(experts, patches),
            per_image(experts, width), per_image(experts, width),
            whole(*wt.shape), whole(*vec.shape), whole(*table.shape),
            per_image(*flat), per_image(*flat), per_image(*flat), per_image(*flat),
            per_image(heads, patches, patches), per_image(*flat), per_image(*flat),
        ],
        out_specs=[
            per_image(*flat), per_image(*flat),
            whole(4 * width, width), whole(8, width), whole(experts, width),
        ],
        out_shape=[
            jax.ShapeDtypeStruct(x.shape, BF16), jax.ShapeDtypeStruct(x.shape, BF16),
            jax.ShapeDtypeStruct((4 * width, width), F32), jax.ShapeDtypeStruct((8, width), F32),
            jax.ShapeDtypeStruct((experts, width), F32),
        ],
        scratch_shapes=[
            pltpu.VMEM((2, patches, patches), BF16),
            pltpu.VMEM((2 * width, patches), BF16),
            pltpu.VMEM(flat, BF16),
            pltpu.VMEM(flat, BF16),
            pltpu.VMEM(flat, BF16),
            pltpu.VMEM(flat, F32),
        ],
        compiler_params=pltpu.CompilerParams(vmem_limit_bytes=VMEM_LIMIT),
        name="backward",
    )(x, g, middle, dispatch, combine, produced, slot_grad, wt, vec, table, h1, q, k, v, p, att, inv)


def here():
    return lax.axis_index("wide"), lax.axis_index("narrow")


def along_z(w, z):
    return [(w, lax.rem(z + step, 4)) for step in (1, 2, 3)]


def in_plane(w, z):
    x_flip = 2 - 4 * lax.rem(w // 2, 2)
    y_flip = 4 - 8 * (w // 4)
    return [(w + x_flip, z), (w + y_flip, z), (w + x_flip + y_flip, z)]


def other_core(w, z):
    return (w + 1 - 2 * lax.rem(w, 2), z)


def greet():
    w, z = here()
    barrier = pltpu.get_barrier_semaphore()
    peers = along_z(w, z) + in_plane(w, z) + [other_core(w, z)]
    for peer in peers:
        pl.semaphore_signal(barrier, inc=1, device_id=peer, device_id_type=MESH)
    pl.semaphore_wait(barrier, len(peers))


def remote(src, dst, send, recv, peer):
    return pltpu.make_async_remote_copy(
        src_ref=src, dst_ref=dst, send_sem=send, recv_sem=recv, device_id=peer, device_id_type=MESH
    )


class Gather:
    def __init__(self, every, send, recv):
        self.every, self.send, self.recv = every, send, recv
        self.w, self.z = here()
        self.core, self.chip = lax.rem(self.w, 2), self.w // 2

    def z_copies(self):
        own = self.every.at[self.core, self.chip, self.z]
        return [
            remote(own, own, self.send.at[n], self.recv.at[n], peer)
            for n, peer in enumerate(along_z(self.w, self.z))
        ]

    def plane_copies(self):
        own = self.every.at[self.core, self.chip]
        return [
            remote(own, own, self.send.at[3 + n], self.recv.at[3 + n], peer)
            for n, peer in enumerate(in_plane(self.w, self.z))
        ]

    def core_copy(self):
        own = self.every.at[self.core]
        return remote(own, own, self.send.at[6], self.recv.at[6], other_core(self.w, self.z))

    def start_z(self):
        for copy in self.z_copies():
            copy.start()

    def start_plane(self):
        for copy in self.z_copies():
            copy.wait()
        for copy in self.plane_copies():
            copy.start()

    def start_core(self):
        for copy in self.plane_copies():
            copy.wait()
        self.core_copy().start()

    def finish(self):
        self.core_copy().wait()


class FineGather:
    def __init__(self, every, z_send, z_recv, p_send, p_recv, c_send, c_recv):
        self.every = every
        self.z_sems, self.p_sems, self.c_sems = (z_send, z_recv), (p_send, p_recv), (c_send, c_recv)
        self.w, self.z = here()
        self.plane = in_plane(self.w, self.z)

    def block(self, w, k):
        return self.every.at[lax.rem(w, 2), w // 2, lax.rem(self.z + 4 - k, 4)]

    def z_copy(self, n):
        own = self.block(self.w, 0)
        peer = along_z(self.w, self.z)[n]
        return remote(own, own, self.z_sems[0].at[n], self.z_sems[1].at[n], peer)

    def plane_copy(self, n, k):
        own = self.block(self.w, k)
        return remote(own, own, self.p_sems[0].at[n, k], self.p_sems[1].at[n, k], self.plane[n])

    def core_copy(self, group, k):
        own = self.block(self.w if group == 0 else self.plane[group - 1][0], k)
        return remote(
            own, own, self.c_sems[0].at[group, k], self.c_sems[1].at[group, k],
            other_core(self.w, self.z),
        )

    def pass_on(self, k):
        for n in range(3):
            self.plane_copy(n, k).start()
        self.core_copy(0, k).start()

    def start(self):
        for n in range(3):
            self.z_copy(n).start()
        self.pass_on(0)

    def start_plane(self):
        for n in range(3):
            self.z_copy(n).wait()
            self.pass_on(n + 1)

    def start_core(self):
        for k in range(4):
            for n in range(3):
                self.plane_copy(n, k).wait()
                self.core_copy(n + 1, k).start()

    def finish(self):
        for group in range(4):
            for k in range(4):
                self.core_copy(group, k).wait()


class Scatter:
    def __init__(self, parts, from_core, chips, from_plane, column, from_z, send, recv):
        self.parts, self.from_core, self.chips = parts, from_core, chips
        self.from_plane, self.column, self.from_z = from_plane, column, from_z
        self.send, self.recv = send, recv
        self.w, self.z = here()
        self.core = lax.rem(self.w, 2)

    def core_copy(self):
        return remote(
            self.parts.at[1 - self.core], self.from_core, self.send.at[0], self.recv.at[0],
            other_core(self.w, self.z),
        )

    def plane_copies(self):
        return [
            remote(
                self.chips.at[peer[0] // 2], self.from_plane.at[n],
                self.send.at[1 + n], self.recv.at[1 + n], peer,
            )
            for n, peer in enumerate(in_plane(self.w, self.z))
        ]

    def z_copies(self):
        return [
            remote(
                self.column.at[peer[1]], self.from_z.at[n],
                self.send.at[4 + n], self.recv.at[4 + n], peer,
            )
            for n, peer in enumerate(along_z(self.w, self.z))
        ]

    def start_core(self):
        self.core_copy().start()

    def start_plane(self):
        self.core_copy().wait()
        total = self.parts[self.core].astype(F32) + self.from_core[...].astype(F32)
        self.chips[...] = total.astype(BF16)
        for copy in self.plane_copies():
            copy.start()

    def start_z(self):
        for copy in self.plane_copies():
            copy.wait()
        total = self.chips[self.w // 2].astype(F32)
        for n in range(3):
            total = total + self.from_plane[n].astype(F32)
        self.column[...] = total.astype(BF16)
        for copy in self.z_copies():
            copy.start()

    def finish(self):
        for copy in self.z_copies():
            copy.wait()

    def total(self):
        total = self.column[self.z].astype(F32)
        for n in range(3):
            total = total + self.from_z[n].astype(F32)
        return total


class FineScatter:
    def __init__(
        self, parts, from_core, chips, from_plane, column, from_z,
        c_send, c_recv, p_send, p_recv, z_send, z_recv,
    ):
        self.parts, self.from_core, self.chips = parts, from_core, chips
        self.from_plane, self.column, self.from_z = from_plane, column, from_z
        self.c_sems, self.p_sems, self.z_sems = (c_send, c_recv), (p_send, p_recv), (z_send, z_recv)
        self.w, self.z = here()
        self.core = lax.rem(self.w, 2)
        self.plane = in_plane(self.w, self.z)

    def goal(self, k):
        return lax.rem(self.z + k, 4)

    def core_copy(self, chip):
        return remote(
            self.parts.at[1 - self.core, chip], self.from_core.at[chip],
            self.c_sems[0].at[chip], self.c_sems[1].at[chip], other_core(self.w, self.z),
        )

    def plane_copy(self, n, k):
        z = self.goal(k)
        return remote(
            self.chips.at[self.plane[n][0] // 2, z], self.from_plane.at[n, z],
            self.p_sems[0].at[n, k], self.p_sems[1].at[n, k], self.plane[n],
        )

    def z_copy(self, k):
        return remote(
            self.column.at[self.goal(k)], self.from_z.at[k - 1],
            self.z_sems[0].at[k - 1], self.z_sems[1].at[k - 1], (self.w, self.goal(k)),
        )

    def start_core(self, chip):
        self.core_copy(chip).start()

    def start_plane(self, chip):
        self.core_copy(chip).wait()
        own = self.parts[self.core, chip].astype(F32)
        self.chips[chip] = (own + self.from_core[chip].astype(F32)).astype(BF16)
        for n, peer in enumerate(self.plane):

            @pl.when(peer[0] // 2 == chip)
            def _(n=n):
                for k in (1, 2, 3, 0):
                    self.plane_copy(n, k).start()

    def plane_sum(self, k):
        z = self.goal(k)
        total = self.chips[self.w // 2, z].astype(F32)
        for n in range(3):
            self.plane_copy(n, k).wait()
            total = total + self.from_plane[n, z].astype(F32)
        return total

    def start_z(self, k):
        self.column[self.goal(k)] = self.plane_sum(k).astype(BF16)
        self.z_copy(k).start()

    def total(self):
        total = self.plane_sum(0)
        for k in (1, 2, 3):
            self.z_copy(k).wait()
            total = total + self.from_z[k - 1].astype(F32)
        return total


def by_device(blocks):
    return jnp.concatenate([blocks[core, chip] for chip in range(4) for core in range(2)], axis=0)


def fill_blocks(blocks, values):
    for chip in range(4):
        for core in range(2):
            at = (2 * chip + core) * 4
            blocks[core, chip] = values[at : at + 4].astype(blocks.dtype)


def gather_scratch(rows, width):
    dma = pltpu.SemaphoreType.DMA
    return [pltpu.VMEM((2, 4, 4, rows, width), BF16), dma((7,)), dma((7,))]


def fine_scratch(rows, width):
    dma = pltpu.SemaphoreType.DMA
    return [
        pltpu.VMEM((2, 4, 4, rows, width), BF16),
        dma((3,)), dma((3,)), dma((3, 4)), dma((3, 4)), dma((4, 4)), dma((4, 4)),
    ]


def scatter_scratch(rows, width):
    return [
        pltpu.VMEM((2, 4, 4, rows, width), BF16),
        pltpu.VMEM((4, 4, rows, width), BF16),
        pltpu.VMEM((4, 4, rows, width), BF16),
        pltpu.VMEM((3, 4, rows, width), BF16),
        pltpu.VMEM((4, rows, width), BF16),
        pltpu.VMEM((3, rows, width), BF16),
        pltpu.SemaphoreType.DMA((7,)),
        pltpu.SemaphoreType.DMA((7,)),
    ]


def expert_rows(slots, grads, w_in, bias, w_out):
    rows, width = slots.shape
    units = w_in.shape[0]
    shape = (rows, units)
    own = lax.rem(lax.broadcasted_iota(jnp.int32, shape, 0), 8)
    start = own * (units // 8)
    lane = lax.broadcasted_iota(jnp.int32, shape, 1)
    keep = (lane >= start) & (lane < start + units // 8)
    hidden = dot(slots, w_in, 1, 1) + bias
    active_grad = dot(grads, w_out, 1, 1)
    half = 0.5 * (1.0 + lax.erf(hidden * 0.7071067811865476))
    active = jnp.where(keep, hidden * half, 0.0).astype(BF16)
    slope = half + hidden * jnp.exp(hidden * hidden * -0.5) * 0.3989422804014327
    hidden_grad = jnp.where(keep, active_grad * slope, 0.0).astype(BF16)
    produced = dot(active, w_out, 1, 0)
    slot_grad = dot(hidden_grad, w_in, 1, 0)
    return produced, slot_grad, active, hidden_grad


def one_hot(length, width):
    row = lax.broadcasted_iota(jnp.int32, (128, width), 0)
    column = lax.broadcasted_iota(jnp.int32, (128, width), 1)
    return (row == lax.rem(column, length)).astype(BF16)


def own_piece(shape, length):
    device = lax.broadcasted_iota(jnp.int32, shape, 0)
    column = lax.broadcasted_iota(jnp.int32, shape, 1)
    return lax.rem(device, shape[1] // length) == column // length


def spread(pieces, length, width):
    devices = pieces.shape[0]
    tall = dot(pieces.astype(BF16), one_hot(length, width), 1, 0)
    tall = jnp.where(own_piece(tall.shape, length), tall, 0.0).astype(BF16)
    row = lax.broadcasted_iota(jnp.int32, (8, devices), 0)
    device = lax.broadcasted_iota(jnp.int32, (8, devices), 1)
    return dot((device // (width // length) == row).astype(BF16), tall, 1, 0)


def pieces_of(rows, length, devices):
    count, width = rows.shape
    per_row = width // length
    tall = jnp.broadcast_to(rows[:, None], (count, per_row, width)).reshape(devices, width)
    tall = jnp.where(own_piece(tall.shape, length), tall, 0.0)
    return dot(tall.astype(BF16), one_hot(length, width), 1, 1)


def layer_kernel(
    lengths,
    x_hbm, g_hbm, valid, own_weights, own_gains, own_biases, own_table, own_shift, w_in, own_bias, w_out,
    g, x, p_hbm, weight_out, vectors_out, in_grad, out_grad, bias_grad,
    h1, q, k, v, att, inv, middle, dispatch, combine, p, ds, grad_t, wt, vec, table, shift, bias,
    weight_grad, sums, table_grad, shift_grad, own_pieces,
    active, hidden_grad,
    x_sem, g_sem, p_out_sem, p_in_sem,
    every, g_send, g_recv,
    parts, from_core, chips, from_plane, column, from_z, s_send, s_recv,
    *rest,
):
    count, patches, width = x.shape
    heads = width // HEAD_DIM
    rows = own_weights.shape[0]
    wide, narrow = here()
    me = (lax.rem(wide, 2), wide // 2, narrow)
    (w_every, *w_sems), (v_every, *v_sems) = rest[:7], rest[7:10]
    w_last, v_last = rest[10:22], rest[22:30]

    for i in range(count):
        pltpu.make_async_copy(x_hbm.at[i], x.at[i], x_sem.at[i]).start()
        pltpu.make_async_copy(g_hbm.at[i], g.at[i], g_sem.at[i]).start()
    w_every[me] = own_weights[...]
    own_pieces[...] = jnp.zeros_like(own_pieces)
    for n, ref in enumerate((own_gains, own_biases, own_table, own_shift)):
        own_pieces[n : n + 1, : lengths[n]] = ref[...].astype(F32).reshape(1, lengths[n])
    v_every[me] = own_pieces[...].astype(BF16)
    greet()
    weights = FineGather(w_every, *w_sems)
    vectors = Gather(v_every, *v_sems)
    vectors.start_z()
    weights.start()
    for ref in (weight_grad, sums, table_grad, shift_grad, in_grad, out_grad, bias_grad):
        ref[...] = jnp.zeros_like(ref)
    units = w_in.shape[0] // 8
    spread_bias = dot(own_bias[...], one_hot(units, 8 * units)[:units], 1, 0)
    at = lax.broadcasted_iota(jnp.int32, spread_bias.shape, 0)
    lane = lax.broadcasted_iota(jnp.int32, spread_bias.shape, 1)
    bias[...] = jnp.sum(jnp.where(lane // units == at, spread_bias, 0.0), axis=0, keepdims=True)
    def arrive(hbm, ref, sem, i):
        pltpu.make_async_copy(hbm.at[i], ref.at[i], sem.at[i]).wait()

    def first_norm(i, carry):
        arrive(x_hbm, x, x_sem, i)
        middle[i] = normalize(x[i].astype(F32))[0]
        return carry

    lax.fori_loop(0, count, first_norm, 0)
    vectors.start_plane()
    weights.start_plane()
    vectors.start_core()
    weights.start_core()
    vectors.finish()
    packed = by_device(v_every).astype(F32)
    gains, biases, slot_rows, shift_rows = (
        spread(packed[:, n], length, width) for n, length in enumerate(lengths)
    )
    vec[...] = jnp.concatenate([gains[:2], biases[:4], jnp.zeros((2, width), F32)], axis=0)
    table[...] = slot_rows
    shift[...] = shift_rows
    weights.finish()
    wt[...] = by_device(w_every).reshape(4 * width, width)

    def slots_way(i):
        return Gather(every.at[i], g_send.at[i], g_recv.at[i])

    def results_way(i):
        ring = lax.rem(i, 2)
        return Scatter(
            parts.at[ring], from_core.at[ring], chips.at[ring], from_plane.at[i], column.at[i],
            from_z.at[i], s_send.at[i], s_recv.at[i],
        )

    def for_image(i, action):
        @pl.when((i >= 0) & (i < count))
        def _():
            action(i)

    def arrived_rows(i):
        both = every[i].astype(F32).reshape(32, 2, 8, width)
        return [both[:, n].reshape(32 * 8, width).astype(BF16) for n in range(2)]

    def experts(i):
        slots_way(i).finish()
        got = expert_rows(*arrived_rows(i), w_in[...], bias[...], w_out[...])
        back = jnp.stack([got[0].reshape(32, 8, width), got[1].reshape(32, 8, width)], axis=1)
        parts[lax.rem(i, 2)] = back.reshape(2, 4, 4, 16, width).astype(BF16)
        active[i], hidden_grad[i] = got[2:]
        results_way(i).start_core()

    def middle_of(step):
        for_image(step - 3, experts)

    def end_of(step):
        for_image(step - 4, lambda i: results_way(i).start_z())
        for_image(step - 3, lambda i: results_way(i).start_plane())
        for_image(step - 2, lambda i: slots_way(i).start_core())
        for_image(step - 1, lambda i: slots_way(i).start_plane())

    def p_out(i, head):
        return pltpu.make_async_copy(p.at[head], p_hbm.at[i, head], p_out_sem.at[head])

    def p_in(i, head):
        return pltpu.make_async_copy(p_hbm.at[i, head], p.at[head], p_in_sem.at[head])

    def forward(i, carry):
        projections(middle.at[i], wt, vec[...], h1.at[i], q.at[i], k.at[i], v.at[i])
        arrive(g_hbm, g, g_sem, i)
        middle_of(i)

        @pl.when(i > 0)
        def _():
            for head in range(heads):
                p_out(i - 1, head).wait()

        got = forward_image(
            x.at[i], g.at[i], valid[pl.ds(i, 1)], wt, vec[...], table[...].astype(BF16),
            q.at[i], k.at[i], v.at[i], p, att.at[i], inv.at[i], lambda head: p_out(i, head).start(),
        )
        middle[i], dispatch[i], combine[i] = got[:3]
        shift_grad[...] += got[4].astype(BF16).astype(F32)
        every[(i,) + me] = jnp.concatenate([got[3], got[4]], axis=0).astype(BF16)
        end_of(i)
        slots_way(i).start_z()
        return carry

    lax.fori_loop(0, count, forward, 0)
    q[count] = jnp.zeros_like(q[count])
    h1[count] = jnp.zeros_like(h1[count])
    grad_t[...] = jnp.zeros_like(grad_t)
    for head in range(heads):
        p_out(count - 1, head).wait()
        p_in(0, head).start()

    def front(i):
        place = lax.rem(i + count + 1, count + 1)
        return front_grads(
            h1.at[place], grad_t, q.at[place], k.at[place], v.at[place], weight_grad, sums
        )

    def backward(i, carry):
        def before_heads():
            middle_of(count + i)
            for head in range(heads):
                p_in(i, head).wait()

        def after_heads():
            @pl.when(i + 1 < count)
            def _():
                for head in range(heads):
                    p_in(i + 1, head).start()

        results_way(i).finish()
        total = results_way(i).total()
        got = backward_image(
            x.at[i], g.at[i], middle.at[i], dispatch[i], combine[i],
            (total[:8] + shift[...]).astype(BF16), total[8:].astype(BF16),
            wt, vec[...], table[...].astype(BF16),
            q.at[i], k.at[i], v.at[i], p, att.at[i], inv.at[i], ds, grad_t,
            q.at[i], g.at[i], middle.at[i], before_heads, after_heads, front(i - 1),
        )
        sums[...] += got[0]
        table_grad[...] += got[1]
        end_of(count + i)
        return carry

    lax.fori_loop(0, count, backward, 0)
    for step in front(count - 1):
        step()

    weights = FineScatter(*w_last)

    def depart(chip):
        for core in range(2):
            block = weight_grad[pl.ds((2 * chip + core) * 4 * rows, 4 * rows), :]
            w_last[0][core, chip] = block.reshape(4, rows, width).astype(BF16)
        weights.start_core(chip)

    for chip in range(3):
        depart(chip)
    for i in range(0, count, 2):
        add_output_grad(weight_grad, middle[i : i + 2], att[i : i + 2])
        if i == 0:
            for chip in range(3):
                weights.start_plane(chip)
    depart(3)
    gains, biases = norm_sums(sums[...], weight_grad[: 3 * width, :], wt, vec[...])
    pieces = [
        pieces_of(value, length, 32)
        for value, length in zip((gains, biases, table_grad[...], shift_grad[...]), lengths)
    ]
    pieces.append(jnp.zeros((32, 128), F32))
    pieces = jnp.stack([pieces[min(n, 4)] for n in range(16)], axis=1)
    fill_blocks(v_last[0], pieces)
    vectors = Scatter(*v_last)
    vectors.start_core()
    weights.start_plane(3)
    vectors.start_plane()

    def finish(i, carry):
        x[i] = finish_image(x.at[i], middle.at[i], wt, vec[...], q.at[i], k.at[i], v.at[i])
        all_slots, all_grads = arrived_rows(i)
        in_grad[...] += dot(hidden_grad[i], all_slots, 0, 0)
        out_grad[...] += dot(active[i], all_grads, 0, 0)
        bias_grad[...] += jnp.sum(hidden_grad[i].astype(F32).reshape(32, 8, -1), axis=0)

        for block in (1, 2, 3):

            @pl.when(i == block)
            def _(block=block):
                weights.start_z(block)

        @pl.when(i == 3)
        def _():
            vectors.start_z()

        return carry

    lax.fori_loop(0, count, finish, 0)
    weight_out[...] = weights.total()
    vectors.finish()
    vectors_out[...] = vectors.total()


def hand_over_kernel(
    mixed, patch_grad, weight_grad, in_grad, out_grad, vectors, bias_grad,
    mixed_out, patch_grad_out, weight_out, in_out, out_out, gains, biases, table, shift, bias_out, sems,
):
    moves = (
        (mixed, mixed_out), (patch_grad, patch_grad_out), (weight_grad, weight_out),
        (in_grad, in_out), (out_grad, out_out),
    )
    copies = [pltpu.make_async_copy(src, dst, sems.at[n]) for n, (src, dst) in enumerate(moves)]
    for copy in copies:
        copy.start()
    for n, ref in enumerate((gains, biases, table, shift)):
        ref[...] = vectors[n : n + 1, : ref.shape[0]].reshape(ref.shape[0])
    experts, units = bias_out.shape
    for e in range(experts):
        bias_out[e : e + 1, :] = bias_grad[e : e + 1, e * units : (e + 1) * units]
    for copy in copies:
        copy.wait()


def run_layer(patches, valid, attn_weights, vectors, expert_in, expert_in_bias, expert_out, out_grad):
    count, length, width = patches.shape
    heads = width // HEAD_DIM
    experts, _, units = expert_in.shape
    rows = attn_weights.shape[1]
    lengths = [v.shape[0] for v in vectors]
    flat = (length, width)
    dma = pltpu.SemaphoreType.DMA
    vmem = pltpu.VMEM
    anywhere = pl.BlockSpec(memory_space=pl.ANY)
    here_all = pl.BlockSpec(memory_space=pltpu.VMEM)
    mixed, patch_grad, _, weight_grad, vector_grads, in_grad, out_grads, bias_grad = pl.pallas_call(
        functools.partial(layer_kernel, lengths),
        in_specs=[anywhere] * 2 + [here_all] * 9,
        out_specs=[here_all] * 2 + [anywhere] + [here_all] * 5,
        out_shape=[
            vmem(patches.shape, BF16), vmem(patches.shape, BF16),
            jax.ShapeDtypeStruct((count, heads, length, length), BF16),
            vmem((rows, width), F32), vmem((16, 128), F32),
            vmem((experts * units, width), F32), vmem((experts * units, width), F32),
            vmem((experts, experts * units), F32),
        ],
        scratch_shapes=[
            vmem((count + 1,) + flat, BF16), vmem((count + 1,) + flat, BF16),
            vmem((count + 1,) + flat, BF16), vmem((count + 1,) + flat, BF16),
            vmem((count,) + flat, BF16), vmem((count,) + flat, BF16), vmem((count,) + flat, F32),
            vmem((count, experts, length), F32), vmem((count, experts, length), F32),
            vmem((heads, length, length), BF16), vmem((2, length, length), BF16),
            vmem((2 * width, length), BF16), vmem((4 * width, width), BF16),
            vmem((8, width), F32), vmem((experts, width), F32), vmem((experts, width), F32),
            vmem((1, experts * units), F32),
            vmem((4 * width, width), F32), vmem((8, width), F32), vmem((experts, width), F32),
            vmem((experts, width), F32), vmem((16, 128), F32),
            vmem((count, 32 * experts, experts * units), BF16),
            vmem((count, 32 * experts, experts * units), BF16),
            dma((count,)), dma((count,)), dma((heads,)), dma((heads,)),
        ]
        + [vmem((count, 2, 4, 4, 16, width), BF16), dma((count, 7)), dma((count, 7))]
        + [
            vmem((2, 2, 4, 4, 16, width), BF16), vmem((2, 4, 4, 16, width), BF16),
            vmem((2, 4, 4, 16, width), BF16), vmem((count, 3, 4, 16, width), BF16),
            vmem((count, 4, 16, width), BF16), vmem((count, 3, 16, width), BF16),
            dma((count, 7)), dma((count, 7)),
        ]
        + fine_scratch(rows, width) + gather_scratch(16, 128)
        + scatter_scratch(rows, width)[:6]
        + [dma((4,)), dma((4,)), dma((3, 4)), dma((3, 4)), dma((3,)), dma((3,))]
        + scatter_scratch(16, 128),
        compiler_params=pltpu.CompilerParams(
            collective_id=0, has_side_effects=True, vmem_limit_bytes=LAYER_LIMIT
        ),
        name="layer",
    )(
        patches, out_grad, valid, attn_weights.T, *vectors,
        expert_in.transpose(0, 2, 1).reshape(experts * units, width), expert_in_bias,
        expert_out.reshape(experts * units, width),
    )
    results = pl.pallas_call(
        hand_over_kernel,
        in_specs=[here_all] * 7,
        out_specs=[anywhere] * 5 + [here_all] * 5,
        out_shape=[
            jax.ShapeDtypeStruct(value.shape, value.dtype)
            for value in (mixed, patch_grad, weight_grad, in_grad, out_grads)
        ]
        + [jax.ShapeDtypeStruct((piece,), F32) for piece in lengths]
        + [jax.ShapeDtypeStruct((experts, units), F32)],
        scratch_shapes=[dma((5,))],
        compiler_params=pltpu.CompilerParams(vmem_limit_bytes=8 * 1024 * 1024),
        name="hand_over",
    )(mixed, patch_grad, weight_grad, in_grad, out_grads, vector_grads, bias_grad)
    mixed, patch_grad, weight_grad, in_grad, out_grads, gains, biases, table, shift, bias_grad = results
    return (
        mixed,
        patch_grad,
        weight_grad.T,
        gains,
        biases,
        table,
        in_grad.reshape(experts, units, width).transpose(0, 2, 1),
        bias_grad,
        out_grads.reshape(experts, units, width),
        shift,
    )


def scatter_sum(parts):
    got = lax.all_to_all(parts.astype(BF16), AXES, 0, 0, tiled=True)
    return jnp.sum(got.astype(F32), axis=0)


def experts_at_home(slots, produced_grad, expert_in, expert_in_bias, expert_out, devices):
    local_images, experts, width = slots.shape
    every = lax.all_gather(jnp.stack([slots, produced_grad]), AXES, axis=1, tiled=True)
    all_slots, all_grads = every[0], every[1]
    hidden = jnp.einsum(
        "bed,edf->bef", all_slots, expert_in, preferred_element_type=F32
    ) + expert_in_bias.astype(F32)
    active, gelu_back = jax.vjp(smooth, hidden)
    active = active.astype(BF16)
    partial = jnp.einsum("bef,efd->bed", active, expert_out, preferred_element_type=F32)
    active_grad = jnp.einsum("bed,efd->bef", all_grads, expert_out, preferred_element_type=F32)
    hidden_grad = gelu_back(active_grad)[0].astype(BF16)
    partial_back = jnp.einsum("bef,edf->bed", hidden_grad, expert_in, preferred_element_type=F32)
    contract_grad = jnp.einsum("bef,bed->efd", active, all_grads, preferred_element_type=F32)
    expand_grad = jnp.einsum("bed,bef->edf", all_slots, hidden_grad, preferred_element_type=F32)
    inner_grad = jnp.sum(hidden_grad.astype(F32), axis=0)
    both = jnp.stack([partial, partial_back]).reshape(2, devices, local_images, experts, width)
    both = scatter_sum(jnp.moveaxis(both, 1, 0))
    return (both[0], both[1], expand_grad, inner_grad, contract_grad)


def on_device(
    patches,
    valid,
    attn_weights,
    norm_gains,
    vec_biases,
    slot_params,
    expert_in,
    expert_in_bias,
    expert_out,
    expert_out_bias,
    out_grad,
):
    local_images, patch_count, width = patches.shape
    experts = expert_in.shape[0]
    devices = lax.axis_size("wide") * lax.axis_size("narrow")

    vectors = (norm_gains, vec_biases, slot_params, expert_out_bias)
    lengths = [v.shape[0] for v in vectors]
    if lax.axis_size("wide") == 8 and lax.axis_size("narrow") == 4:
        return run_layer(
            patches, valid, attn_weights, vectors, expert_in, expert_in_bias, expert_out, out_grad
        )
    wt = lax.all_gather(attn_weights.T, AXES, axis=0, tiled=True)
    small = lax.all_gather(jnp.concatenate(vectors), AXES)
    pieces = []
    at = 0
    for length in lengths:
        pieces.append(small[:, at : at + length].reshape(-1, width))
        at += length
    gains, biases, table, expert_shift = pieces
    vec = jnp.concatenate([gains, biases, jnp.zeros((2, width), BF16)]).astype(F32)

    *kept, slots, produced_grad = run_forward(
        patches, out_grad, valid.reshape(local_images, 1, patch_count), wt, vec, table
    )
    produced, slot_grad, expand_grad, inner_grad, contract_grad = experts_at_home(
        slots, produced_grad, expert_in, expert_in_bias, expert_out, devices
    )
    produced = (produced + expert_shift.astype(F32)).astype(BF16)
    slot_grad = slot_grad.astype(BF16)
    shift_grad = jnp.sum(produced_grad.astype(F32), axis=0)
    mixed_out, patch_grad, weight_grad, rows, table_grad = run_backward(
        patches, out_grad, kept, produced, slot_grad, wt, vec, table
    )
    weight_front = weight_grad[: 3 * width]
    weight_grad = weight_grad.reshape(devices, -1, width)
    gain_grads, bias_grads = norm_sums(rows, weight_front, wt, vec)
    small_grads = jnp.concatenate(
        [v.reshape(devices, -1) for v in (gain_grads, bias_grads, table_grad, shift_grad)], axis=1
    )
    weight_grad = scatter_sum(weight_grad).T
    small_grads = jnp.sum(lax.all_to_all(small_grads, AXES, 0, 0, tiled=True), axis=0)
    grads = []
    at = 0
    for length in lengths:
        grads.append(small_grads[at : at + length])
        at += length
    return (
        mixed_out,
        patch_grad,
        weight_grad,
        grads[0],
        grads[1],
        grads[2],
        expand_grad,
        inner_grad,
        contract_grad,
        grads[3],
    )


def solution(mesh):
    images = P(AXES, None, None)
    vector = P(AXES)
    second = P(None, AXES)
    return jax.shard_map(
        on_device,
        mesh=mesh,
        in_specs=(
            images, P(AXES, None), second, vector, vector, vector,
            P(None, None, AXES), second, P(None, AXES, None), vector, images,
        ),
        out_specs=(
            images, images, second, vector, vector, vector,
            P(None, None, AXES), second, P(None, AXES, None), vector,
        ),
        check_vma=False,
    )
```

```python
import functools

import jax
import jax.numpy as jnp
from jax import lax
from jax.experimental import pallas as pl
from jax.experimental.pallas import tpu as pltpu
from jax.sharding import PartitionSpec as P

HEAD_DIM = 64
PAIR = 2 * HEAD_DIM
MASKED = -1000000000.0
AXES = ("wide", "narrow")
BF16 = jnp.bfloat16
F32 = jnp.float32
MESH = pl.DeviceIdType.MESH
VMEM_LIMIT = 60 * 1024 * 1024
LAYER_LIMIT = 56 * 1024 * 1024
GAIN1, GAIN2, BIAS1, VBIAS, OBIAS, BIAS2 = range(6)


def dot(left, right, left_dim, right_dim):
    return lax.dot_general(
        left, right, (((left_dim,), (right_dim,)), ((), ())), preferred_element_type=F32
    )


def normalize(values):
    centred = values - jnp.mean(values, axis=-1, keepdims=True)
    factor = lax.rsqrt(jnp.mean(centred * centred, axis=-1, keepdims=True) + 1e-06)
    return (centred * factor, factor)


def norm_back(grad_hat, normed, factor):
    return factor * (
        grad_hat
        - jnp.mean(grad_hat, axis=-1, keepdims=True)
        - normed * jnp.mean(grad_hat * normed, axis=-1, keepdims=True)
    )


def smooth(values):
    return jax.nn.gelu(values, approximate=False)


def lower_half(shape):
    return lax.broadcasted_iota(jnp.int32, shape, 1) < HEAD_DIM


def own_half(low, head, own, other):
    return jnp.where(low, own, other) if head % 2 == 0 else jnp.where(low, other, own)


def own_rows(head, rows, other):
    own = rows[head * HEAD_DIM : (head + 1) * HEAD_DIM]
    return jnp.concatenate([own, other] if head % 2 == 0 else [other, own], axis=0)


def projections(normed, wt, vec, h1_ref, q_ref, k_ref, v_ref):
    width = wt.shape[1]
    first = (normed[...] * vec[GAIN1 : GAIN1 + 1] + vec[BIAS1 : BIAS1 + 1]).astype(BF16)
    h1_ref[...] = first
    got = dot(first, wt[: 3 * width], 1, 1)
    q_ref[...] = (got[:, :width] * HEAD_DIM ** (-0.5)).astype(BF16)
    k_ref[...] = got[:, width : 2 * width].astype(BF16)
    v_ref[...] = (got[:, 2 * width :] + vec[VBIAS : VBIAS + 1]).astype(BF16)


def forward_image(
    x, g, valid_row, wt, vec, table, q_ref, k_ref, v_ref, p_ref, att_ref, inv_ref,
    after_head=None, after_heads=None,
):
    patches, width = x.shape
    heads = width // HEAD_DIM
    bias_row = jnp.where(valid_row > 0, 0.0, MASKED).astype(F32)
    fill = jnp.broadcast_to(bias_row * (1.0 / HEAD_DIM), (HEAD_DIM, patches)).astype(BF16)
    key_t = k_ref[...].T
    low = lower_half((patches, PAIR))
    one = jnp.ones((patches, PAIR), BF16)
    scores = {}

    def pair_of(ref, head):
        at = head // 2 * PAIR
        return ref[:, at : at + PAIR]

    def score(head):
        scores[head] = dot(
            own_half(low, head, pair_of(q_ref, head), one),
            own_rows(head, key_t, fill),
            1,
            0,
        )

    sums = {}

    def product(head):
        sums[head] = dot(p_ref[head], own_half(low, head, pair_of(v_ref, head), one), 1, 0)
        if after_head is not None:
            after_head(head)
        if head % 2 == 1:
            even, odd = sums.pop(head - 1), sums.pop(head)
            inverse = 1.0 / pltpu.roll(jnp.where(low, odd, even), HEAD_DIM, 1)
            at = head // 2 * PAIR
            inv_ref[:, at : at + PAIR] = inverse.astype(inv_ref.dtype)
            att_ref[:, at : at + PAIR] = (jnp.where(low, even, odd) * inverse).astype(BF16)

    score(0)
    for head in range(heads):
        if head + 1 < heads:
            score(head + 1)
        if head > 0:
            product(head - 1)
        raw = scores.pop(head)
        p_ref[head] = jnp.exp(raw - jnp.max(raw, axis=1, keepdims=True)).astype(BF16)
    product(heads - 1)
    if after_heads is not None:
        after_heads()
    branch = dot(att_ref[...], wt[3 * width :], 1, 1)
    middle = x[...].astype(F32) + branch + vec[OBIAS : OBIAS + 1]
    normed, _ = normalize(middle)
    second = (normed * vec[GAIN2 : GAIN2 + 1] + vec[BIAS2 : BIAS2 + 1]).astype(BF16)
    logits = dot(table, second, 1, 1)
    masked = jnp.where(valid_row > 0, logits, MASKED)
    dispatch = jnp.exp(masked - jnp.max(masked, axis=1, keepdims=True))
    dispatch = dispatch / jnp.sum(dispatch, axis=1, keepdims=True)
    combine = jnp.exp(logits - jnp.max(logits, axis=0, keepdims=True))
    combine = combine / jnp.sum(combine, axis=0, keepdims=True)
    slots = dot(dispatch.astype(BF16), second, 1, 0)
    produced_grad = dot(combine.astype(BF16), g[...], 1, 0)
    return middle, dispatch, combine, slots, produced_grad


def backward_image(
    x, g, middle_ref, dispatch, combine, produced, slot_grad, wt, vec, table,
    q_ref, k_ref, v_ref, p_ref, att_ref, inv_ref, ds_ref, grad_t_ref, dq_ref,
    mixed_ref, grad_ref,
    before_heads=None, after_heads=None, between=(),
):
    patches, width = x.shape
    heads = width // HEAD_DIM
    dispatch_low = dispatch.astype(BF16)
    middle = middle_ref[...]
    normed, factor = normalize(middle)
    second = (normed * vec[GAIN2 : GAIN2 + 1] + vec[BIAS2 : BIAS2 + 1]).astype(BF16)
    upstream = g[...]
    other_work = list(between)

    def other():
        if other_work:
            other_work.pop(0)()

    other()
    mixed = (middle + dot(combine.astype(BF16), produced, 0, 0)).astype(BF16)
    combine_grad = dot(produced, upstream, 1, 1)
    dispatch_grad = dot(slot_grad, second, 1, 1)
    logit_grad = dispatch * (
        dispatch_grad - jnp.sum(dispatch * dispatch_grad, axis=1, keepdims=True)
    ) + combine * (combine_grad - jnp.sum(combine * combine_grad, axis=0, keepdims=True))
    logit_grad = logit_grad.astype(BF16)
    other()
    table_grad = dot(logit_grad, second, 1, 0)
    second_grad = dot(
        jnp.concatenate([dispatch_low, logit_grad], axis=0),
        jnp.concatenate([slot_grad, table], axis=0),
        0,
        0,
    )
    gain_two = jnp.sum(second_grad * normed, axis=0, keepdims=True)
    shift_two = jnp.sum(second_grad, axis=0, keepdims=True)
    middle_grad = upstream.astype(F32) + norm_back(
        second_grad * vec[GAIN2 : GAIN2 + 1], normed, factor
    )
    mixed_ref[...] = mixed
    grad_ref[...] = middle_grad
    other()
    branch_grad = middle_grad.astype(BF16)
    branch_shift = jnp.sum(branch_grad.astype(F32), axis=0, keepdims=True)
    attended_grad = dot(branch_grad, wt[3 * width :], 1, 0).astype(BF16).astype(F32)
    scaled = attended_grad * inv_ref[...].astype(F32)
    drop = (-(scaled * att_ref[...].astype(F32))).astype(BF16)
    scaled = scaled.astype(BF16)
    scaled_t = scaled.T
    query_t = q_ref[...].T
    value_t = v_ref[...].T
    one_t = jnp.ones((HEAD_DIM, patches), BF16)
    if before_heads is not None:
        before_heads()
    low = lower_half((patches, PAIR))
    one = jnp.ones((patches, PAIR), BF16)
    prob_grads = {}

    def pair_of(ref, head):
        at = head // 2 * PAIR
        return ref[:, at : at + PAIR]

    def prob_grad(head):
        rolled = pltpu.roll(pair_of(drop, head).astype(F32), HEAD_DIM, 1).astype(BF16)
        prob_grads[head] = dot(
            own_half(low, head, pair_of(scaled, head), rolled),
            own_rows(head, value_t, one_t),
            1,
            0,
        )

    query_grads = {}
    prob_grad(0)
    for head in range(heads):
        if head + 1 < heads:
            prob_grad(head + 1)
        rows = slice(head * HEAD_DIM, (head + 1) * HEAD_DIM)
        prob = p_ref[head]
        grad_t_ref[width + rows.start : width + rows.stop, :] = dot(
            scaled_t[rows], prob, 1, 0
        ).astype(BF16)
        score_grad = (prob.astype(F32) * prob_grads.pop(head)).astype(BF16)
        ds_ref[head % 2] = score_grad
        score_grad = ds_ref[head % 2]
        query_grads[head] = dot(score_grad, pair_of(k_ref, head), 1, 0)
        grad_t_ref[rows, :] = dot(query_t[rows], score_grad, 1, 0).astype(BF16)
        if head % 2 == 1:
            both = jnp.where(low, query_grads.pop(head - 1), query_grads.pop(head))
            at = head // 2 * PAIR
            dq_ref[:, at : at + PAIR] = (both * HEAD_DIM ** (-0.5)).astype(BF16)
    if after_heads is not None:
        after_heads()
    sums = jnp.concatenate(
        [jnp.zeros((3, width), F32), gain_two, branch_shift, shift_two, jnp.zeros((2, width), F32)],
        axis=0,
    )
    return sums, table_grad


def front_grads(first, grad_t_ref, dq_ref, dk_ref, dv_ref, weight_grad, sums):
    width = first.shape[1]

    def turn():
        dk_ref[...] = grad_t_ref[:width, :].T
        dv_ref[...] = grad_t_ref[width:, :].T

    def key_and_value():
        weight_grad[width : 3 * width, :] += dot(grad_t_ref[...], first[...], 1, 0)

    def query():
        weight_grad[:width, :] += dot(dq_ref[...].T, first[...], 1, 0)
        for n, ref in enumerate((dq_ref, dk_ref, dv_ref)):
            sums[n : n + 1, :] += jnp.sum(ref[...].astype(F32), axis=0, keepdims=True)

    return [turn, key_and_value, query]


def finish_image(x, middle_grad, wt, vec, dq_ref, dk_ref, dv_ref):
    width = x.shape[1]
    normed, factor = normalize(x[...].astype(F32))
    project_grad = jnp.concatenate([dq_ref[...], dk_ref[...], dv_ref[...]], axis=1)
    first_grad = dot(project_grad, wt[: 3 * width], 1, 0)
    grad = middle_grad[...] + norm_back(first_grad * vec[GAIN1 : GAIN1 + 1], normed, factor)
    return grad.astype(BF16)


def norm_sums(sums, weight_grad, wt, vec):
    width = wt.shape[1]
    high = sums.astype(BF16)
    both = jnp.concatenate([high, (sums - high.astype(F32)).astype(BF16)], axis=0)
    shift_one = jnp.zeros((1, width), F32)
    for part in range(3):
        got = dot(both, wt[part * width : (part + 1) * width], 1, 0)
        shift_one += got[part : part + 1] + got[8 + part : 9 + part]
    product = jnp.sum(weight_grad * wt[: 3 * width].astype(F32), axis=0, keepdims=True)
    gain_one = (product - vec[BIAS1 : BIAS1 + 1] * shift_one) / vec[GAIN1 : GAIN1 + 1]
    gains = jnp.concatenate([gain_one, sums[3:4]], axis=0)
    return gains, jnp.concatenate([shift_one, sums[2:3], sums[4:5], sums[5:6]], axis=0)


def forward_kernel(
    x, g, valid, wt, vec, table,
    h1, q, k, v, p, att, inv, middle, dispatch, combine, slots, produced_grad,
):
    middle[0] = normalize(x[0].astype(F32))[0]
    projections(middle.at[0], wt, vec[...], h1.at[0], q.at[0], k.at[0], v.at[0])
    got = forward_image(
        x.at[0], g.at[0], valid[0], wt, vec[...], table[...],
        q.at[0], k.at[0], v.at[0], p.at[0], att.at[0], inv.at[0],
    )
    for ref, value in zip((middle, dispatch, combine, slots, produced_grad), got):
        ref[0] = value.astype(ref.dtype)


def add_output_grad(weight_grad, middle_grad, att):
    width = weight_grad.shape[1]
    branch_grad = middle_grad.astype(BF16).reshape(-1, width)
    weight_grad[3 * width :, :] += dot(branch_grad.T, att.reshape(-1, width), 1, 0)


def backward_kernel(
    x, g, middle, dispatch, combine, produced, slot_grad, wt, vec, table,
    h1, q, k, v, p, att, inv,
    mixed, patch_grad, weight_grad, sums, table_grad,
    ds, grad_t, dq, dk, dv, middle_grad,
):
    @pl.when(pl.program_id(0) == 0)
    def _():
        weight_grad[...] = jnp.zeros_like(weight_grad)
        sums[...] = jnp.zeros_like(sums)
        table_grad[...] = jnp.zeros_like(table_grad)

    got = backward_image(
        x.at[0], g.at[0], middle.at[0], dispatch[0], combine[0], produced[0], slot_grad[0],
        wt, vec[...], table[...],
        q.at[0], k.at[0], v.at[0], p.at[0], att.at[0], inv.at[0], ds, grad_t, dq,
        mixed.at[0], middle_grad,
    )
    sums[...] += got[0]
    table_grad[...] += got[1]
    for step in front_grads(h1.at[0], grad_t, dq, dk, dv, weight_grad, sums):
        step()
    add_output_grad(weight_grad, middle_grad[...], att[0])
    patch_grad[0] = finish_image(x.at[0], middle_grad, wt, vec[...], dq, dk, dv)


def per_image(*shape):
    return pl.BlockSpec((1,) + shape, lambda i: (i,) + (0,) * len(shape))


def whole(*shape):
    return pl.BlockSpec(shape, lambda i: (0,) * len(shape))


def run_forward(x, g, valid, wt, vec, table):
    count, patches, width = x.shape
    heads = width // HEAD_DIM
    experts = table.shape[0]
    flat = (patches, width)
    outs = [
        (flat, BF16), (flat, BF16), (flat, BF16), (flat, BF16), ((heads, patches, patches), BF16),
        (flat, BF16), (flat, F32), (flat, F32),
        ((experts, patches), F32), ((experts, patches), F32),
        ((experts, width), BF16), ((experts, width), BF16),
    ]
    return pl.pallas_call(
        forward_kernel,
        grid=(count,),
        in_specs=[
            per_image(*flat), per_image(*flat), per_image(1, patches),
            whole(*wt.shape), whole(*vec.shape), whole(*table.shape),
        ],
        out_specs=[per_image(*shape) for shape, _ in outs],
        out_shape=[jax.ShapeDtypeStruct((count,) + shape, kind) for shape, kind in outs],
        compiler_params=pltpu.CompilerParams(vmem_limit_bytes=VMEM_LIMIT),
        name="forward",
    )(x, g, valid, wt, vec, table)


def run_backward(x, g, kept, produced, slot_grad, wt, vec, table):
    count, patches, width = x.shape
    heads = width // HEAD_DIM
    experts = table.shape[0]
    flat = (patches, width)
    h1, q, k, v, p, att, inv, middle, dispatch, combine = kept
    return pl.pallas_call(
        backward_kernel,
        grid=(count,),
        in_specs=[
            per_image(*flat), per_image(*flat), per_image(*flat),
            per_image(experts, patches), per_image(experts, patches),
            per_image(experts, width), per_image(experts, width),
            whole(*wt.shape), whole(*vec.shape), whole(*table.shape),
            per_image(*flat), per_image(*flat), per_image(*flat), per_image(*flat),
            per_image(heads, patches, patches), per_image(*flat), per_image(*flat),
        ],
        out_specs=[
            per_image(*flat), per_image(*flat),
            whole(4 * width, width), whole(8, width), whole(experts, width),
        ],
        out_shape=[
            jax.ShapeDtypeStruct(x.shape, BF16), jax.ShapeDtypeStruct(x.shape, BF16),
            jax.ShapeDtypeStruct((4 * width, width), F32), jax.ShapeDtypeStruct((8, width), F32),
            jax.ShapeDtypeStruct((experts, width), F32),
        ],
        scratch_shapes=[
            pltpu.VMEM((2, patches, patches), BF16),
            pltpu.VMEM((2 * width, patches), BF16),
            pltpu.VMEM(flat, BF16),
            pltpu.VMEM(flat, BF16),
            pltpu.VMEM(flat, BF16),
            pltpu.VMEM(flat, F32),
        ],
        compiler_params=pltpu.CompilerParams(vmem_limit_bytes=VMEM_LIMIT),
        name="backward",
    )(x, g, middle, dispatch, combine, produced, slot_grad, wt, vec, table, h1, q, k, v, p, att, inv)


def here():
    return lax.axis_index("wide"), lax.axis_index("narrow")


def along_z(w, z):
    return [(w, lax.rem(z + step, 4)) for step in (1, 2, 3)]


def in_plane(w, z):
    x_flip = 2 - 4 * lax.rem(w // 2, 2)
    y_flip = 4 - 8 * (w // 4)
    return [(w + x_flip, z), (w + y_flip, z), (w + x_flip + y_flip, z)]


def other_core(w, z):
    return (w + 1 - 2 * lax.rem(w, 2), z)


def greet():
    w, z = here()
    barrier = pltpu.get_barrier_semaphore()
    peers = along_z(w, z) + in_plane(w, z) + [other_core(w, z)]
    for peer in peers:
        pl.semaphore_signal(barrier, inc=1, device_id=peer, device_id_type=MESH)
    pl.semaphore_wait(barrier, len(peers))


def remote(src, dst, send, recv, peer):
    return pltpu.make_async_remote_copy(
        src_ref=src, dst_ref=dst, send_sem=send, recv_sem=recv, device_id=peer, device_id_type=MESH
    )


class Gather:
    def __init__(self, every, send, recv):
        self.every, self.send, self.recv = every, send, recv
        self.w, self.z = here()
        self.core, self.chip = lax.rem(self.w, 2), self.w // 2

    def z_copies(self):
        own = self.every.at[self.core, self.chip, self.z]
        return [
            remote(own, own, self.send.at[n], self.recv.at[n], peer)
            for n, peer in enumerate(along_z(self.w, self.z))
        ]

    def plane_copies(self):
        own = self.every.at[self.core, self.chip]
        return [
            remote(own, own, self.send.at[3 + n], self.recv.at[3 + n], peer)
            for n, peer in enumerate(in_plane(self.w, self.z))
        ]

    def core_copy(self):
        own = self.every.at[self.core]
        return remote(own, own, self.send.at[6], self.recv.at[6], other_core(self.w, self.z))

    def start_z(self):
        for copy in self.z_copies():
            copy.start()

    def start_plane(self):
        for copy in self.z_copies():
            copy.wait()
        for copy in self.plane_copies():
            copy.start()

    def start_core(self):
        for copy in self.plane_copies():
            copy.wait()
        self.core_copy().start()

    def finish(self):
        self.core_copy().wait()


class FineGather:
    def __init__(self, every, z_send, z_recv, p_send, p_recv, c_send, c_recv):
        self.every = every
        self.z_sems, self.p_sems, self.c_sems = (z_send, z_recv), (p_send, p_recv), (c_send, c_recv)
        self.w, self.z = here()
        self.plane = in_plane(self.w, self.z)

    def block(self, w, k):
        return self.every.at[lax.rem(w, 2), w // 2, lax.rem(self.z + 4 - k, 4)]

    def z_copy(self, n):
        own = self.block(self.w, 0)
        peer = along_z(self.w, self.z)[n]
        return remote(own, own, self.z_sems[0].at[n], self.z_sems[1].at[n], peer)

    def plane_copy(self, n, k):
        own = self.block(self.w, k)
        return remote(own, own, self.p_sems[0].at[n, k], self.p_sems[1].at[n, k], self.plane[n])

    def core_copy(self, group, k):
        own = self.block(self.w if group == 0 else self.plane[group - 1][0], k)
        return remote(
            own, own, self.c_sems[0].at[group, k], self.c_sems[1].at[group, k],
            other_core(self.w, self.z),
        )

    def pass_on(self, k):
        for n in range(3):
            self.plane_copy(n, k).start()
        self.core_copy(0, k).start()

    def start(self):
        for n in range(3):
            self.z_copy(n).start()
        self.pass_on(0)

    def start_plane(self):
        for n in range(3):
            self.z_copy(n).wait()
            self.pass_on(n + 1)

    def start_core(self):
        for k in range(4):
            for n in range(3):
                self.plane_copy(n, k).wait()
                self.core_copy(n + 1, k).start()

    def finish(self):
        for group in range(4):
            for k in range(4):
                self.core_copy(group, k).wait()


class Scatter:
    def __init__(self, parts, from_core, chips, from_plane, column, from_z, send, recv):
        self.parts, self.from_core, self.chips = parts, from_core, chips
        self.from_plane, self.column, self.from_z = from_plane, column, from_z
        self.send, self.recv = send, recv
        self.w, self.z = here()
        self.core = lax.rem(self.w, 2)

    def core_copy(self):
        return remote(
            self.parts.at[1 - self.core], self.from_core, self.send.at[0], self.recv.at[0],
            other_core(self.w, self.z),
        )

    def plane_copies(self):
        return [
            remote(
                self.chips.at[peer[0] // 2], self.from_plane.at[n],
                self.send.at[1 + n], self.recv.at[1 + n], peer,
            )
            for n, peer in enumerate(in_plane(self.w, self.z))
        ]

    def z_copies(self):
        return [
            remote(
                self.column.at[peer[1]], self.from_z.at[n],
                self.send.at[4 + n], self.recv.at[4 + n], peer,
            )
            for n, peer in enumerate(along_z(self.w, self.z))
        ]

    def start_core(self):
        self.core_copy().start()

    def start_plane(self):
        self.core_copy().wait()
        total = self.parts[self.core].astype(F32) + self.from_core[...].astype(F32)
        self.chips[...] = total.astype(BF16)
        for copy in self.plane_copies():
            copy.start()

    def start_z(self):
        for copy in self.plane_copies():
            copy.wait()
        total = self.chips[self.w // 2].astype(F32)
        for n in range(3):
            total = total + self.from_plane[n].astype(F32)
        self.column[...] = total.astype(BF16)
        for copy in self.z_copies():
            copy.start()

    def finish(self):
        for copy in self.z_copies():
            copy.wait()

    def total(self):
        total = self.column[self.z].astype(F32)
        for n in range(3):
            total = total + self.from_z[n].astype(F32)
        return total


class FineScatter:
    def __init__(
        self, parts, from_core, chips, from_plane, column, from_z,
        c_send, c_recv, p_send, p_recv, z_send, z_recv,
    ):
        self.parts, self.from_core, self.chips = parts, from_core, chips
        self.from_plane, self.column, self.from_z = from_plane, column, from_z
        self.c_sems, self.p_sems, self.z_sems = (c_send, c_recv), (p_send, p_recv), (z_send, z_recv)
        self.w, self.z = here()
        self.core = lax.rem(self.w, 2)
        self.plane = in_plane(self.w, self.z)

    def goal(self, k):
        return lax.rem(self.z + k, 4)

    def core_copy(self, chip):
        return remote(
            self.parts.at[1 - self.core, chip], self.from_core.at[chip],
            self.c_sems[0].at[chip], self.c_sems[1].at[chip], other_core(self.w, self.z),
        )

    def plane_copy(self, n, k):
        z = self.goal(k)
        return remote(
            self.chips.at[self.plane[n][0] // 2, z], self.from_plane.at[n, z],
            self.p_sems[0].at[n, k], self.p_sems[1].at[n, k], self.plane[n],
        )

    def z_copy(self, k):
        return remote(
            self.column.at[self.goal(k)], self.from_z.at[k - 1],
            self.z_sems[0].at[k - 1], self.z_sems[1].at[k - 1], (self.w, self.goal(k)),
        )

    def start_core(self, chip):
        self.core_copy(chip).start()

    def start_plane(self, chip):
        self.core_copy(chip).wait()
        own = self.parts[self.core, chip].astype(F32)
        self.chips[chip] = (own + self.from_core[chip].astype(F32)).astype(BF16)
        for n, peer in enumerate(self.plane):

            @pl.when(peer[0] // 2 == chip)
            def _(n=n):
                for k in (1, 2, 3, 0):
                    self.plane_copy(n, k).start()

    def plane_sum(self, k):
        z = self.goal(k)
        total = self.chips[self.w // 2, z].astype(F32)
        for n in range(3):
            self.plane_copy(n, k).wait()
            total = total + self.from_plane[n, z].astype(F32)
        return total

    def start_z(self, k):
        self.column[self.goal(k)] = self.plane_sum(k).astype(BF16)
        self.z_copy(k).start()

    def total(self):
        total = self.plane_sum(0)
        for k in (1, 2, 3):
            self.z_copy(k).wait()
            total = total + self.from_z[k - 1].astype(F32)
        return total


def by_device(blocks):
    return jnp.concatenate([blocks[core, chip] for chip in range(4) for core in range(2)], axis=0)


def fill_blocks(blocks, values):
    for chip in range(4):
        for core in range(2):
            at = (2 * chip + core) * 4
            blocks[core, chip] = values[at : at + 4].astype(blocks.dtype)


def gather_scratch(rows, width):
    dma = pltpu.SemaphoreType.DMA
    return [pltpu.VMEM((2, 4, 4, rows, width), BF16), dma((7,)), dma((7,))]


def fine_scratch(rows, width):
    dma = pltpu.SemaphoreType.DMA
    return [
        pltpu.VMEM((2, 4, 4, rows, width), BF16),
        dma((3,)), dma((3,)), dma((3, 4)), dma((3, 4)), dma((4, 4)), dma((4, 4)),
    ]


def scatter_scratch(rows, width):
    return [
        pltpu.VMEM((2, 4, 4, rows, width), BF16),
        pltpu.VMEM((4, 4, rows, width), BF16),
        pltpu.VMEM((4, 4, rows, width), BF16),
        pltpu.VMEM((3, 4, rows, width), BF16),
        pltpu.VMEM((4, rows, width), BF16),
        pltpu.VMEM((3, rows, width), BF16),
        pltpu.SemaphoreType.DMA((7,)),
        pltpu.SemaphoreType.DMA((7,)),
    ]


def expert_rows(slots, grads, w_in, bias, w_out):
    rows, width = slots.shape
    units = w_in.shape[0]
    shape = (rows, units)
    own = lax.rem(lax.broadcasted_iota(jnp.int32, shape, 0), 8)
    start = own * (units // 8)
    lane = lax.broadcasted_iota(jnp.int32, shape, 1)
    keep = (lane >= start) & (lane < start + units // 8)
    hidden = dot(slots, w_in, 1, 1) + bias
    active_grad = dot(grads, w_out, 1, 1)
    half = 0.5 * (1.0 + lax.erf(hidden * 0.7071067811865476))
    active = jnp.where(keep, hidden * half, 0.0).astype(BF16)
    slope = half + hidden * jnp.exp(hidden * hidden * -0.5) * 0.3989422804014327
    hidden_grad = jnp.where(keep, active_grad * slope, 0.0).astype(BF16)
    produced = dot(active, w_out, 1, 0)
    slot_grad = dot(hidden_grad, w_in, 1, 0)
    return produced, slot_grad, active, hidden_grad


def one_hot(length, width):
    row = lax.broadcasted_iota(jnp.int32, (128, width), 0)
    column = lax.broadcasted_iota(jnp.int32, (128, width), 1)
    return (row == lax.rem(column, length)).astype(BF16)


def own_piece(shape, length):
    device = lax.broadcasted_iota(jnp.int32, shape, 0)
    column = lax.broadcasted_iota(jnp.int32, shape, 1)
    return lax.rem(device, shape[1] // length) == column // length


def spread(pieces, length, width):
    devices = pieces.shape[0]
    tall = dot(pieces.astype(BF16), one_hot(length, width), 1, 0)
    tall = jnp.where(own_piece(tall.shape, length), tall, 0.0).astype(BF16)
    row = lax.broadcasted_iota(jnp.int32, (8, devices), 0)
    device = lax.broadcasted_iota(jnp.int32, (8, devices), 1)
    return dot((device // (width // length) == row).astype(BF16), tall, 1, 0)


def pieces_of(rows, length, devices):
    count, width = rows.shape
    per_row = width // length
    tall = jnp.broadcast_to(rows[:, None], (count, per_row, width)).reshape(devices, width)
    tall = jnp.where(own_piece(tall.shape, length), tall, 0.0)
    return dot(tall.astype(BF16), one_hot(length, width), 1, 1)


def layer_kernel(
    lengths,
    x_hbm, g_hbm, valid, own_weights, own_gains, own_biases, own_table, own_shift, w_in, own_bias, w_out,
    g, x, p_hbm, weight_out, vectors_out, in_grad, out_grad, bias_grad,
    h1, q, k, v, att, inv, middle, dispatch, combine, p, ds, grad_t, wt, vec, table, shift, bias,
    weight_grad, sums, table_grad, shift_grad, own_pieces,
    active, hidden_grad,
    x_sem, g_sem, p_out_sem, p_in_sem,
    every, g_send, g_recv,
    parts, from_core, chips, from_plane, column, from_z, s_send, s_recv,
    *rest,
):
    count, patches, width = x.shape
    heads = width // HEAD_DIM
    rows = own_weights.shape[0]
    wide, narrow = here()
    me = (lax.rem(wide, 2), wide // 2, narrow)
    (w_every, *w_sems), (v_every, *v_sems) = rest[:7], rest[7:10]
    w_last, v_last = rest[10:22], rest[22:30]

    for i in range(count):
        pltpu.make_async_copy(x_hbm.at[i], x.at[i], x_sem.at[i]).start()
        pltpu.make_async_copy(g_hbm.at[i], g.at[i], g_sem.at[i]).start()
    w_every[me] = own_weights[...]
    own_pieces[...] = jnp.zeros_like(own_pieces)
    for n, ref in enumerate((own_gains, own_biases, own_table, own_shift)):
        own_pieces[n : n + 1, : lengths[n]] = ref[...].astype(F32).reshape(1, lengths[n])
    v_every[me] = own_pieces[...].astype(BF16)
    greet()
    weights = FineGather(w_every, *w_sems)
    vectors = Gather(v_every, *v_sems)
    vectors.start_z()
    weights.start()
    for ref in (weight_grad, sums, table_grad, shift_grad, in_grad, out_grad, bias_grad):
        ref[...] = jnp.zeros_like(ref)
    units = w_in.shape[0] // 8
    spread_bias = dot(own_bias[...], one_hot(units, 8 * units)[:units], 1, 0)
    at = lax.broadcasted_iota(jnp.int32, spread_bias.shape, 0)
    lane = lax.broadcasted_iota(jnp.int32, spread_bias.shape, 1)
    bias[...] = jnp.sum(jnp.where(lane // units == at, spread_bias, 0.0), axis=0, keepdims=True)
    def arrive(hbm, ref, sem, i):
        pltpu.make_async_copy(hbm.at[i], ref.at[i], sem.at[i]).wait()

    def first_norm(i, carry):
        arrive(x_hbm, x, x_sem, i)
        middle[i] = normalize(x[i].astype(F32))[0]
        return carry

    lax.fori_loop(0, count, first_norm, 0)
    vectors.start_plane()
    weights.start_plane()
    vectors.start_core()
    weights.start_core()
    vectors.finish()
    packed = by_device(v_every).astype(F32)
    gains, biases, slot_rows, shift_rows = (
        spread(packed[:, n], length, width) for n, length in enumerate(lengths)
    )
    vec[...] = jnp.concatenate([gains[:2], biases[:4], jnp.zeros((2, width), F32)], axis=0)
    table[...] = slot_rows
    shift[...] = shift_rows
    weights.finish()
    wt[...] = by_device(w_every).reshape(4 * width, width)

    def slots_way(i):
        return Gather(every.at[i], g_send.at[i], g_recv.at[i])

    def results_way(i):
        ring = lax.rem(i, 2)
        return Scatter(
            parts.at[ring], from_core.at[ring], chips.at[ring], from_plane.at[i], column.at[i],
            from_z.at[i], s_send.at[i], s_recv.at[i],
        )

    def for_image(i, action):
        @pl.when((i >= 0) & (i < count))
        def _():
            action(i)

    def arrived_rows(i):
        both = every[i].astype(F32).reshape(32, 2, 8, width)
        return [both[:, n].reshape(32 * 8, width).astype(BF16) for n in range(2)]

    def experts(i):
        slots_way(i).finish()
        got = expert_rows(*arrived_rows(i), w_in[...], bias[...], w_out[...])
        back = jnp.stack([got[0].reshape(32, 8, width), got[1].reshape(32, 8, width)], axis=1)
        parts[lax.rem(i, 2)] = back.reshape(2, 4, 4, 16, width).astype(BF16)
        active[i], hidden_grad[i] = got[2:]
        results_way(i).start_core()

    def middle_of(step):
        for_image(step - 3, experts)

    def end_of(step):
        for_image(step - 4, lambda i: results_way(i).start_z())
        for_image(step - 3, lambda i: results_way(i).start_plane())
        for_image(step - 2, lambda i: slots_way(i).start_core())
        for_image(step - 1, lambda i: slots_way(i).start_plane())

    def p_out(i, head):
        return pltpu.make_async_copy(p.at[head], p_hbm.at[i, head], p_out_sem.at[head])

    def p_in(i, head):
        return pltpu.make_async_copy(p_hbm.at[i, head], p.at[head], p_in_sem.at[head])

    def forward(i, carry):
        arrive(g_hbm, g, g_sem, i)

        @pl.when(i > 0)
        def _():
            for head in range(heads):
                p_out(i - 1, head).wait()

        projections(middle.at[i], wt, vec[...], h1.at[i], q.at[i], k.at[i], v.at[i])
        got = forward_image(
            x.at[i], g.at[i], valid[pl.ds(i, 1)], wt, vec[...], table[...].astype(BF16),
            q.at[i], k.at[i], v.at[i], p, att.at[i], inv.at[i], lambda head: p_out(i, head).start(),
            lambda: middle_of(i),
        )
        middle[i], dispatch[i], combine[i] = got[:3]
        shift_grad[...] += got[4].astype(BF16).astype(F32)
        every[(i,) + me] = jnp.concatenate([got[3], got[4]], axis=0).astype(BF16)
        end_of(i)
        slots_way(i).start_z()
        return carry

    lax.fori_loop(0, count, forward, 0)
    q[count] = jnp.zeros_like(q[count])
    h1[count] = jnp.zeros_like(h1[count])
    grad_t[...] = jnp.zeros_like(grad_t)
    for head in range(heads):
        p_out(count - 1, head).wait()
        p_in(0, head).start()

    def front(i):
        place = lax.rem(i + count + 1, count + 1)
        return front_grads(
            h1.at[place], grad_t, q.at[place], k.at[place], v.at[place], weight_grad, sums
        )

    def backward(i, carry):
        def before_heads():
            middle_of(count + i)
            for head in range(heads):
                p_in(i, head).wait()

        def after_heads():
            @pl.when(i + 1 < count)
            def _():
                for head in range(heads):
                    p_in(i + 1, head).start()

        results_way(i).finish()
        total = results_way(i).total()
        got = backward_image(
            x.at[i], g.at[i], middle.at[i], dispatch[i], combine[i],
            (total[:8] + shift[...]).astype(BF16), total[8:].astype(BF16),
            wt, vec[...], table[...].astype(BF16),
            q.at[i], k.at[i], v.at[i], p, att.at[i], inv.at[i], ds, grad_t,
            q.at[i], g.at[i], middle.at[i], before_heads, after_heads, front(i - 1),
        )
        sums[...] += got[0]
        table_grad[...] += got[1]
        end_of(count + i)
        return carry

    lax.fori_loop(0, count, backward, 0)
    weights = FineScatter(*w_last)

    def depart(chip):
        for core in range(2):
            block = weight_grad[pl.ds((2 * chip + core) * 4 * rows, 4 * rows), :]
            w_last[0][core, chip] = block.reshape(4, rows, width).astype(BF16)
        weights.start_core(chip)

    turn, key_and_value, query = front(count - 1)
    turn()
    key_and_value()
    depart(1)
    depart(2)
    query()
    depart(0)
    for i in range(0, count, 2):
        add_output_grad(weight_grad, middle[i : i + 2], att[i : i + 2])
        if i == 0:
            for chip in (1, 2, 0):
                weights.start_plane(chip)
    depart(3)
    gains, biases = norm_sums(sums[...], weight_grad[: 3 * width, :], wt, vec[...])
    pieces = [
        pieces_of(value, length, 32)
        for value, length in zip((gains, biases, table_grad[...], shift_grad[...]), lengths)
    ]
    pieces.append(jnp.zeros((32, 128), F32))
    pieces = jnp.stack([pieces[min(n, 4)] for n in range(16)], axis=1)
    fill_blocks(v_last[0], pieces)
    vectors = Scatter(*v_last)
    vectors.start_core()
    weights.start_plane(3)
    vectors.start_plane()

    def finish(i, carry):
        x[i] = finish_image(x.at[i], middle.at[i], wt, vec[...], q.at[i], k.at[i], v.at[i])
        all_slots, all_grads = arrived_rows(i)
        in_grad[...] += dot(hidden_grad[i], all_slots, 0, 0)
        out_grad[...] += dot(active[i], all_grads, 0, 0)
        bias_grad[...] += jnp.sum(hidden_grad[i].astype(F32).reshape(32, 8, -1), axis=0)

        for block in (2, 3, 4):

            @pl.when(i == block)
            def _(block=block):
                weights.start_z(block - 1)

        @pl.when(i == 3)
        def _():
            vectors.start_z()

        return carry

    lax.fori_loop(0, count, finish, 0)
    weight_out[...] = weights.total()
    vectors.finish()
    vectors_out[...] = vectors.total()


def hand_over_kernel(
    mixed, patch_grad, weight_grad, in_grad, out_grad, vectors, bias_grad,
    mixed_out, patch_grad_out, weight_out, in_out, out_out, gains, biases, table, shift, bias_out, sems,
):
    moves = (
        (mixed, mixed_out), (patch_grad, patch_grad_out), (weight_grad, weight_out),
        (in_grad, in_out), (out_grad, out_out),
    )
    copies = [pltpu.make_async_copy(src, dst, sems.at[n]) for n, (src, dst) in enumerate(moves)]
    for copy in copies:
        copy.start()
    for n, ref in enumerate((gains, biases, table, shift)):
        ref[...] = vectors[n : n + 1, : ref.shape[0]].reshape(ref.shape[0])
    experts, units = bias_out.shape
    for e in range(experts):
        bias_out[e : e + 1, :] = bias_grad[e : e + 1, e * units : (e + 1) * units]
    for copy in copies:
        copy.wait()


def run_layer(patches, valid, attn_weights, vectors, expert_in, expert_in_bias, expert_out, out_grad):
    count, length, width = patches.shape
    heads = width // HEAD_DIM
    experts, _, units = expert_in.shape
    rows = attn_weights.shape[1]
    lengths = [v.shape[0] for v in vectors]
    flat = (length, width)
    dma = pltpu.SemaphoreType.DMA
    vmem = pltpu.VMEM
    anywhere = pl.BlockSpec(memory_space=pl.ANY)
    here_all = pl.BlockSpec(memory_space=pltpu.VMEM)
    mixed, patch_grad, _, weight_grad, vector_grads, in_grad, out_grads, bias_grad = pl.pallas_call(
        functools.partial(layer_kernel, lengths),
        in_specs=[anywhere] * 2 + [here_all] * 9,
        out_specs=[here_all] * 2 + [anywhere] + [here_all] * 5,
        out_shape=[
            vmem(patches.shape, BF16), vmem(patches.shape, BF16),
            jax.ShapeDtypeStruct((count, heads, length, length), BF16),
            vmem((rows, width), F32), vmem((16, 128), F32),
            vmem((experts * units, width), F32), vmem((experts * units, width), F32),
            vmem((experts, experts * units), F32),
        ],
        scratch_shapes=[
            vmem((count + 1,) + flat, BF16), vmem((count + 1,) + flat, BF16),
            vmem((count + 1,) + flat, BF16), vmem((count + 1,) + flat, BF16),
            vmem((count,) + flat, BF16), vmem((count,) + flat, BF16), vmem((count,) + flat, F32),
            vmem((count, experts, length), F32), vmem((count, experts, length), F32),
            vmem((heads, length, length), BF16), vmem((2, length, length), BF16),
            vmem((2 * width, length), BF16), vmem((4 * width, width), BF16),
            vmem((8, width), F32), vmem((experts, width), F32), vmem((experts, width), F32),
            vmem((1, experts * units), F32),
            vmem((4 * width, width), F32), vmem((8, width), F32), vmem((experts, width), F32),
            vmem((experts, width), F32), vmem((16, 128), F32),
            vmem((count, 32 * experts, experts * units), BF16),
            vmem((count, 32 * experts, experts * units), BF16),
            dma((count,)), dma((count,)), dma((heads,)), dma((heads,)),
        ]
        + [vmem((count, 2, 4, 4, 16, width), BF16), dma((count, 7)), dma((count, 7))]
        + [
            vmem((2, 2, 4, 4, 16, width), BF16), vmem((2, 4, 4, 16, width), BF16),
            vmem((2, 4, 4, 16, width), BF16), vmem((count, 3, 4, 16, width), BF16),
            vmem((count, 4, 16, width), BF16), vmem((count, 3, 16, width), BF16),
            dma((count, 7)), dma((count, 7)),
        ]
        + fine_scratch(rows, width) + gather_scratch(16, 128)
        + scatter_scratch(rows, width)[:6]
        + [dma((4,)), dma((4,)), dma((3, 4)), dma((3, 4)), dma((3,)), dma((3,))]
        + scatter_scratch(16, 128),
        compiler_params=pltpu.CompilerParams(
            collective_id=0, has_side_effects=True, vmem_limit_bytes=LAYER_LIMIT
        ),
        name="layer",
    )(
        patches, out_grad, valid, attn_weights.T, *vectors,
        expert_in.transpose(0, 2, 1).reshape(experts * units, width), expert_in_bias,
        expert_out.reshape(experts * units, width),
    )
    results = pl.pallas_call(
        hand_over_kernel,
        in_specs=[here_all] * 7,
        out_specs=[anywhere] * 5 + [here_all] * 5,
        out_shape=[
            jax.ShapeDtypeStruct(value.shape, value.dtype)
            for value in (mixed, patch_grad, weight_grad, in_grad, out_grads)
        ]
        + [jax.ShapeDtypeStruct((piece,), F32) for piece in lengths]
        + [jax.ShapeDtypeStruct((experts, units), F32)],
        scratch_shapes=[dma((5,))],
        compiler_params=pltpu.CompilerParams(vmem_limit_bytes=8 * 1024 * 1024),
        name="hand_over",
    )(mixed, patch_grad, weight_grad, in_grad, out_grads, vector_grads, bias_grad)
    mixed, patch_grad, weight_grad, in_grad, out_grads, gains, biases, table, shift, bias_grad = results
    return (
        mixed,
        patch_grad,
        weight_grad.T,
        gains,
        biases,
        table,
        in_grad.reshape(experts, units, width).transpose(0, 2, 1),
        bias_grad,
        out_grads.reshape(experts, units, width),
        shift,
    )


def scatter_sum(parts):
    got = lax.all_to_all(parts.astype(BF16), AXES, 0, 0, tiled=True)
    return jnp.sum(got.astype(F32), axis=0)


def experts_at_home(slots, produced_grad, expert_in, expert_in_bias, expert_out, devices):
    local_images, experts, width = slots.shape
    every = lax.all_gather(jnp.stack([slots, produced_grad]), AXES, axis=1, tiled=True)
    all_slots, all_grads = every[0], every[1]
    hidden = jnp.einsum(
        "bed,edf->bef", all_slots, expert_in, preferred_element_type=F32
    ) + expert_in_bias.astype(F32)
    active, gelu_back = jax.vjp(smooth, hidden)
    active = active.astype(BF16)
    partial = jnp.einsum("bef,efd->bed", active, expert_out, preferred_element_type=F32)
    active_grad = jnp.einsum("bed,efd->bef", all_grads, expert_out, preferred_element_type=F32)
    hidden_grad = gelu_back(active_grad)[0].astype(BF16)
    partial_back = jnp.einsum("bef,edf->bed", hidden_grad, expert_in, preferred_element_type=F32)
    contract_grad = jnp.einsum("bef,bed->efd", active, all_grads, preferred_element_type=F32)
    expand_grad = jnp.einsum("bed,bef->edf", all_slots, hidden_grad, preferred_element_type=F32)
    inner_grad = jnp.sum(hidden_grad.astype(F32), axis=0)
    both = jnp.stack([partial, partial_back]).reshape(2, devices, local_images, experts, width)
    both = scatter_sum(jnp.moveaxis(both, 1, 0))
    return (both[0], both[1], expand_grad, inner_grad, contract_grad)


def on_device(
    patches,
    valid,
    attn_weights,
    norm_gains,
    vec_biases,
    slot_params,
    expert_in,
    expert_in_bias,
    expert_out,
    expert_out_bias,
    out_grad,
):
    local_images, patch_count, width = patches.shape
    experts = expert_in.shape[0]
    devices = lax.axis_size("wide") * lax.axis_size("narrow")

    vectors = (norm_gains, vec_biases, slot_params, expert_out_bias)
    lengths = [v.shape[0] for v in vectors]
    if lax.axis_size("wide") == 8 and lax.axis_size("narrow") == 4:
        return run_layer(
            patches, valid, attn_weights, vectors, expert_in, expert_in_bias, expert_out, out_grad
        )
    wt = lax.all_gather(attn_weights.T, AXES, axis=0, tiled=True)
    small = lax.all_gather(jnp.concatenate(vectors), AXES)
    pieces = []
    at = 0
    for length in lengths:
        pieces.append(small[:, at : at + length].reshape(-1, width))
        at += length
    gains, biases, table, expert_shift = pieces
    vec = jnp.concatenate([gains, biases, jnp.zeros((2, width), BF16)]).astype(F32)

    *kept, slots, produced_grad = run_forward(
        patches, out_grad, valid.reshape(local_images, 1, patch_count), wt, vec, table
    )
    produced, slot_grad, expand_grad, inner_grad, contract_grad = experts_at_home(
        slots, produced_grad, expert_in, expert_in_bias, expert_out, devices
    )
    produced = (produced + expert_shift.astype(F32)).astype(BF16)
    slot_grad = slot_grad.astype(BF16)
    shift_grad = jnp.sum(produced_grad.astype(F32), axis=0)
    mixed_out, patch_grad, weight_grad, rows, table_grad = run_backward(
        patches, out_grad, kept, produced, slot_grad, wt, vec, table
    )
    weight_front = weight_grad[: 3 * width]
    weight_grad = weight_grad.reshape(devices, -1, width)
    gain_grads, bias_grads = norm_sums(rows, weight_front, wt, vec)
    small_grads = jnp.concatenate(
        [v.reshape(devices, -1) for v in (gain_grads, bias_grads, table_grad, shift_grad)], axis=1
    )
    weight_grad = scatter_sum(weight_grad).T
    small_grads = jnp.sum(lax.all_to_all(small_grads, AXES, 0, 0, tiled=True), axis=0)
    grads = []
    at = 0
    for length in lengths:
        grads.append(small_grads[at : at + length])
        at += length
    return (
        mixed_out,
        patch_grad,
        weight_grad,
        grads[0],
        grads[1],
        grads[2],
        expand_grad,
        inner_grad,
        contract_grad,
        grads[3],
    )


def solution(mesh):
    images = P(AXES, None, None)
    vector = P(AXES)
    second = P(None, AXES)
    return jax.shard_map(
        on_device,
        mesh=mesh,
        in_specs=(
            images, P(AXES, None), second, vector, vector, vector,
            P(None, None, AXES), second, P(None, AXES, None), vector, images,
        ),
        out_specs=(
            images, images, second, vector, vector, vector,
            P(None, None, AXES), second, P(None, AXES, None), vector,
        ),
        check_vma=False,
    )
```
